512 devices in a mesh: dom: 128 (over z, x, core), feat: 4 (over y).
Axes of the slice: x: 4, y: 4, z: 16, core: 2. Of those that a mesh axis runs over, the one named last changes fastest.
Arguments:
- grid_feat: bfloat16 [262144, 512], P(('dom', 'feat')), may hold values from -6 to 6
- mesh_feat: bfloat16 [20480, 512], P(('dom', 'feat')), may hold values from -6 to 6
- w_grid: bfloat16 [512, 512], P('feat'), may hold values from -0.25 to 0.25
- w_mesh: bfloat16 [512, 512], P('feat'), may hold values from -0.25 to 0.25
- w_enc2: bfloat16 [512, 512], P('feat'), may hold values from -0.25 to 0.25
- w_src: bfloat16 [512, 512], P('feat'), may hold values from -0.25 to 0.25
- w_dst: bfloat16 [512, 512], P('feat'), may hold values from -0.25 to 0.25
- w_proc2: bfloat16 [512, 512], P('feat'), may hold values from -0.25 to 0.25
- enc_send: int32 [65536, 2], P(('dom', 'feat')), may hold values from -1 to 511, as said below
- enc_dst: int32 [65536, 2], P(('dom', 'feat')), may hold values from -1 to 159, as said below
- hal_send: int32 [16384, 4], P('dom'), may hold values from -1 to 159, as said below
- proc_src: int32 [81920], P(('dom', 'feat')), may hold values from 0 to 671, as said below
- proc_dst: int32 [81920], P(('dom', 'feat')), may hold values from 0 to 159
- cotangent: bfloat16 [20480, 512], P(('dom', 'feat')), may hold values from -6 to 6
Outputs:
- out: bfloat16 [20480, 512], P(('dom', 'feat'))
- g_grid: bfloat16 [262144, 512], P(('dom', 'feat'))
- g_mesh: bfloat16 [20480, 512], P(('dom', 'feat'))
- g_wgrid: float32 [512, 512], P('feat')
- g_wmesh: float32 [512, 512], P('feat')
- g_wenc2: float32 [512, 512], P('feat')
- g_wsrc: float32 [512, 512], P('feat')
- g_wdst: float32 [512, 512], P('feat')
- g_wproc2: float32 [512, 512], P('feat')
The draws below stay inside these ranges and needn't reach their ends.
Inputs may be any that keep to these rules, and one draw needn't show every extreme that they name: `enc_send`: row j * 128 + r lists, for sender device j, the local grid rows of its slots to partition r in the first n slots and -1 after them; enc_dst's row of the receiver (r, f) for that sender partition has the same n live slots. A quarter of the partitions get half or more of the slots from every sender, and one gets all 2 from every sender. `enc_dst`: row (r * 4 + f) * 128 + s gives the target node, within partition r, of each slot that device s * 4 + f sends to device (r, f); -1 exactly where enc_send's slot is -1. `hal_send`: row s * 128 + r lists the rows of partition s sent to partition r; each pair has 1 to 4 live slots first, -1 after them; some pairs are full. `proc_src`: A value under 160 is a node of the edge's own partition; a value 160 + s * 4 + c names halo slot c from partition s, always a live one.
All inputs are finite; a program needn't handle non-finite values.
Results may differ from the reference program's by a relative error of at most 0.014.
Values may be sent and summed in bfloat16 or wider, within the bound.
No kernel may reach another device: no remote copies, remote signals or barrier semaphores. Data moves between devices by JAX's collectives and lax.ppermute only.
A program may use at most 64 MiB of HBM per device.

```python
import math
import jax
import jax.numpy as jnp
from jax import lax

D = 512
G_DEV = 512
M_DEV = 40
CAP = 2
HCAP = 4
E_DEV = 160
PART = 160
GRID = 262144
MESH = 20480
EDGES = 81920
N_DOM = 128
N_FEAT = 4


def enc_counts(key):
    base = jax.random.fold_in(key, 101)
    order_key, heavy_key, light_key = jax.random.split(base, 3)
    ranking = jax.random.permutation(order_key, N_DOM)
    quarter = max(N_DOM // 4, 1)
    senders = N_DOM * N_FEAT
    heavy = jax.random.randint(heavy_key, (senders, N_DOM), CAP // 2, CAP + 1)
    light = jax.random.randint(light_key, (senders, N_DOM), 0, CAP // 2 + 1)
    counts = jnp.where((ranking < quarter)[None, :], heavy, light)
    return jnp.where((ranking == 0)[None, :], CAP, counts).astype(jnp.int32)


def halo_counts(key):
    base = jax.random.fold_in(key, 201)
    counts = jax.random.randint(base, (N_DOM, N_DOM), 1, HCAP + 1)
    source = jnp.arange(N_DOM, dtype=jnp.int32)
    paired = source[None, :] == (source[:, None] + 1) % N_DOM
    return jnp.where(paired, HCAP, counts).astype(jnp.int32)


def draw_enc_send(key, part):
    counts = enc_counts(key)
    picks = jax.random.randint(jax.random.fold_in(key, 102), (N_DOM * N_FEAT, N_DOM, CAP), 0, G_DEV)
    column = jnp.arange(CAP, dtype=jnp.int32)
    filled = jnp.where(column[None, None, :] < counts[:, :, None], picks, -1)
    return filled.reshape(N_DOM * N_FEAT * N_DOM, CAP).astype(jnp.int32)


def draw_enc_dst(key, part):
    counts = enc_counts(key).reshape(N_DOM, N_FEAT, N_DOM)
    flipped = jnp.transpose(counts, (2, 1, 0)).reshape(N_DOM * N_FEAT, N_DOM)
    picks = jax.random.randint(jax.random.fold_in(key, 103), (N_DOM * N_FEAT, N_DOM, CAP), 0, M_DEV * N_FEAT)
    column = jnp.arange(CAP, dtype=jnp.int32)
    filled = jnp.where(column[None, None, :] < flipped[:, :, None], picks, -1)
    return filled.reshape(N_DOM * N_FEAT * N_DOM, CAP).astype(jnp.int32)


def draw_hal_send(key, part):
    counts = halo_counts(key)
    picks = jax.random.randint(jax.random.fold_in(key, 202), (N_DOM, N_DOM, HCAP), 0, M_DEV * N_FEAT)
    column = jnp.arange(HCAP, dtype=jnp.int32)
    filled = jnp.where(column[None, None, :] < counts[:, :, None], picks, -1)
    return filled.reshape(N_DOM * N_DOM, HCAP).astype(jnp.int32)


def draw_proc_src(key, part):
    counts = halo_counts(key)
    devices = N_DOM * N_FEAT
    owner = (jnp.arange(devices, dtype=jnp.int32) // N_FEAT)[:, None]
    pick_key, local_key, source_key, spread_key = jax.random.split(jax.random.fold_in(key, 203), 4)
    choose = jax.random.randint(pick_key, (devices, E_DEV), 0, 2)
    local = jax.random.randint(local_key, (devices, E_DEV), 0, M_DEV * N_FEAT)
    source = jax.random.randint(source_key, (devices, E_DEV), 0, N_DOM)
    spread = jax.random.randint(spread_key, (devices, E_DEV), 0, 1 << 20)
    available = counts[source, owner]
    remote = M_DEV * N_FEAT + source * HCAP + spread % available
    return jnp.where(choose == 1, remote, local).reshape(-1).astype(jnp.int32)


def touch_ends(array, rng, least, largest):
    dims = array.shape
    place = [jax.random.randint(jax.random.fold_in(rng, axis), (), 0, dims[axis]) for axis in range(len(dims))]
    array = array.at[tuple(place)].set(least)
    longest = dims.index(max(dims))
    place[longest] = (place[longest] + 1) % dims[longest]
    return array.at[tuple(place)].set(largest)


def block_scale(rng, dims, cuts, low, high):
    loudness, own = 1.0, jax.random.fold_in(rng, 6)
    for dim, blocks in cuts:
        draws = jnp.exp(jax.random.uniform(jax.random.fold_in(own, dim), (blocks,), jnp.float32, low / len(cuts), high / len(cuts)))
        loudness = loudness * jnp.repeat(draws, dims[dim] // blocks).reshape([-1 if axis == dim else 1 for axis in range(len(dims))])
    return loudness


def normal_values(rng, extent, deviation, reach, cuts=(), kind=jnp.bfloat16):
    entries = deviation * jax.random.normal(rng, extent, jnp.float32)
    if cuts:
        entries = entries * block_scale(rng, extent, cuts, -0.22, 0.18)
    return jnp.clip(entries, -reach, reach).astype(kind)


def setup_inputs(seed: int = 0) -> dict:
    keys = jax.random.split(jax.random.key(seed), 15)
    return {
        "grid_feat": normal_values(keys[0], (GRID, D), 1.0, 6.0, ((0, 512),)),
        "mesh_feat": normal_values(keys[1], (MESH, D), 1.0, 6.0, ((0, 512),)),
        "w_grid": normal_values(keys[2], (D, D), D ** -0.5, 0.25, ((0, 4),)),
        "w_mesh": normal_values(keys[3], (D, D), D ** -0.5, 0.25, ((0, 4),)),
        "w_enc2": normal_values(keys[4], (D, D), D ** -0.5, 0.25, ((0, 4),)),
        "w_src": normal_values(keys[5], (D, D), D ** -0.5, 0.25, ((0, 4),)),
        "w_dst": normal_values(keys[6], (D, D), D ** -0.5, 0.25, ((0, 4),)),
        "w_proc2": normal_values(keys[7], (D, D), D ** -0.5, 0.25, ((0, 4),)),
        "enc_send": draw_enc_send(jax.random.fold_in(keys[14], 71), 0),
        "enc_dst": draw_enc_dst(jax.random.fold_in(keys[14], 71), 0),
        "hal_send": draw_hal_send(jax.random.fold_in(keys[14], 71), 0),
        "proc_src": draw_proc_src(jax.random.fold_in(keys[14], 71), 0),
        "proc_dst": touch_ends(jax.random.randint(keys[12], (EDGES,), 0, PART), jax.random.fold_in(keys[12], 1), 0, PART - 1).astype(jnp.int32),
        "cotangent": normal_values(keys[13], (MESH, D), 1.0, 6.0, ((0, 512),)),
    }


EPS = 1e-05

def matmul(left, right):
    return jnp.dot(left, right, preferred_element_type=jnp.float32)

def matmul_t(left, right):
    return lax.dot_general(left, right, (((left.ndim - 1,), (1,)), ((), ())), preferred_element_type=jnp.float32)

def outer_batch(left, right):
    return jnp.einsum('fnd,fne->fde', left.astype(jnp.float32), right.astype(jnp.float32), precision=lax.Precision.HIGHEST)

def layer_norm(values):
    center = values - lax.optimization_barrier(jnp.mean(values, axis=-1, keepdims=True))
    spread = lax.optimization_barrier(jnp.mean(center * center, axis=-1, keepdims=True))
    scaling = lax.rsqrt(spread + EPS)
    return (center * scaling, scaling)

def norm_back(normed, scaling, upstream):
    inner = lax.optimization_barrier(jnp.mean(upstream, axis=-1, keepdims=True))
    along = lax.optimization_barrier(jnp.mean(upstream * normed, axis=-1, keepdims=True))
    return scaling * (upstream - inner - normed * along)

def silu_slope(preact):
    sigma = jax.nn.sigmoid(preact)
    return sigma * (1.0 + preact * (1.0 - sigma))

def edge_forward(preact, weight):
    hidden = jax.nn.silu(preact).astype(jnp.bfloat16)
    normed, scaling = layer_norm(matmul(hidden, weight))
    return (hidden, normed, scaling)

def rounded_sum(pieces):
    narrow = lax.optimization_barrier(pieces.astype(jnp.bfloat16))
    return lax.optimization_barrier(jnp.sum(narrow.astype(jnp.float32), axis=0))

def reference(grid_feat, mesh_feat, w_grid, w_mesh, w_enc2, w_src, w_dst, w_proc2, enc_send, enc_dst, hal_send, proc_src, proc_dst, cotangent):
    device_count = N_DOM * N_FEAT
    part_rows = M_DEV * N_FEAT
    table_rows = part_rows + N_DOM * HCAP
    factor = 1.0 / math.sqrt(M_DEV * device_count)
    feat_ids = jnp.arange(N_FEAT, dtype=jnp.int32)
    dom_ids = jnp.arange(N_DOM, dtype=jnp.int32)
    sender_dev = dom_ids[None, :] * N_FEAT + feat_ids[:, None]
    grid_dev = grid_feat.reshape(device_count, G_DEV, D)
    projected = matmul(grid_feat, w_grid).astype(jnp.bfloat16).reshape(device_count, G_DEV, D)
    send_idx = enc_send.reshape(device_count, N_DOM, CAP)
    dst_all = enc_dst.reshape(N_DOM, N_FEAT, N_DOM * CAP)
    mesh_all = mesh_feat.reshape(N_DOM, part_rows, D)
    zero_square = jnp.zeros((D, D), jnp.float32)

    def encoder_values(dom_index):
        rows_idx = send_idx[sender_dev, dom_index]
        received = projected[sender_dev[:, :, None], jnp.maximum(rows_idx, 0)]
        received = jnp.where((rows_idx >= 0)[..., None], received, jnp.zeros_like(received))
        targets_raw = dst_all[dom_index]
        targets = jnp.maximum(targets_raw, 0)
        valid = (targets_raw >= 0).astype(jnp.float32)[..., None]
        mesh_part = mesh_all[dom_index]
        node_proj = matmul(mesh_part, w_mesh)
        preact = received.reshape(N_FEAT, N_DOM * CAP, D).astype(jnp.float32) + node_proj[targets]
        hidden, normed, scaling = edge_forward(preact, w_enc2)
        return (mesh_part, targets, valid, preact, hidden, normed, scaling)

    def encode(dom_index):
        mesh_part, targets, valid, preact, hidden, normed, scaling = encoder_values(dom_index)
        summed = jax.ops.segment_sum((normed * valid).reshape(-1, D), targets.reshape(-1), num_segments=part_rows)
        return (mesh_part.astype(jnp.float32) + summed).astype(jnp.bfloat16)
    latent = lax.map(encode, dom_ids)
    hal_idx = hal_send.reshape(N_DOM, N_DOM, HCAP)
    src_all = proc_src.reshape(N_DOM, N_FEAT, E_DEV)
    dstp_all = proc_dst.reshape(N_DOM, N_FEAT, E_DEV)
    cot_all = cotangent.reshape(N_DOM, part_rows, D)

    def process(carry, dom_index):
        node_rows = latent[dom_index]
        wanted = hal_idx[:, dom_index, :]
        halo_rows = latent[dom_ids[:, None], jnp.maximum(wanted, 0)]
        halo_rows = jnp.where((wanted >= 0)[..., None], halo_rows, jnp.zeros_like(halo_rows))
        lookup = jnp.concatenate([node_rows, halo_rows.reshape(N_DOM * HCAP, D)], axis=0)
        sources = src_all[dom_index]
        targets = dstp_all[dom_index]
        src_rows = lookup[sources]
        dst_rows = node_rows[targets]
        preact = matmul(src_rows, w_src) + matmul(dst_rows, w_dst)
        hidden, normed, scaling = edge_forward(preact, w_proc2)
        summed = jax.ops.segment_sum(normed.reshape(-1, D), targets.reshape(-1), num_segments=part_rows)
        out_part = (node_rows.astype(jnp.float32) + summed).astype(jnp.bfloat16)
        cot_rows = cot_all[dom_index].astype(jnp.float32)
        grad_mid = norm_back(normed, scaling, cot_rows[targets]).astype(jnp.bfloat16)
        grad_pre = (matmul_t(grad_mid, w_proc2) * silu_slope(preact)).astype(jnp.bfloat16)
        flat_pre = grad_pre.reshape(-1, D)
        g_lookup = jax.ops.segment_sum(matmul_t(flat_pre, w_src), sources.reshape(-1), num_segments=table_rows)
        g_node = cot_rows + g_lookup[:part_rows] + jax.ops.segment_sum(matmul_t(flat_pre, w_dst), targets.reshape(-1), num_segments=part_rows)
        pieces = (outer_batch(hidden, grad_mid), outer_batch(src_rows, grad_pre), outer_batch(dst_rows, grad_pre))
        carry = (carry[0] + rounded_sum(pieces[0]), carry[1] + rounded_sum(pieces[1]), carry[2] + rounded_sum(pieces[2]))
        return (carry, (out_part, g_node, g_lookup[part_rows:].reshape(N_DOM, HCAP, D)))
    proc_sums, (out_all, g_node_all, g_halo_all) = lax.scan(process, (zero_square, zero_square, zero_square), dom_ids)
    back_idx = jnp.transpose(hal_idx, (1, 0, 2))
    segment = dom_ids[None, :, None] * part_rows + jnp.maximum(back_idx, 0)
    contrib = jnp.where((back_idx >= 0)[..., None], g_halo_all, jnp.zeros_like(g_halo_all))
    node_grad = g_node_all.reshape(N_DOM * part_rows, D) + jax.ops.segment_sum(contrib.reshape(-1, D), segment.reshape(-1), num_segments=N_DOM * part_rows)
    node_grad = node_grad.reshape(N_DOM, part_rows, D)

    def encode_back(carry, dom_index):
        mesh_part, targets, valid, preact, hidden, normed, scaling = encoder_values(dom_index)
        g_nodes = node_grad[dom_index]
        grad_mid = norm_back(normed, scaling, g_nodes[targets] * valid).astype(jnp.bfloat16)
        grad_pre = (matmul_t(grad_mid, w_enc2) * silu_slope(preact)).astype(jnp.bfloat16)
        back_mesh = jax.ops.segment_sum(matmul_t(grad_pre.reshape(-1, D), w_mesh), targets.reshape(-1), num_segments=part_rows)
        g_mesh_part = (g_nodes + back_mesh).astype(jnp.bfloat16)
        carry = (carry[0] + rounded_sum(outer_batch(hidden, grad_mid)), carry[1] + rounded_sum(outer_batch(mesh_part[targets], grad_pre)))
        return (carry, (g_mesh_part, grad_pre.reshape(N_FEAT, N_DOM, CAP, D)))
    enc_sums, (g_mesh_all, returned) = lax.scan(encode_back, (zero_square, zero_square), dom_ids)

    def segment_rows(values, indices):
        return jax.ops.segment_sum(values, indices, num_segments=G_DEV)

    def send_back(carry, dom_index):
        grads = jnp.transpose(returned[:, :, dom_index], (1, 0, 2, 3)).reshape(N_FEAT, N_DOM * CAP, D)
        devices = dom_index * N_FEAT + feat_ids
        rows_idx = send_idx[devices].reshape(N_FEAT, N_DOM * CAP)
        row_pick = jnp.maximum(rows_idx, 0)
        grid_rows = grid_dev[devices[:, None], row_pick]
        back_rows = matmul_t(grads, w_grid) * (rows_idx >= 0).astype(jnp.float32)[..., None]
        g_grid_part = jax.vmap(segment_rows)(back_rows, row_pick).astype(jnp.bfloat16)
        return (carry + rounded_sum(outer_batch(grid_rows, grads)), g_grid_part)
    grid_sum, g_grid_all = lax.scan(send_back, zero_square, dom_ids)
    return (out_all.reshape(N_DOM * part_rows, D), g_grid_all.reshape(device_count * G_DEV, D), g_mesh_all.reshape(N_DOM * part_rows, D), factor * grid_sum, factor * enc_sums[1], factor * enc_sums[0], factor * proc_sums[1], factor * proc_sums[2], factor * proc_sums[0])
```

```python
import functools
import math

import jax
import jax.numpy as jnp
from jax import lax
from jax.experimental import pallas as pl
from jax.experimental.pallas import tpu as pltpu
from jax.sharding import Mesh
from jax.sharding import PartitionSpec as P

DOM = ("z", "x", "c")
ALL = ("z", "x", "c", "y")
EPS = 1e-05
BF = jnp.bfloat16
F32 = jnp.float32
PAD = 16


def call(kernel, outs, *operands):
    return pl.pallas_call(
        kernel,
        out_shape=tuple(jax.ShapeDtypeStruct(s, d) for s, d in outs),
        in_specs=[pl.BlockSpec(memory_space=pltpu.VMEM)] * len(operands),
        out_specs=tuple(pl.BlockSpec(memory_space=pltpu.VMEM) for _ in outs),
        compiler_params=pltpu.CompilerParams(vmem_limit_bytes=48 * 1024 * 1024),
    )(*operands)


def exchange(array, axes):
    return lax.all_to_all(array, axes, 0, 0, tiled=True)


def dot(left, right):
    return jnp.dot(left, right, preferred_element_type=F32)


def dot_t(left, right):
    return lax.dot_general(left, right, (((1,), (1,)), ((), ())), preferred_element_type=F32)


def outer(left, right):
    return lax.dot_general(left, right, (((0,), (0,)), ((), ())), preferred_element_type=F32)


def one_hot(column, count):
    places = lax.broadcasted_iota(jnp.int32, (column.shape[0], count), 1)
    return jnp.where(places == column, 1.0, 0.0).astype(BF)


def slots_hot(indices, count):
    width = indices.shape[1]
    return jnp.concatenate([one_hot(indices[:, c : c + 1], count) for c in range(width)], axis=0)


def slot_rows(wide, width):
    return jnp.concatenate(
        [wide[:, c * width : (c + 1) * width] for c in range(wide.shape[1] // width)], axis=0
    )


def wide_rows(rows, count):
    each = rows.shape[0] // count
    return jnp.concatenate([rows[c * each : (c + 1) * each] for c in range(count)], axis=1)


def whole(ref, at, rows):
    return jnp.concatenate(
        [ref[y, at * rows : (at + 1) * rows, :] for y in range(ref.shape[0])], axis=0
    )


def sigmoid(v):
    return 1.0 / (1.0 + jnp.exp(-v))


def layer_norm(values):
    center = values - jnp.mean(values, axis=-1, keepdims=True)
    spread = jnp.mean(center * center, axis=-1, keepdims=True)
    scaling = lax.rsqrt(spread + EPS)
    return (center * scaling, scaling)


def norm_back(normed, scaling, upstream):
    inner = jnp.mean(upstream, axis=-1, keepdims=True)
    along = jnp.mean(upstream * normed, axis=-1, keepdims=True)
    return scaling * (upstream - inner - normed * along)


def pick_kernel(send_ref, grid_ref, out_ref):
    grid = grid_ref[...]
    width = grid.shape[1]
    for c in range(send_ref.shape[1]):
        hot = one_hot(send_ref[:, c : c + 1], grid.shape[0])
        out_ref[:, c * width : (c + 1) * width] = dot(hot, grid).astype(BF)


def encode_kernel(rows, recv_ref, dst_ref, gath_ref, mesh_ref, sum_ref, pre_ref, norm_ref, scale_ref):
    width = mesh_ref.shape[1]
    mesh_part = mesh_ref[...]
    received = slot_rows(recv_ref[...], width)
    hot = slots_hot(dst_ref[...], mesh_part.shape[0])
    projected = dot(received, whole(gath_ref, 0, rows)).astype(BF)
    nodes = dot(hot, mesh_part).astype(BF)
    preact = projected.astype(F32) + dot(nodes, whole(gath_ref, 1, rows))
    pre_ref[...] = preact
    hidden = (preact * sigmoid(preact)).astype(BF)
    normed, scaling = layer_norm(dot(hidden, whole(gath_ref, 2, rows)))
    norm_ref[...] = normed
    scale_ref[...] = scaling
    partial_sum = outer(hot, normed.astype(BF)).astype(BF)
    for y in range(sum_ref.shape[0]):
        sum_ref[y] = partial_sum


def latent_kernel(sums_ref, mesh_ref, send_ref, latent_ref, halo_ref):
    total = sums_ref[0].astype(F32)
    for y in range(1, sums_ref.shape[0]):
        total = total + sums_ref[y].astype(F32)
    latent = (mesh_ref[...].astype(F32) + total).astype(BF)
    latent_ref[...] = latent
    halo_ref[...] = dot(one_hot(send_ref[...], latent.shape[0]), latent).astype(BF)


def process_kernel(
    rows, own, latent_ref, halo_ref, edge_ref, gath_ref, cot_ref, pay_ref, back_ref, local_ref, term_ref
):
    latent = latent_ref[...]
    table = jnp.concatenate([latent, halo_ref[...]], axis=0)
    nodes = latent.shape[0]
    hot_src = one_hot(edge_ref[:, 0:1], table.shape[0])
    hot_dst = one_hot(edge_ref[:, 1:2], nodes)
    w_src, w_dst, w_out = [whole(gath_ref, k, rows) for k in range(3)]
    src_rows = dot(hot_src, table).astype(BF)
    dst_rows = dot(hot_dst, latent).astype(BF)
    preact = dot(src_rows, w_src) + dot(dst_rows, w_dst)
    gate = sigmoid(preact)
    hidden = (preact * gate).astype(BF)
    normed, scaling = layer_norm(dot(hidden, w_out))
    messages = outer(hot_dst, normed.astype(BF))
    upstream = dot(hot_dst, cot_ref[...])
    mid = norm_back(normed, scaling, upstream).astype(BF)
    grad = (dot_t(mid, w_out) * (gate * (1.0 + preact * (1.0 - gate)))).astype(BF)
    term_ref[...] = outer(hidden, mid).astype(BF)
    at_dst = outer(hot_dst, grad).astype(BF)
    at_src = outer(hot_src, grad)
    local_ref[...] = at_src[:nodes]
    back_ref[...] = at_src[nodes:].astype(BF)
    spare = pay_ref.shape[1] - nodes - own
    for y in range(pay_ref.shape[0]):
        block = messages[y * own : (y + 1) * own]
        block = jnp.concatenate([block, jnp.zeros((spare, block.shape[1]), F32)], axis=0)
        pay_ref[y, :nodes, :] = at_dst
        pay_ref[y, nodes:, :] = block.astype(BF)


def owner_kernel(back_ref, send_ref, local_ref, out_ref):
    nodes = local_ref.shape[0]
    hot = one_hot(send_ref[...], nodes)
    total = (local_ref[...] + outer(hot, back_ref[...])).astype(BF)
    for y in range(out_ref.shape[0]):
        out_ref[y] = total


def backward_kernel(
    rows,
    own,
    src_ref,
    pay_ref,
    cot_ref,
    proc_ref,
    latent_ref,
    enc_ref,
    recv_ref,
    dst_ref,
    mesh_ref,
    pre_ref,
    norm_ref,
    scale_ref,
    proc_term_ref,
    node_ref,
    slot_ref,
    share_ref,
    term_ref,
):
    nodes, width = latent_ref.shape
    count = src_ref.shape[0]
    at_src = src_ref[0].astype(F32)
    at_dst = pay_ref[0, :nodes, :].astype(F32)
    for y in range(1, count):
        at_src = at_src + src_ref[y].astype(F32)
        at_dst = at_dst + pay_ref[y, :nodes, :].astype(F32)
    at_src = at_src.astype(BF)
    at_dst = at_dst.astype(BF)
    node_grad = (
        cot_ref[...].astype(F32)
        + dot_t(at_src, whole(proc_ref, 0, rows))
        + dot_t(at_dst, whole(proc_ref, 1, rows))
    )
    node_ref[...] = node_grad
    hot = slots_hot(dst_ref[...], nodes)
    upstream = dot(hot, node_grad.astype(BF))
    mid = norm_back(norm_ref[...], scale_ref[...], upstream).astype(BF)
    preact = pre_ref[...]
    gate = sigmoid(preact)
    hidden = (preact * gate).astype(BF)
    grad = dot_t(mid, whole(enc_ref, 2, rows)) * (gate * (1.0 + preact * (1.0 - gate)))
    grad = grad.astype(BF)
    slot_ref[...] = wide_rows(grad, recv_ref.shape[1] // width)
    at_node = outer(hot, grad)
    spare = share_ref.shape[1] - own
    for y in range(count):
        block = at_node[y * own : (y + 1) * own]
        block = jnp.concatenate([block, jnp.zeros((spare, width), F32)], axis=0)
        share_ref[y] = block.astype(BF)
    part = 1.0 / count
    latent = latent_ref[...]
    received = slot_rows(recv_ref[...], width)
    terms = (
        outer(received, grad),
        outer(mesh_ref[...], at_node.astype(BF)),
        outer(hidden, mid),
        outer(latent, at_src) * part,
        outer(latent, at_dst) * part,
    )
    for k, term in enumerate(terms):
        term_ref[:, k * width : (k + 1) * width] = term.astype(BF)
    term_ref[:, 5 * width :] = proc_term_ref[...]


def grid_kernel(rows, back_ref, send_ref, enc_ref, out_ref):
    nodes, width = out_ref.shape
    grads = dot_t(slot_rows(back_ref[...], width), whole(enc_ref, 0, rows)).astype(BF)
    out_ref[...] = outer(slots_hot(send_ref[...], nodes), grads).astype(BF)


def sum_kernel(in_ref, out_ref):
    total = in_ref[0].astype(F32)
    for k in range(1, in_ref.shape[0]):
        total = total + in_ref[k].astype(F32)
    out_ref[...] = total.astype(out_ref.dtype)


def finish_kernel(
    rows, own, latent_ref, pay_ref, node_ref, share_ref, enc_ref, out_ref, mesh_ref
):
    nodes = pay_ref.shape[1] - own - (-own % PAD)
    total = pay_ref[0, nodes:, :].astype(F32)
    share = share_ref[0].astype(F32)
    for y in range(1, pay_ref.shape[0]):
        total = total + pay_ref[y, nodes:, :].astype(F32)
        share = share + share_ref[y].astype(F32)
    out_ref[...] = (latent_ref[...].astype(F32) + total[:own]).astype(BF)
    back = dot_t(share.astype(BF), whole(enc_ref, 1, rows))
    mesh_ref[...] = (node_ref[...] + back[:own]).astype(BF)


def per_device(
    grid_feat,
    mesh_feat,
    w_grid,
    w_mesh,
    w_enc2,
    w_src,
    w_dst,
    w_proc2,
    enc_send,
    enc_dst,
    hal_send,
    proc_src,
    proc_dst,
    cotangent,
):
    dom = lax.axis_size(DOM)
    feat = lax.axis_size("y")
    deep = lax.axis_size("z")
    own, width = mesh_feat.shape
    nodes = own * feat
    rows = w_grid.shape[0]
    caps = enc_send.shape[1]
    halo = hal_send.shape[1]
    edges = proc_src.shape[0]
    held = own + (-own % PAD)
    factor = 1.0 / math.sqrt(own * dom * feat)
    me = lax.axis_index("y")
    if halo != feat or held == own or 3 * edges > width:
        raise ValueError("sizes")

    blank = jnp.zeros((held - own, width), BF)
    enc_gath = lax.all_gather(
        jnp.concatenate([w_grid, w_mesh, w_enc2, mesh_feat, blank], axis=0), "y", axis=0
    )
    line = jnp.concatenate([proc_src // 16, proc_src % 16, proc_dst]).astype(BF)
    line = jnp.pad(line, (0, width - 3 * edges))[None]
    proc_gath = lax.all_gather(
        jnp.concatenate([w_src, w_dst, w_proc2, cotangent, line, blank[1:]], axis=0), "y", axis=0
    )

    (outgoing,) = call(pick_kernel, [((dom, caps * width), BF)], enc_send, grid_feat)
    received = exchange(outgoing.reshape(dom, caps, width), DOM).reshape(dom, caps * width)
    mesh_part = enc_gath[:, 3 * rows : 3 * rows + own].reshape(nodes, width)
    slots = dom * caps
    partial_sum, preact, normed, scaling = call(
        functools.partial(encode_kernel, rows),
        [((feat, nodes, width), BF), ((slots, width), F32), ((slots, width), F32), ((slots, 1), F32)],
        received,
        enc_dst,
        enc_gath,
        mesh_part,
    )
    sums = exchange(partial_sum, "y")
    hal_own = lax.dynamic_slice_in_dim(hal_send, me, 1, 1)
    latent, halo_out = call(
        latent_kernel, [((nodes, width), BF), ((dom, width), BF)], sums, mesh_part, hal_own
    )
    halo_rows = exchange(halo_out, DOM)

    cot_part = proc_gath[:, 3 * rows : 3 * rows + own].reshape(nodes, width)
    lines = proc_gath[:, 3 * rows + own].astype(jnp.int32)
    source = lines[:, :edges] * 16 + lines[:, edges : 2 * edges]
    target = lines[:, 2 * edges : 3 * edges]
    slot = source - nodes
    place = jnp.where(slot < 0, source, nodes + slot // halo)
    keeper = jnp.where(slot < 0, jnp.arange(feat, dtype=jnp.int32)[:, None], slot % halo)
    mine = keeper == me
    edge_index = jnp.stack(
        [jnp.where(mine, place, -1).reshape(-1), jnp.where(mine, target, -1).reshape(-1)], axis=1
    )
    payload, halo_back, at_local, proc_term = call(
        functools.partial(process_kernel, rows, own),
        [
            ((feat, nodes + held, width), BF),
            ((dom, width), BF),
            ((nodes, width), F32),
            ((width, width), BF),
        ],
        latent,
        halo_rows,
        edge_index,
        proc_gath,
        cot_part,
    )
    returned = exchange(halo_back, DOM)
    payload = exchange(payload, "y")
    (at_owner,) = call(
        owner_kernel, [((feat, nodes, width), BF)], returned, hal_own, at_local
    )
    at_src = exchange(at_owner, "y")

    node_grad, slot_out, share, terms = call(
        functools.partial(backward_kernel, rows, own),
        [
            ((nodes, width), F32),
            ((dom, caps * width), BF),
            ((feat, held, width), BF),
            ((width, 6 * width), BF),
        ],
        at_src,
        payload,
        cot_part,
        proc_gath,
        latent,
        enc_gath,
        received,
        enc_dst,
        mesh_part,
        preact,
        normed,
        scaling,
        proc_term,
    )
    near = lax.axis_size(("y", "x", "c"))
    thin = width // near
    arrived = exchange(terms.reshape(near, thin, 6 * width), ("y", "x", "c"))
    (level,) = call(sum_kernel, [((thin, 6 * width), BF)], arrived)
    slot_back = exchange(slot_out.reshape(dom, caps, width), DOM).reshape(dom, caps * width)
    share = exchange(share, "y")
    level = exchange(level.reshape(deep, thin // deep, 6 * width), "z")
    mine_sum = level.astype(F32).sum(axis=0).astype(BF)
    deep_rows = exchange(jnp.broadcast_to(mine_sum[None], (deep, *mine_sum.shape)), "z")
    deep_rows = deep_rows.reshape(thin, 6 * width)
    flat = lax.axis_size(("x", "c"))
    totals = exchange(jnp.broadcast_to(deep_rows[None], (flat, *deep_rows.shape)), ("x", "c"))
    totals = totals.reshape(rows, 6 * width).astype(F32) * factor

    (g_grid,) = call(
        functools.partial(grid_kernel, rows), [(grid_feat.shape, BF)], slot_back, enc_send, enc_gath
    )
    out_rows, g_mesh = call(
        functools.partial(finish_kernel, rows, own),
        [((own, width), BF), ((own, width), BF)],
        lax.dynamic_slice_in_dim(latent, me * own, own, 0),
        payload,
        lax.dynamic_slice_in_dim(node_grad, me * own, own, 0),
        share,
        enc_gath,
    )
    return (out_rows, g_grid, g_mesh) + tuple(
        totals[:, k * width : (k + 1) * width] for k in range(6)
    )


def solution(mesh):
    dom, feat = mesh.shape["dom"], mesh.shape["feat"]
    x = 4 if dom % 8 == 0 else 1
    finer = Mesh(mesh.devices.reshape(dom // (2 * x), x, 2, feat), ALL)
    return jax.shard_map(
        per_device,
        mesh=finer,
        in_specs=(
            P(ALL, None),
            P(ALL, None),
            P("y", None),
            P("y", None),
            P("y", None),
            P("y", None),
            P("y", None),
            P("y", None),
            P(ALL, None),
            P(ALL, None),
            P(DOM, None),
            P(ALL),
            P(ALL),
            P(ALL, None),
        ),
        out_specs=(
            P(ALL, None),
            P(ALL, None),
            P(ALL, None),
            P("y", None),
            P("y", None),
            P("y", None),
            P("y", None),
            P("y", None),
            P("y", None),
        ),
        check_vma=False,
    )
```

```python
import functools
import math

import jax
import jax.numpy as jnp
from jax import lax
from jax.experimental import pallas as pl
from jax.experimental.pallas import tpu as pltpu
from jax.sharding import Mesh
from jax.sharding import PartitionSpec as P

DOM = ("z", "x", "c")
ALL = ("z", "x", "c", "y")
EPS = 1e-05
BF = jnp.bfloat16
F32 = jnp.float32
PAD = 16


def call(kernel, outs, *operands, me=None, scratch=()):
    specs = [pl.BlockSpec()] * len(operands)
    if me is not None:
        operands = (me, *operands)
        specs = [pl.BlockSpec(memory_space=pltpu.SMEM), *specs]
    return pl.pallas_call(
        kernel,
        out_shape=tuple(jax.ShapeDtypeStruct(s, d) for s, d in outs),
        in_specs=specs,
        out_specs=tuple(pl.BlockSpec() for _ in outs),
        scratch_shapes=list(scratch),
        compiler_params=pltpu.CompilerParams(vmem_limit_bytes=60 * 1024 * 1024),
    )(*operands)


def onward(blocks):
    n = len(blocks)
    return [blocks[0]] + [
        lax.ppermute(blocks[k], "y", [(i, (i + k) % n) for i in range(n)]) for k in range(1, n)
    ]


def exchange(array, axes):
    return lax.all_to_all(array, axes, 0, 0, tiled=True)


def dot(left, right):
    return jnp.dot(left, right, preferred_element_type=F32)


def dot_t(left, right):
    return lax.dot_general(left, right, (((1,), (1,)), ((), ())), preferred_element_type=F32)


def outer(left, right):
    return lax.dot_general(left, right, (((0,), (0,)), ((), ())), preferred_element_type=F32)


def one_hot(column, count):
    places = lax.broadcasted_iota(jnp.int32, (column.shape[0], count), 1)
    return jnp.where(places == column, 1.0, 0.0).astype(BF)


def slots_hot(indices, count):
    width = indices.shape[1]
    return jnp.concatenate([one_hot(indices[:, c : c + 1], count) for c in range(width)], axis=0)


def slot_rows(wide, width):
    return jnp.concatenate(
        [wide[:, c * width : (c + 1) * width] for c in range(wide.shape[1] // width)], axis=0
    )


def wide_rows(rows, count):
    each = rows.shape[0] // count
    return jnp.concatenate([rows[c * each : (c + 1) * each] for c in range(count)], axis=1)


def whole(ref, at, rows):
    return jnp.concatenate(
        [ref[y, at * rows : (at + 1) * rows, :] for y in range(ref.shape[0])], axis=0
    )


def sigmoid(v):
    return 1.0 / (1.0 + jnp.exp(-v))


def layer_norm(values):
    center = values - jnp.mean(values, axis=-1, keepdims=True)
    spread = jnp.mean(center * center, axis=-1, keepdims=True)
    scaling = lax.rsqrt(spread + EPS)
    return (center * scaling, scaling)


def norm_back(normed, scaling, upstream):
    inner = jnp.mean(upstream, axis=-1, keepdims=True)
    along = jnp.mean(upstream * normed, axis=-1, keepdims=True)
    return scaling * (upstream - inner - normed * along)


def pack_kernel(
    send_ref, grid_ref, src_ref, dst_ref, wg_ref, wm_ref, we_ref, ws_ref, wd_ref, wp_ref, mesh_ref, cot_ref,
    out_ref, enc_ref, proc_ref, line_ref,
):
    grid = grid_ref[...]
    width = grid.shape[1]
    for c in range(send_ref.shape[1]):
        hot = one_hot(send_ref[:, c : c + 1], grid.shape[0])
        out_ref[:, c * width : (c + 1) * width] = dot(hot, grid).astype(BF)
    edges = src_ref.shape[1]
    spare = line_ref.shape[0]
    line_ref[...] = jnp.zeros_like(line_ref)
    place = lax.broadcasted_iota(jnp.int32, (spare, edges), 0)
    source = jnp.broadcast_to(src_ref[...], (spare, edges))
    target = jnp.broadcast_to(dst_ref[...], (spare, edges))
    values = jnp.where(place == 0, source >> 4, jnp.where(place == 1, source & 15, target))
    line_ref[:, :edges] = jnp.where(place < 3, values, 0).astype(F32)
    rows = wg_ref.shape[0]
    for ref, arrays, tail in (
        (enc_ref, (wg_ref, wm_ref, we_ref), mesh_ref),
        (proc_ref, (ws_ref, wd_ref, wp_ref), cot_ref),
    ):
        for k, array in enumerate(arrays):
            ref[k * rows : (k + 1) * rows, :] = array[...]
        both = jnp.concatenate([tail[...].astype(F32), line_ref[...]], axis=0)
        ref[3 * rows :, :] = both.astype(BF)


def node_rows(gath_ref, at, own):
    return jnp.concatenate(
        [gath_ref[y, at:, :].astype(F32)[:own] for y in range(gath_ref.shape[0])], axis=0
    )


def own_column(ref, me):
    table = ref[...]
    column = lax.broadcasted_iota(jnp.int32, table.shape, 1)
    return jnp.sum(jnp.where(column == me, table, 0), axis=1, keepdims=True)


def total_of(refs):
    total = refs[0].astype(F32)
    for block in refs[1:]:
        total = total + block.astype(F32)
    return total


def encode_kernel(rows, own, recv_ref, dst_ref, gath_ref, sum_ref, pre_ref, norm_ref, scale_ref):
    width = gath_ref.shape[2]
    mesh_part = node_rows(gath_ref, 3 * rows, own).astype(BF)
    received = slot_rows(recv_ref[...], width)
    hot = slots_hot(dst_ref[...], mesh_part.shape[0])
    projected = dot(received, whole(gath_ref, 0, rows)).astype(BF)
    nodes = dot(hot, mesh_part).astype(BF)
    preact = projected.astype(F32) + dot(nodes, whole(gath_ref, 1, rows))
    pre_ref[...] = preact
    hidden = (preact * sigmoid(preact)).astype(BF)
    normed, scaling = layer_norm(dot(hidden, whole(gath_ref, 2, rows)))
    norm_ref[...] = normed
    scale_ref[...] = scaling
    partial_sum = outer(hot, normed.astype(BF)).astype(BF)
    for y in range(sum_ref.shape[0]):
        sum_ref[y] = partial_sum


def latent_kernel(rows, own, me_ref, sums_ref, gath_ref, send_ref, latent_ref, halo_ref):
    total = total_of([sums_ref[y] for y in range(sums_ref.shape[0])])
    latent = (node_rows(gath_ref, 3 * rows, own) + total).astype(BF)
    latent_ref[...] = latent
    hot = one_hot(own_column(send_ref, me_ref[0]), latent.shape[0])
    halo_ref[...] = dot(hot, latent).astype(BF)


def deal(me, refs, term_ref, rows, node_ref, own):
    count = len(refs)
    width = refs[0].shape[1]
    terms = term_ref.shape[1] // width
    spare = refs[0].shape[0] - terms * rows - own
    for k, ref in enumerate(refs):
        to = lax.rem(me + k, count)
        at = pl.ds(pl.multiple_of(to * rows, rows), rows)
        for t in range(terms):
            ref[t * rows : (t + 1) * rows, :] = term_ref[at, t * width : (t + 1) * width]
        block = node_ref[pl.ds(pl.multiple_of(to * own, 8), own), :]
        block = jnp.concatenate([block, jnp.zeros((spare, width), F32)], axis=0)
        ref[terms * rows :, :] = block.astype(BF)


def process_kernel(
    rows, own, me_ref, latent_ref, halo_ref, edge_ref, gath_ref,
    back_ref, local_ref, dst_ref, b0_ref, b1_ref, b2_ref, b3_ref, term_ref, node_ref,
):
    latent = latent_ref[...]
    table = jnp.concatenate([latent, halo_ref[...]], axis=0)
    nodes, width = latent.shape
    hot_src = one_hot(edge_ref[:, 0:1], table.shape[0])
    hot_dst = one_hot(edge_ref[:, 1:2], nodes)
    w_src, w_dst, w_out = [whole(gath_ref, k, rows) for k in range(3)]
    src_rows = dot(hot_src, table).astype(BF)
    dst_rows = dot(hot_dst, latent).astype(BF)
    preact = dot(src_rows, w_src) + dot(dst_rows, w_dst)
    gate = sigmoid(preact)
    hidden = (preact * gate).astype(BF)
    normed, scaling = layer_norm(dot(hidden, w_out))
    node_ref[...] = outer(hot_dst, normed.astype(BF))
    upstream = dot(hot_dst, node_rows(gath_ref, 3 * rows, own).astype(BF))
    mid = norm_back(normed, scaling, upstream).astype(BF)
    grad = (dot_t(mid, w_out) * (gate * (1.0 + preact * (1.0 - gate)))).astype(BF)
    at_dst = outer(hot_dst, grad).astype(BF)
    dst_ref[...] = at_dst
    at_src = outer(hot_src, grad)
    local_ref[...] = at_src[:nodes]
    back_ref[...] = at_src[nodes:].astype(BF)
    term_ref[:, :width] = outer(latent, at_dst).astype(BF)
    term_ref[:, width:] = outer(hidden, mid).astype(BF)
    deal(me_ref[0], (b0_ref, b1_ref, b2_ref, b3_ref), term_ref, rows, node_ref, own)


def owner_kernel(rows, me_ref, back_ref, send_ref, local_ref, dst_ref, gath_ref, out_ref, src_ref):
    hot = one_hot(own_column(send_ref, me_ref[0]), local_ref.shape[0])
    at_src = (local_ref[...] + outer(hot, back_ref[...])).astype(BF)
    src_ref[...] = at_src
    total = dot_t(at_src, whole(gath_ref, 0, rows)) + dot_t(dst_ref[...], whole(gath_ref, 1, rows))
    total = total.astype(BF)
    for y in range(out_ref.shape[0]):
        out_ref[y] = total


def backward_kernel(
    rows, own, me_ref, node_in_ref, proc_ref, latent_ref, src_ref, enc_ref, recv_ref, dst_ref,
    pre_ref, norm_ref, scale_ref,
    node_ref, slot_ref, b0_ref, b1_ref, b2_ref, b3_ref, term_ref, share_ref,
):
    nodes, width = latent_ref.shape
    node_grad = node_rows(proc_ref, 3 * rows, own) + total_of(
        [node_in_ref[y] for y in range(node_in_ref.shape[0])]
    )
    node_ref[...] = node_grad
    hot = slots_hot(dst_ref[...], nodes)
    upstream = dot(hot, node_grad.astype(BF))
    mid = norm_back(norm_ref[...], scale_ref[...], upstream).astype(BF)
    preact = pre_ref[...]
    gate = sigmoid(preact)
    hidden = (preact * gate).astype(BF)
    grad = dot_t(mid, whole(enc_ref, 2, rows)) * (gate * (1.0 + preact * (1.0 - gate)))
    grad = grad.astype(BF)
    slot_ref[...] = wide_rows(grad, recv_ref.shape[1] // width)
    at_node = outer(hot, grad)
    share_ref[...] = at_node
    terms = (
        outer(slot_rows(recv_ref[...], width), grad),
        outer(node_rows(enc_ref, 3 * rows, own).astype(BF), at_node.astype(BF)),
        outer(hidden, mid),
        outer(latent_ref[...], src_ref[...]),
    )
    for k, term in enumerate(terms):
        term_ref[:, k * width : (k + 1) * width] = term.astype(BF)
    deal(me_ref[0], (b0_ref, b1_ref, b2_ref, b3_ref), term_ref, rows, share_ref, own)


def grid_kernel(rows, back_ref, send_ref, enc_ref, out_ref):
    nodes, width = out_ref.shape
    grads = dot_t(slot_rows(back_ref[...], width), whole(enc_ref, 0, rows)).astype(BF)
    out_ref[...] = outer(slots_hot(send_ref[...], nodes), grads).astype(BF)


def out_kernel(rows, me_ref, latent_ref, b0_ref, b1_ref, b2_ref, b3_ref, out_ref, sum_ref):
    total = total_of([b0_ref[...], b1_ref[...], b2_ref[...], b3_ref[...]])
    sum_ref[...] = total[: 2 * rows].astype(BF)
    own, nodes = out_ref.shape[0], latent_ref.shape[0]
    mine = lax.broadcasted_iota(jnp.int32, (own, 1), 0) + me_ref[0] * own
    latent = dot(one_hot(mine, nodes), latent_ref[...])
    out_ref[...] = (latent + total[2 * rows : 2 * rows + own]).astype(BF)


def mesh_kernel(
    rows, me_ref, sum_ref, node_ref, enc_ref, b0_ref, b1_ref, b2_ref, b3_ref, mesh_ref, pay_ref
):
    total = total_of([b0_ref[...], b1_ref[...], b2_ref[...], b3_ref[...]])
    own, width = mesh_ref.shape
    for k in range(4):
        pay_ref[:, k * width : (k + 1) * width] = total[k * rows : (k + 1) * rows].astype(BF)
    pay_ref[:, 4 * width : 5 * width] = sum_ref[:rows, :]
    pay_ref[:, 5 * width :] = sum_ref[rows:, :]
    back = dot_t(total[4 * rows :].astype(BF), whole(enc_ref, 1, rows))[:own]
    node = node_ref[pl.ds(pl.multiple_of(me_ref[0] * own, 8), own), :]
    mesh_ref[...] = (node + back).astype(BF)


def sum_kernel(in_ref, out_ref):
    out_ref[...] = total_of([in_ref[k] for k in range(in_ref.shape[0])]).astype(out_ref.dtype)


def split_kernel(factor, in_ref, *out_refs):
    count, thin, _ = in_ref.shape
    width = out_refs[0].shape[1]
    for r in range(count):
        for k, ref in enumerate(out_refs):
            block = in_ref[r, :, k * width : (k + 1) * width]
            ref[r * thin : (r + 1) * thin, :] = block.astype(F32) * factor


def per_device(
    grid_feat,
    mesh_feat,
    w_grid,
    w_mesh,
    w_enc2,
    w_src,
    w_dst,
    w_proc2,
    enc_send,
    enc_dst,
    hal_send,
    proc_src,
    proc_dst,
    cotangent,
):
    dom = lax.axis_size(DOM)
    feat = lax.axis_size("y")
    deep = lax.axis_size("z")
    own, width = mesh_feat.shape
    nodes = own * feat
    rows = w_grid.shape[0]
    caps = enc_send.shape[1]
    halo = hal_send.shape[1]
    edges = proc_src.shape[0]
    held = own + (-own % PAD)
    factor = 1.0 / math.sqrt(own * dom * feat)
    index = lax.axis_index("y")
    me = index.reshape(1)
    if halo != feat or held - own < 8 or edges > width:
        raise ValueError("sizes")
    bind = functools.partial

    packed = ((3 * rows + held, width), BF)
    outgoing, enc_pack, proc_pack = call(
        pack_kernel,
        [((dom, caps * width), BF), packed, packed],
        enc_send,
        grid_feat,
        proc_src.reshape(1, edges),
        proc_dst.reshape(1, edges),
        w_grid,
        w_mesh,
        w_enc2,
        w_src,
        w_dst,
        w_proc2,
        mesh_feat,
        cotangent,
        scratch=[pltpu.VMEM((held - own, width), F32)],
    )
    received = exchange(outgoing.reshape(dom, caps, width), DOM).reshape(dom, caps * width)
    enc_gath = lax.all_gather(enc_pack, "y", axis=0)
    proc_gath = lax.all_gather(proc_pack, "y", axis=0)

    slots = dom * caps
    partial_sum, preact, normed, scaling = call(
        bind(encode_kernel, rows, own),
        [((feat, nodes, width), BF), ((slots, width), F32), ((slots, width), F32), ((slots, 1), F32)],
        received,
        enc_dst,
        enc_gath,
    )
    sums = exchange(partial_sum, "y")
    latent, halo_out = call(
        bind(latent_kernel, rows, own),
        [((nodes, width), BF), ((dom, width), BF)],
        sums,
        enc_gath,
        hal_send,
        me=me,
    )
    halo_rows = exchange(halo_out, DOM)

    lines = enc_gath[:, 3 * rows + own : 3 * rows + own + 3, :edges].astype(jnp.int32)
    source = lines[:, 0] * 16 + lines[:, 1]
    slot = source - nodes
    place = jnp.where(slot < 0, source, nodes + slot // halo)
    keeper = jnp.where(slot < 0, jnp.arange(feat, dtype=jnp.int32)[:, None], slot % halo)
    mine = keeper == index
    edge_index = jnp.stack(
        [jnp.where(mine, place, -1).reshape(-1), jnp.where(mine, lines[:, 2], -1).reshape(-1)], axis=1
    )
    blocks = [((2 * rows + held, width), BF)] * 4
    halo_back, at_local, at_dst, *first = call(
        bind(process_kernel, rows, own),
        [((dom, width), BF), ((nodes, width), F32), ((nodes, width), BF)] + blocks,
        latent,
        halo_rows,
        edge_index,
        proc_gath,
        me=me,
        scratch=[pltpu.VMEM((width, 2 * width), BF), pltpu.VMEM((nodes, width), F32)],
    )
    returned = exchange(halo_back, DOM)
    returned, *first = lax.optimization_barrier((returned, *onward(first)))
    node_part, at_src = call(
        bind(owner_kernel, rows),
        [((feat, nodes, width), BF), ((nodes, width), BF)],
        returned,
        hal_send,
        at_local,
        at_dst,
        proc_gath,
        me=me,
    )
    node_in = exchange(node_part, "y")

    blocks = [((4 * rows + held, width), BF)] * 4
    node_grad, slot_out, *second = call(
        bind(backward_kernel, rows, own),
        [((nodes, width), F32), ((dom, caps * width), BF)] + blocks,
        node_in,
        proc_gath,
        latent,
        at_src,
        enc_gath,
        received,
        enc_dst,
        preact,
        normed,
        scaling,
        me=me,
        scratch=[pltpu.VMEM((width, 4 * width), BF), pltpu.VMEM((nodes, width), F32)],
    )
    slot_back = exchange(slot_out.reshape(dom, caps, width), DOM).reshape(dom, caps * width)
    slot_back, *second = lax.optimization_barrier((slot_back, *onward(second)))
    out_rows, first_sum = call(
        bind(out_kernel, rows), [((own, width), BF), ((2 * rows, width), BF)], latent, *first, me=me
    )
    g_mesh, level = call(
        bind(mesh_kernel, rows),
        [((own, width), BF), ((rows, 6 * width), BF)],
        first_sum,
        node_grad,
        enc_gath,
        *second,
        me=me,
    )
    near = lax.axis_size(("x", "c"))
    thin = rows // near
    level = exchange(level.reshape(near, thin, 6 * width), ("x", "c"))
    (level,) = call(sum_kernel, [((thin, 6 * width), BF)], level)
    level = exchange(level.reshape(deep, thin // deep, 6 * width), "z")
    mine_sum = level.astype(F32).sum(axis=0).astype(BF)
    level = exchange(jnp.broadcast_to(mine_sum[None], (deep, *mine_sum.shape)), "z")
    level = level.reshape(thin, 6 * width)
    totals = exchange(jnp.broadcast_to(level[None], (near, *level.shape)), ("x", "c"))
    totals = call(bind(split_kernel, factor), [((rows, width), F32)] * 6, totals)
    (g_grid,) = call(
        bind(grid_kernel, rows), [(grid_feat.shape, BF)], slot_back, enc_send, enc_gath
    )
    return (out_rows, g_grid, g_mesh) + tuple(totals)


def solution(mesh):
    dom, feat = mesh.shape["dom"], mesh.shape["feat"]
    x = 4 if dom % 8 == 0 else 1
    finer = Mesh(mesh.devices.reshape(dom // (2 * x), x, 2, feat), ALL)
    return jax.shard_map(
        per_device,
        mesh=finer,
        in_specs=(
            P(ALL, None),
            P(ALL, None),
            P("y", None),
            P("y", None),
            P("y", None),
            P("y", None),
            P("y", None),
            P("y", None),
            P(ALL, None),
            P(ALL, None),
            P(DOM, None),
            P(ALL),
            P(ALL),
            P(ALL, None),
        ),
        out_specs=(
            P(ALL, None),
            P(ALL, None),
            P(ALL, None),
            P("y", None),
            P("y", None),
            P("y", None),
            P("y", None),
            P("y", None),
            P("y", None),
        ),
        check_vma=False,
    )
```

```python
import functools
import math

import jax
import jax.numpy as jnp
from jax import lax
from jax.experimental import pallas as pl
from jax.experimental.pallas import tpu as pltpu
from jax.sharding import Mesh
from jax.sharding import PartitionSpec as P

DOM = ("z", "x", "c")
ALL = ("z", "x", "c", "y")
EPS = 1e-05
BF = jnp.bfloat16
F32 = jnp.float32
PAD = 16


def call(kernel, outs, *operands, me=None, scratch=()):
    specs = [pl.BlockSpec()] * len(operands)
    if me is not None:
        operands = (me, *operands)
        specs = [pl.BlockSpec(memory_space=pltpu.SMEM), *specs]
    return pl.pallas_call(
        kernel,
        out_shape=tuple(jax.ShapeDtypeStruct(s, d) for s, d in outs),
        in_specs=specs,
        out_specs=tuple(pl.BlockSpec() for _ in outs),
        scratch_shapes=list(scratch),
        compiler_params=pltpu.CompilerParams(vmem_limit_bytes=60 * 1024 * 1024),
    )(*operands)


def onward(blocks):
    n = len(blocks)
    return [blocks[0]] + [
        lax.ppermute(blocks[k], "y", [(i, (i + k) % n) for i in range(n)]) for k in range(1, n)
    ]


def two_rounds(block):
    n = lax.axis_size("y")
    other = lax.ppermute(block, "y", [(i, i ^ 1) for i in range(n)])
    (both,) = call(add_kernel, [(block.shape, block.dtype)], block, other)
    return both, lax.ppermute(both, "y", [(i, i ^ 2) for i in range(n)])


def exchange(array, axes):
    return lax.all_to_all(array, axes, 0, 0, tiled=True)


def dot(left, right):
    return jnp.dot(left, right, preferred_element_type=F32)


def dot_t(left, right):
    return lax.dot_general(left, right, (((1,), (1,)), ((), ())), preferred_element_type=F32)


def outer(left, right):
    return lax.dot_general(left, right, (((0,), (0,)), ((), ())), preferred_element_type=F32)


def one_hot(row, count):
    places = lax.broadcasted_iota(jnp.int32, (count, row.shape[1]), 0)
    return jnp.where(places == row, 1.0, 0.0).astype(BF)


def slots_hot(indices, count):
    return jnp.concatenate(
        [one_hot(indices[c : c + 1, :], count) for c in range(indices.shape[0])], axis=1
    )


def slot_rows(wide, width):
    return jnp.concatenate(
        [wide[:, c * width : (c + 1) * width] for c in range(wide.shape[1] // width)], axis=0
    )


def wide_rows(rows, count):
    each = rows.shape[0] // count
    return jnp.concatenate([rows[c * each : (c + 1) * each] for c in range(count)], axis=1)


def whole(ref, at, rows):
    return jnp.concatenate(
        [ref[y, at * rows : (at + 1) * rows, :] for y in range(ref.shape[0])], axis=0
    )


def sigmoid(v):
    return 1.0 / (1.0 + jnp.exp(-v))


def layer_norm(values):
    center = values - jnp.mean(values, axis=-1, keepdims=True)
    spread = jnp.mean(center * center, axis=-1, keepdims=True)
    scaling = lax.rsqrt(spread + EPS)
    return (center * scaling, scaling)


def norm_back(normed, scaling, upstream):
    inner = jnp.mean(upstream, axis=-1, keepdims=True)
    along = jnp.mean(upstream * normed, axis=-1, keepdims=True)
    return scaling * (upstream - inner - normed * along)


def pack_kernel(
    send_ref, grid_ref, src_ref, dst_ref, wg_ref, wm_ref, we_ref, ws_ref, wd_ref, wp_ref, mesh_ref, cot_ref,
    out_ref, enc_ref, proc_ref, line_ref,
):
    grid = grid_ref[...]
    width = grid.shape[1]
    for c in range(send_ref.shape[0]):
        hot = one_hot(send_ref[c : c + 1, :], grid.shape[0])
        out_ref[:, c * width : (c + 1) * width] = outer(hot, grid).astype(BF)
    edges = src_ref.shape[1]
    spare = line_ref.shape[0]
    line_ref[...] = jnp.zeros_like(line_ref)
    place = lax.broadcasted_iota(jnp.int32, (spare, edges), 0)
    source = jnp.broadcast_to(src_ref[...], (spare, edges))
    target = jnp.broadcast_to(dst_ref[...], (spare, edges))
    values = jnp.where(place == 0, source >> 4, jnp.where(place == 1, source & 15, target))
    line_ref[:, :edges] = jnp.where(place < 3, values, 0).astype(F32)
    rows = wg_ref.shape[0]
    for ref, arrays, tail in (
        (enc_ref, (wg_ref, wm_ref, we_ref), mesh_ref),
        (proc_ref, (ws_ref, wd_ref, wp_ref), cot_ref),
    ):
        for k, array in enumerate(arrays):
            ref[k * rows : (k + 1) * rows, :] = array[...]
        both = jnp.concatenate([tail[...].astype(F32), line_ref[...]], axis=0)
        ref[3 * rows :, :] = both.astype(BF)


def node_rows(gath_ref, at, own):
    return jnp.concatenate(
        [gath_ref[y, at:, :].astype(F32)[:own] for y in range(gath_ref.shape[0])], axis=0
    )


def own_row(ref, me):
    table = ref[...]
    place = lax.broadcasted_iota(jnp.int32, table.shape, 0)
    return jnp.sum(jnp.where(place == me, table, 0), axis=0, keepdims=True)


def total_of(refs):
    total = refs[0].astype(F32)
    for block in refs[1:]:
        total = total + block.astype(F32)
    return total


def encode_kernel(rows, own, recv_ref, dst_ref, gath_ref, sum_ref, pre_ref, norm_ref, scale_ref):
    width = gath_ref.shape[2]
    mesh_part = node_rows(gath_ref, 3 * rows, own).astype(BF)
    received = slot_rows(recv_ref[...], width)
    hot = slots_hot(dst_ref[...], mesh_part.shape[0])
    projected = dot(received, whole(gath_ref, 0, rows)).astype(BF)
    nodes = outer(hot, mesh_part).astype(BF)
    preact = projected.astype(F32) + dot(nodes, whole(gath_ref, 1, rows))
    pre_ref[...] = preact
    hidden = (preact * sigmoid(preact)).astype(BF)
    normed, scaling = layer_norm(dot(hidden, whole(gath_ref, 2, rows)))
    norm_ref[...] = normed
    scale_ref[...] = scaling
    sum_ref[...] = dot(hot, normed.astype(BF)).astype(BF)


def add_kernel(left_ref, right_ref, out_ref):
    out_ref[...] = total_of([left_ref[...], right_ref[...]]).astype(out_ref.dtype)


def latent_kernel(rows, own, me_ref, near_ref, far_ref, gath_ref, send_ref, latent_ref, halo_ref):
    total = total_of([near_ref[...], far_ref[...]])
    latent = (node_rows(gath_ref, 3 * rows, own) + total).astype(BF)
    latent_ref[...] = latent
    hot = one_hot(own_row(send_ref, me_ref[0]), latent.shape[0])
    halo_ref[...] = outer(hot, latent).astype(BF)


def deal(me, refs, term_ref, rows, node_ref, own):
    count = len(refs)
    width = refs[0].shape[1]
    terms = term_ref.shape[1] // width
    spare = refs[0].shape[0] - terms * rows - own
    for k, ref in enumerate(refs):
        to = lax.rem(me + k, count)
        at = pl.ds(pl.multiple_of(to * rows, rows), rows)
        for t in range(terms):
            ref[t * rows : (t + 1) * rows, :] = term_ref[at, t * width : (t + 1) * width]
        block = node_ref[pl.ds(pl.multiple_of(to * own, 8), own), :]
        block = jnp.concatenate([block, jnp.zeros((spare, width), F32)], axis=0)
        ref[terms * rows :, :] = block.astype(BF)


def process_kernel(
    rows, own, latent_ref, halo_ref, source_ref, target_ref, gath_ref,
    back_ref, local_ref, dst_ref, node_ref, hidden_ref, mid_ref,
):
    latent = latent_ref[...]
    table = jnp.concatenate([latent, halo_ref[...]], axis=0)
    nodes = latent.shape[0]
    hot_src = one_hot(source_ref[...], table.shape[0])
    hot_dst = one_hot(target_ref[...], nodes)
    w_src, w_dst, w_out = [whole(gath_ref, k, rows) for k in range(3)]
    src_rows = outer(hot_src, table).astype(BF)
    dst_rows = outer(hot_dst, latent).astype(BF)
    preact = dot(src_rows, w_src) + dot(dst_rows, w_dst)
    gate = sigmoid(preact)
    hidden = (preact * gate).astype(BF)
    hidden_ref[...] = hidden
    normed, scaling = layer_norm(dot(hidden, w_out))
    node_ref[...] = dot(hot_dst, normed.astype(BF))
    upstream = outer(hot_dst, node_rows(gath_ref, 3 * rows, own).astype(BF))
    mid = norm_back(normed, scaling, upstream).astype(BF)
    mid_ref[...] = mid
    grad = (dot_t(mid, w_out) * (gate * (1.0 + preact * (1.0 - gate)))).astype(BF)
    dst_ref[...] = dot(hot_dst, grad).astype(BF)
    at_src = dot(hot_src, grad)
    local_ref[...] = at_src[:nodes]
    back_ref[...] = at_src[nodes:].astype(BF)


def process_terms_kernel(
    rows, own, me_ref, latent_ref, dst_ref, hidden_ref, mid_ref, node_ref,
    b0_ref, b1_ref, b2_ref, b3_ref, term_ref,
):
    width = latent_ref.shape[1]
    term_ref[:, :width] = outer(latent_ref[...], dst_ref[...]).astype(BF)
    term_ref[:, width:] = outer(hidden_ref[...], mid_ref[...]).astype(BF)
    deal(me_ref[0], (b0_ref, b1_ref, b2_ref, b3_ref), term_ref, rows, node_ref, own)


def owner_kernel(rows, me_ref, back_ref, send_ref, local_ref, dst_ref, gath_ref, out_ref, src_ref):
    hot = one_hot(own_row(send_ref, me_ref[0]), local_ref.shape[0])
    at_src = (local_ref[...] + dot(hot, back_ref[...])).astype(BF)
    src_ref[...] = at_src
    total = dot_t(at_src, whole(gath_ref, 0, rows)) + dot_t(dst_ref[...], whole(gath_ref, 1, rows))
    out_ref[...] = total.astype(BF)


def backward_kernel(
    rows, own, me_ref, near_ref, far_ref, proc_ref, latent_ref, src_ref, enc_ref, recv_ref, dst_ref,
    pre_ref, norm_ref, scale_ref,
    node_ref, slot_ref, b0_ref, b1_ref, b2_ref, b3_ref, term_ref, share_ref,
):
    nodes, width = latent_ref.shape
    node_grad = node_rows(proc_ref, 3 * rows, own) + total_of([near_ref[...], far_ref[...]])
    node_ref[...] = node_grad
    hot = slots_hot(dst_ref[...], nodes)
    upstream = outer(hot, node_grad.astype(BF))
    mid = norm_back(norm_ref[...], scale_ref[...], upstream).astype(BF)
    preact = pre_ref[...]
    gate = sigmoid(preact)
    hidden = (preact * gate).astype(BF)
    grad = dot_t(mid, whole(enc_ref, 2, rows)) * (gate * (1.0 + preact * (1.0 - gate)))
    grad = grad.astype(BF)
    slot_ref[...] = wide_rows(grad, recv_ref.shape[1] // width)
    at_node = dot(hot, grad)
    share_ref[...] = at_node
    terms = (
        outer(slot_rows(recv_ref[...], width), grad),
        outer(node_rows(enc_ref, 3 * rows, own).astype(BF), at_node.astype(BF)),
        outer(hidden, mid),
        outer(latent_ref[...], src_ref[...]),
    )
    for k, term in enumerate(terms):
        term_ref[:, k * width : (k + 1) * width] = term.astype(BF)
    deal(me_ref[0], (b0_ref, b1_ref, b2_ref, b3_ref), term_ref, rows, share_ref, own)


def grid_kernel(rows, back_ref, send_ref, enc_ref, out_ref):
    nodes, width = out_ref.shape
    grads = dot_t(slot_rows(back_ref[...], width), whole(enc_ref, 0, rows)).astype(BF)
    out_ref[...] = dot(slots_hot(send_ref[...], nodes), grads).astype(BF)


def out_kernel(rows, me_ref, latent_ref, b0_ref, b1_ref, b2_ref, b3_ref, out_ref, sum_ref):
    total = total_of([b0_ref[...], b1_ref[...], b2_ref[...], b3_ref[...]])
    sum_ref[...] = total[: 2 * rows].astype(BF)
    own, nodes = out_ref.shape[0], latent_ref.shape[0]
    mine = lax.broadcasted_iota(jnp.int32, (1, own), 1) + me_ref[0] * own
    latent = outer(one_hot(mine, nodes), latent_ref[...])
    out_ref[...] = (latent + total[2 * rows : 2 * rows + own]).astype(BF)


def level_kernel(rows, me_ref, sum_ref, b0_ref, b1_ref, b2_ref, b3_ref, keep_ref, give_ref):
    width = sum_ref.shape[1]
    half = rows // 2
    for ref, core in ((keep_ref, me_ref[1]), (give_ref, 1 - me_ref[1])):
        for k in range(4):
            at = pl.ds(pl.multiple_of(k * rows + core * half, half), half)
            block = total_of([b0_ref[at, :], b1_ref[at, :], b2_ref[at, :], b3_ref[at, :]])
            ref[:, k * width : (k + 1) * width] = block.astype(BF)
        for k in range(2):
            at = pl.ds(pl.multiple_of(k * rows + core * half, half), half)
            ref[:, (4 + k) * width : (5 + k) * width] = sum_ref[at, :]


def mesh_kernel(rows, me_ref, node_ref, enc_ref, b0_ref, b1_ref, b2_ref, b3_ref, mesh_ref):
    own = mesh_ref.shape[0]
    total = total_of([b[4 * rows :, :] for b in (b0_ref, b1_ref, b2_ref, b3_ref)])
    back = dot_t(total.astype(BF), whole(enc_ref, 1, rows))[:own]
    node = node_ref[pl.ds(pl.multiple_of(me_ref[0] * own, 8), own), :]
    mesh_ref[...] = (node + back).astype(BF)


def split_kernel(factor, in_ref, *out_refs):
    count, thin, _ = in_ref.shape
    width = out_refs[0].shape[1]
    for r in range(count):
        for k, ref in enumerate(out_refs):
            block = in_ref[r, :, k * width : (k + 1) * width]
            ref[r * thin : (r + 1) * thin, :] = block.astype(F32) * factor


def per_device(
    grid_feat,
    mesh_feat,
    w_grid,
    w_mesh,
    w_enc2,
    w_src,
    w_dst,
    w_proc2,
    enc_send,
    enc_dst,
    hal_send,
    proc_src,
    proc_dst,
    cotangent,
):
    enc_send, enc_dst, hal_send = enc_send.T, enc_dst.T, hal_send.T
    dom = lax.axis_size(DOM)
    feat = lax.axis_size("y")
    deep = lax.axis_size("z")
    own, width = mesh_feat.shape
    nodes = own * feat
    rows = w_grid.shape[0]
    caps = enc_send.shape[0]
    pair = (dom, 2, width // 2)
    halo = hal_send.shape[0]
    edges = proc_src.shape[0]
    held = own + (-own % PAD)
    factor = 1.0 / math.sqrt(own * dom * feat)
    index = lax.axis_index("y")
    me = jnp.stack([index, lax.axis_index("c")])
    if halo != feat or held - own < 8 or edges > width:
        raise ValueError("sizes")
    bind = functools.partial

    packed = ((3 * rows + held, width), BF)
    outgoing, enc_pack, proc_pack = call(
        pack_kernel,
        [((dom, caps * width), BF), packed, packed],
        enc_send,
        grid_feat,
        proc_src.reshape(1, edges),
        proc_dst.reshape(1, edges),
        w_grid,
        w_mesh,
        w_enc2,
        w_src,
        w_dst,
        w_proc2,
        mesh_feat,
        cotangent,
        scratch=[pltpu.VMEM((held - own, width), F32)],
    )
    received = exchange(outgoing.reshape(dom, caps, width), DOM).reshape(dom, caps * width)
    enc_gath = lax.all_gather(enc_pack, "y", axis=0)
    proc_gath = lax.all_gather(proc_pack, "y", axis=0)

    slots = dom * caps
    one_sum = ((nodes, width), BF)
    partial_sum, preact, normed, scaling = call(
        bind(encode_kernel, rows, own),
        [one_sum, ((slots, width), F32), ((slots, width), F32), ((slots, 1), F32)],
        received,
        enc_dst,
        enc_gath,
    )
    latent, halo_out = call(
        bind(latent_kernel, rows, own),
        [one_sum, ((dom, width), BF)],
        *two_rounds(partial_sum),
        enc_gath,
        hal_send,
        me=me,
    )
    halo_rows = exchange(halo_out.reshape(pair), DOM).reshape(dom, width)

    lines = enc_gath[:, 3 * rows + own : 3 * rows + own + 3, :edges].astype(jnp.int32)
    source = lines[:, 0] * 16 + lines[:, 1]
    slot = source - nodes
    place = jnp.where(slot < 0, source, nodes + slot // halo)
    keeper = jnp.where(slot < 0, jnp.arange(feat, dtype=jnp.int32)[:, None], slot % halo)
    mine = keeper == index
    halo_back, at_local, at_dst, messages, hidden, mid = call(
        bind(process_kernel, rows, own),
        [
            ((dom, width), BF),
            ((nodes, width), F32),
            one_sum,
            ((nodes, width), F32),
            ((feat * edges, width), BF),
            ((feat * edges, width), BF),
        ],
        latent,
        halo_rows,
        jnp.where(mine, place, -1).reshape(1, feat * edges),
        jnp.where(mine, lines[:, 2], -1).reshape(1, feat * edges),
        proc_gath,
    )
    returned = exchange(halo_back.reshape(pair), DOM)
    first = call(
        bind(process_terms_kernel, rows, own),
        [((2 * rows + held, width), BF)] * 4,
        latent,
        at_dst,
        hidden,
        mid,
        messages,
        me=me,
        scratch=[pltpu.VMEM((width, 2 * width), BF)],
    )
    first = onward(first)
    returned, *first = lax.optimization_barrier((returned, *first))
    node_part, at_src = call(
        bind(owner_kernel, rows),
        [one_sum, one_sum],
        returned.reshape(dom, width),
        hal_send,
        at_local,
        at_dst,
        proc_gath,
        me=me,
    )

    node_grad, slot_out, *second = call(
        bind(backward_kernel, rows, own),
        [((nodes, width), F32), ((dom, caps * width), BF)] + [((4 * rows + held, width), BF)] * 4,
        *two_rounds(node_part),
        proc_gath,
        latent,
        at_src,
        enc_gath,
        received,
        enc_dst,
        preact,
        normed,
        scaling,
        me=me,
        scratch=[pltpu.VMEM((width, 4 * width), BF), pltpu.VMEM((nodes, width), F32)],
    )
    slot_back = exchange(slot_out.reshape(dom, caps, width), DOM)
    second = onward(second)
    out_rows, first_sum = call(
        bind(out_kernel, rows), [((own, width), BF), ((2 * rows, width), BF)], latent, *first, me=me
    )
    half = ((rows // 2, 6 * width), BF)
    keep, give = call(bind(level_kernel, rows), [half, half], first_sum, *second, me=me)
    given = lax.ppermute(give, "c", [(0, 1), (1, 0)])
    slot_back, given = lax.optimization_barrier((slot_back, given))
    (level,) = call(add_kernel, [half], keep, given)
    level = exchange(level.reshape(rows // 2, 2, 3 * width), ("x", "z"))
    level = level.astype(F32).sum(axis=0).astype(BF)
    level = exchange(jnp.broadcast_to(level[None], (deep, *level.shape)), "z")
    level = level.reshape(deep, 6 * width)
    near = lax.axis_size(("x", "c"))
    totals = exchange(jnp.broadcast_to(level[None], (near, *level.shape)), ("c", "x"))
    totals = call(bind(split_kernel, factor), [((rows, width), F32)] * 6, totals)
    (g_mesh,) = call(
        bind(mesh_kernel, rows), [((own, width), BF)], node_grad, enc_gath, *second, me=me
    )
    (g_grid,) = call(
        bind(grid_kernel, rows),
        [(grid_feat.shape, BF)],
        slot_back.reshape(dom, caps * width),
        enc_send,
        enc_gath,
    )
    return (out_rows, g_grid, g_mesh) + tuple(totals)


def solution(mesh):
    dom, feat = mesh.shape["dom"], mesh.shape["feat"]
    x = 4 if dom % 8 == 0 else 1
    finer = Mesh(mesh.devices.reshape(dom // (2 * x), x, 2, feat), ALL)
    return jax.shard_map(
        per_device,
        mesh=finer,
        in_specs=(
            P(ALL, None),
            P(ALL, None),
            P("y", None),
            P("y", None),
            P("y", None),
            P("y", None),
            P("y", None),
            P("y", None),
            P(ALL, None),
            P(ALL, None),
            P(DOM, None),
            P(ALL),
            P(ALL),
            P(ALL, None),
        ),
        out_specs=(
            P(ALL, None),
            P(ALL, None),
            P(ALL, None),
            P("y", None),
            P("y", None),
            P("y", None),
            P("y", None),
            P("y", None),
            P("y", None),
        ),
        check_vma=False,
    )
```

```python
import functools
import math

import jax
import jax.numpy as jnp
from jax import lax
from jax.experimental import pallas as pl
from jax.experimental.pallas import tpu as pltpu
from jax.sharding import Mesh
from jax.sharding import PartitionSpec as P

DOM = ("z", "x", "c")
ALL = ("z", "x", "c", "y")
EPS = 1e-05
BF = jnp.bfloat16
F32 = jnp.float32
PAD = 16


def call(kernel, outs, *operands, me=None, scratch=()):
    specs = [pl.BlockSpec()] * len(operands)
    if me is not None:
        operands = (me, *operands)
        specs = [pl.BlockSpec(memory_space=pltpu.SMEM), *specs]
    return pl.pallas_call(
        kernel,
        out_shape=tuple(jax.ShapeDtypeStruct(s, d) for s, d in outs),
        in_specs=specs,
        out_specs=tuple(pl.BlockSpec() for _ in outs),
        scratch_shapes=list(scratch),
        compiler_params=pltpu.CompilerParams(vmem_limit_bytes=60 * 1024 * 1024),
    )(*operands)


def onward(keep, give, tail):
    n = lax.axis_size("y")
    given = lax.ppermute(give, "c", [(0, 1), (1, 0)])
    size = (keep.shape[0] + tail.shape[0]) // n
    blocks = call(merge_kernel, [((size, keep.shape[1]), BF)] * n, keep, given, tail)
    return [blocks[0]] + [
        lax.ppermute(blocks[k], "y", [(i, (i + k) % n) for i in range(n)]) for k in range(1, n)
    ]


def exchange(array, axes):
    return lax.all_to_all(array, axes, 0, 0, tiled=True)


def dot(left, right):
    return jnp.dot(left, right, preferred_element_type=F32)


def dot_t(left, right):
    return lax.dot_general(left, right, (((1,), (1,)), ((), ())), preferred_element_type=F32)


def outer(left, right):
    return lax.dot_general(left, right, (((0,), (0,)), ((), ())), preferred_element_type=F32)


def one_hot(row, count):
    places = lax.broadcasted_iota(jnp.int32, (count, row.shape[1]), 0)
    return jnp.where(places == row, 1.0, 0.0).astype(BF)


def slots_hot(indices, count):
    return jnp.concatenate(
        [one_hot(indices[c : c + 1, :], count) for c in range(indices.shape[0])], axis=1
    )


def slot_rows(wide, width):
    return jnp.concatenate(
        [wide[:, c * width : (c + 1) * width] for c in range(wide.shape[1] // width)], axis=0
    )


def wide_rows(rows, count):
    each = rows.shape[0] // count
    return jnp.concatenate([rows[c * each : (c + 1) * each] for c in range(count)], axis=1)


def whole(ref, at, rows):
    return jnp.concatenate(
        [ref[y, at * rows : (at + 1) * rows, :] for y in range(ref.shape[0])], axis=0
    )


def sigmoid(v):
    return 1.0 / (1.0 + jnp.exp(-v))


def layer_norm(values):
    center = values - jnp.mean(values, axis=-1, keepdims=True)
    spread = jnp.mean(center * center, axis=-1, keepdims=True)
    scaling = lax.rsqrt(spread + EPS)
    return (center * scaling, scaling)


def norm_back(normed, scaling, upstream):
    inner = jnp.mean(upstream, axis=-1, keepdims=True)
    along = jnp.mean(upstream * normed, axis=-1, keepdims=True)
    return scaling * (upstream - inner - normed * along)


def pack_kernel(
    send_ref, grid_ref, src_ref, dst_ref, wg_ref, wm_ref, we_ref, ws_ref, wd_ref, wp_ref, mesh_ref, cot_ref,
    out_ref, enc_ref, proc_ref, line_ref,
):
    grid = grid_ref[...]
    width = grid.shape[1]
    for c in range(send_ref.shape[0]):
        hot = one_hot(send_ref[c : c + 1, :], grid.shape[0])
        out_ref[:, c * width : (c + 1) * width] = outer(hot, grid).astype(BF)
    edges = src_ref.shape[1]
    spare = line_ref.shape[0]
    line_ref[...] = jnp.zeros_like(line_ref)
    place = lax.broadcasted_iota(jnp.int32, (spare, edges), 0)
    source = jnp.broadcast_to(src_ref[...], (spare, edges))
    target = jnp.broadcast_to(dst_ref[...], (spare, edges))
    values = jnp.where(place == 0, source >> 4, jnp.where(place == 1, source & 15, target))
    line_ref[:, :edges] = jnp.where(place < 3, values, 0).astype(F32)
    rows = wg_ref.shape[0]
    for ref, arrays, tail in (
        (enc_ref, (wg_ref, wm_ref, we_ref), mesh_ref),
        (proc_ref, (ws_ref, wd_ref, wp_ref), cot_ref),
    ):
        for k, array in enumerate(arrays):
            ref[k * rows : (k + 1) * rows, :] = array[...]
        both = jnp.concatenate([tail[...].astype(F32), line_ref[...]], axis=0)
        ref[3 * rows :, :] = both.astype(BF)


def node_rows(gath_ref, at, own):
    return jnp.concatenate(
        [gath_ref[y, at:, :].astype(F32)[:own] for y in range(gath_ref.shape[0])], axis=0
    )


def own_row(ref, me):
    table = ref[...]
    place = lax.broadcasted_iota(jnp.int32, table.shape, 0)
    return jnp.sum(jnp.where(place == me, table, 0), axis=0, keepdims=True)


def total_of(refs):
    total = refs[0].astype(F32)
    for block in refs[1:]:
        total = total + block.astype(F32)
    return total


def encode_kernel(rows, own, recv_ref, dst_ref, gath_ref, sum_ref, pre_ref, norm_ref, scale_ref):
    width = gath_ref.shape[2]
    mesh_part = node_rows(gath_ref, 3 * rows, own).astype(BF)
    received = slot_rows(recv_ref[...], width)
    hot = slots_hot(dst_ref[...], mesh_part.shape[0])
    projected = dot(received, whole(gath_ref, 0, rows)).astype(BF)
    nodes = outer(hot, mesh_part).astype(BF)
    preact = projected.astype(F32) + dot(nodes, whole(gath_ref, 1, rows))
    pre_ref[...] = preact
    hidden = (preact * sigmoid(preact)).astype(BF)
    normed, scaling = layer_norm(dot(hidden, whole(gath_ref, 2, rows)))
    norm_ref[...] = normed
    scale_ref[...] = scaling
    partial_sum = dot(hot, normed.astype(BF)).astype(BF)
    for y in range(sum_ref.shape[0]):
        sum_ref[y] = partial_sum


def latent_kernel(rows, own, me_ref, sums_ref, gath_ref, send_ref, latent_ref, halo_ref):
    total = total_of([sums_ref[y] for y in range(sums_ref.shape[0])])
    latent = (node_rows(gath_ref, 3 * rows, own) + total).astype(BF)
    latent_ref[...] = latent
    hot = one_hot(own_row(send_ref, me_ref[0]), latent.shape[0])
    halo_ref[...] = outer(hot, latent).astype(BF)


def deal(me_ref, keep_ref, give_ref, tail_ref, term_ref, rows, node_ref, own):
    width = keep_ref.shape[1]
    terms = term_ref.shape[1] // width
    count = term_ref.shape[0] // rows
    half = rows // 2
    held = tail_ref.shape[0] // count
    me, core = me_ref[0], me_ref[1]
    for k in range(count):
        to = lax.rem(me + k, count)
        for ref, side in ((keep_ref, core), (give_ref, 1 - core)):
            at = pl.ds(pl.multiple_of(to * rows + side * half, half), half)
            for t in range(terms):
                place = (k * terms + t) * half
                ref[place : place + half, :] = term_ref[at, t * width : (t + 1) * width]
        block = node_ref[pl.ds(pl.multiple_of(to * own, 8), own), :]
        block = jnp.concatenate([block, jnp.zeros((held - own, width), F32)], axis=0)
        tail_ref[k * held : (k + 1) * held, :] = block.astype(BF)


def merge_kernel(keep_ref, given_ref, tail_ref, *out_refs):
    count = len(out_refs)
    size, held = keep_ref.shape[0] // count, tail_ref.shape[0] // count
    for k, ref in enumerate(out_refs):
        at = slice(k * size, (k + 1) * size)
        ref[:size, :] = total_of([keep_ref[at, :], given_ref[at, :]]).astype(BF)
        ref[size:, :] = tail_ref[k * held : (k + 1) * held, :]


def process_kernel(
    rows, own, latent_ref, halo_ref, source_ref, target_ref, gath_ref,
    back_ref, local_ref, dst_ref, node_ref, hidden_ref, mid_ref,
):
    latent = latent_ref[...]
    table = jnp.concatenate([latent, halo_ref[...]], axis=0)
    nodes = latent.shape[0]
    hot_src = one_hot(source_ref[...], table.shape[0])
    hot_dst = one_hot(target_ref[...], nodes)
    w_src, w_dst, w_out = [whole(gath_ref, k, rows) for k in range(3)]
    src_rows = outer(hot_src, table).astype(BF)
    dst_rows = outer(hot_dst, latent).astype(BF)
    preact = dot(src_rows, w_src) + dot(dst_rows, w_dst)
    gate = sigmoid(preact)
    hidden = (preact * gate).astype(BF)
    hidden_ref[...] = hidden
    normed, scaling = layer_norm(dot(hidden, w_out))
    node_ref[...] = dot(hot_dst, normed.astype(BF))
    upstream = outer(hot_dst, node_rows(gath_ref, 3 * rows, own).astype(BF))
    mid = norm_back(normed, scaling, upstream).astype(BF)
    mid_ref[...] = mid
    grad = (dot_t(mid, w_out) * (gate * (1.0 + preact * (1.0 - gate)))).astype(BF)
    dst_ref[...] = dot(hot_dst, grad).astype(BF)
    at_src = dot(hot_src, grad)
    local_ref[...] = at_src[:nodes]
    back_ref[...] = at_src[nodes:].astype(BF)


def process_terms_kernel(
    rows, own, me_ref, latent_ref, dst_ref, hidden_ref, mid_ref, node_ref,
    keep_ref, give_ref, tail_ref, term_ref,
):
    width = latent_ref.shape[1]
    term_ref[:, :width] = outer(latent_ref[...], dst_ref[...]).astype(BF)
    term_ref[:, width:] = outer(hidden_ref[...], mid_ref[...]).astype(BF)
    deal(me_ref, keep_ref, give_ref, tail_ref, term_ref, rows, node_ref, own)


def owner_kernel(rows, me_ref, back_ref, send_ref, local_ref, dst_ref, gath_ref, out_ref, src_ref):
    hot = one_hot(own_row(send_ref, me_ref[0]), local_ref.shape[0])
    at_src = (local_ref[...] + dot(hot, back_ref[...])).astype(BF)
    src_ref[...] = at_src
    total = dot_t(at_src, whole(gath_ref, 0, rows)) + dot_t(dst_ref[...], whole(gath_ref, 1, rows))
    total = total.astype(BF)
    for y in range(out_ref.shape[0]):
        out_ref[y] = total


def backward_kernel(
    rows, own, me_ref, sums_ref, proc_ref, latent_ref, src_ref, enc_ref, recv_ref, dst_ref,
    pre_ref, norm_ref, scale_ref,
    node_ref, slot_ref, keep_ref, give_ref, tail_ref, term_ref, share_ref,
):
    nodes, width = latent_ref.shape
    node_grad = node_rows(proc_ref, 3 * rows, own) + total_of(
        [sums_ref[y] for y in range(sums_ref.shape[0])]
    )
    node_ref[...] = node_grad
    hot = slots_hot(dst_ref[...], nodes)
    upstream = outer(hot, node_grad.astype(BF))
    mid = norm_back(norm_ref[...], scale_ref[...], upstream).astype(BF)
    preact = pre_ref[...]
    gate = sigmoid(preact)
    hidden = (preact * gate).astype(BF)
    grad = dot_t(mid, whole(enc_ref, 2, rows)) * (gate * (1.0 + preact * (1.0 - gate)))
    grad = grad.astype(BF)
    slot_ref[...] = wide_rows(grad, recv_ref.shape[1] // width)
    at_node = dot(hot, grad)
    share_ref[...] = at_node
    terms = (
        outer(slot_rows(recv_ref[...], width), grad),
        outer(node_rows(enc_ref, 3 * rows, own).astype(BF), at_node.astype(BF)),
        outer(hidden, mid),
        outer(latent_ref[...], src_ref[...]),
    )
    for k, term in enumerate(terms):
        term_ref[:, k * width : (k + 1) * width] = term.astype(BF)
    deal(me_ref, keep_ref, give_ref, tail_ref, term_ref, rows, share_ref, own)


def grid_kernel(rows, back_ref, send_ref, enc_ref, out_ref):
    nodes, width = out_ref.shape
    grads = dot_t(slot_rows(back_ref[...], width), whole(enc_ref, 0, rows)).astype(BF)
    out_ref[...] = dot(slots_hot(send_ref[...], nodes), grads).astype(BF)


def out_kernel(me_ref, latent_ref, b0_ref, b1_ref, b2_ref, b3_ref, out_ref, sum_ref):
    total = total_of([b0_ref[...], b1_ref[...], b2_ref[...], b3_ref[...]])
    size = sum_ref.shape[0]
    sum_ref[...] = total[:size].astype(BF)
    own, nodes = out_ref.shape[0], latent_ref.shape[0]
    mine = lax.broadcasted_iota(jnp.int32, (1, own), 1) + me_ref[0] * own
    latent = outer(one_hot(mine, nodes), latent_ref[...])
    out_ref[...] = (latent + total[size : size + own]).astype(BF)


def level_kernel(sum_ref, b0_ref, b1_ref, b2_ref, b3_ref, out_ref):
    width = sum_ref.shape[1]
    half = out_ref.shape[0]
    for k in range(4):
        at = slice(k * half, (k + 1) * half)
        block = total_of([b0_ref[at, :], b1_ref[at, :], b2_ref[at, :], b3_ref[at, :]])
        out_ref[:, k * width : (k + 1) * width] = block.astype(BF)
    for k in range(2):
        out_ref[:, (4 + k) * width : (5 + k) * width] = sum_ref[k * half : (k + 1) * half, :]


def mesh_kernel(rows, me_ref, node_ref, enc_ref, b0_ref, b1_ref, b2_ref, b3_ref, mesh_ref):
    own = mesh_ref.shape[0]
    total = total_of([b[2 * rows :, :] for b in (b0_ref, b1_ref, b2_ref, b3_ref)])
    back = dot_t(total.astype(BF), whole(enc_ref, 1, rows))[:own]
    node = node_ref[pl.ds(pl.multiple_of(me_ref[0] * own, 8), own), :]
    mesh_ref[...] = (node + back).astype(BF)


def sum_kernel(in_ref, out_ref):
    out_ref[...] = total_of([in_ref[k] for k in range(in_ref.shape[0])]).astype(out_ref.dtype)


def split_kernel(factor, in_ref, *out_refs):
    count, thin, _ = in_ref.shape
    width = out_refs[0].shape[1]
    for r in range(count):
        for k, ref in enumerate(out_refs):
            block = in_ref[r, :, k * width : (k + 1) * width]
            ref[r * thin : (r + 1) * thin, :] = block.astype(F32) * factor


def per_device(
    grid_feat,
    mesh_feat,
    w_grid,
    w_mesh,
    w_enc2,
    w_src,
    w_dst,
    w_proc2,
    enc_send,
    enc_dst,
    hal_send,
    proc_src,
    proc_dst,
    cotangent,
):
    enc_send, enc_dst, hal_send = enc_send.T, enc_dst.T, hal_send.T
    dom = lax.axis_size(DOM)
    feat = lax.axis_size("y")
    deep = lax.axis_size("z")
    own, width = mesh_feat.shape
    nodes = own * feat
    rows = w_grid.shape[0]
    caps = enc_send.shape[0]
    pair = (dom, 2, width // 2)
    halo = hal_send.shape[0]
    edges = proc_src.shape[0]
    held = own + (-own % PAD)
    factor = 1.0 / math.sqrt(own * dom * feat)
    index = lax.axis_index("y")
    me = jnp.stack([index, lax.axis_index("c")])
    if halo != feat or held - own < 8 or edges > width:
        raise ValueError("sizes")
    bind = functools.partial

    packed = ((3 * rows + held, width), BF)
    outgoing, enc_pack, proc_pack = call(
        pack_kernel,
        [((dom, caps * width), BF), packed, packed],
        enc_send,
        grid_feat,
        proc_src.reshape(1, edges),
        proc_dst.reshape(1, edges),
        w_grid,
        w_mesh,
        w_enc2,
        w_src,
        w_dst,
        w_proc2,
        mesh_feat,
        cotangent,
        scratch=[pltpu.VMEM((held - own, width), F32)],
    )
    received = exchange(outgoing.reshape(dom, caps, width), DOM).reshape(dom, caps * width)
    enc_gath = lax.all_gather(enc_pack, "y", axis=0)
    proc_gath = lax.all_gather(proc_pack, "y", axis=0)

    slots = dom * caps
    one_sum, all_sums = ((nodes, width), BF), ((feat, nodes, width), BF)
    partial_sum, preact, normed, scaling = call(
        bind(encode_kernel, rows, own),
        [all_sums, ((slots, width), F32), ((slots, width), F32), ((slots, 1), F32)],
        received,
        enc_dst,
        enc_gath,
    )
    latent, halo_out = call(
        bind(latent_kernel, rows, own),
        [one_sum, ((dom, width), BF)],
        exchange(partial_sum, "y"),
        enc_gath,
        hal_send,
        me=me,
    )
    halo_rows = exchange(halo_out.reshape(pair), DOM).reshape(dom, width)

    lines = enc_gath[:, 3 * rows + own : 3 * rows + own + 3, :edges].astype(jnp.int32)
    source = lines[:, 0] * 16 + lines[:, 1]
    slot = source - nodes
    place = jnp.where(slot < 0, source, nodes + slot // halo)
    keeper = jnp.where(slot < 0, jnp.arange(feat, dtype=jnp.int32)[:, None], slot % halo)
    mine = keeper == index
    halo_back, at_local, at_dst, messages, hidden, mid = call(
        bind(process_kernel, rows, own),
        [
            ((dom, width), BF),
            ((nodes, width), F32),
            one_sum,
            ((nodes, width), F32),
            ((feat * edges, width), BF),
            ((feat * edges, width), BF),
        ],
        latent,
        halo_rows,
        jnp.where(mine, place, -1).reshape(1, feat * edges),
        jnp.where(mine, lines[:, 2], -1).reshape(1, feat * edges),
        proc_gath,
    )
    returned = exchange(halo_back.reshape(pair), DOM)
    first = call(
        bind(process_terms_kernel, rows, own),
        [((4 * rows, width), BF), ((4 * rows, width), BF), ((feat * held, width), BF)],
        latent,
        at_dst,
        hidden,
        mid,
        messages,
        me=me,
        scratch=[pltpu.VMEM((width, 2 * width), BF)],
    )
    first = onward(*first)
    node_part, at_src = call(
        bind(owner_kernel, rows),
        [all_sums, one_sum],
        returned.reshape(dom, width),
        hal_send,
        at_local,
        at_dst,
        proc_gath,
        me=me,
    )

    node_in = exchange(node_part, "y")
    node_in, *first = lax.optimization_barrier((node_in, *first))

    node_grad, slot_out, *second = call(
        bind(backward_kernel, rows, own),
        [
            ((nodes, width), F32),
            ((dom, caps * width), BF),
            ((8 * rows, width), BF),
            ((8 * rows, width), BF),
            ((feat * held, width), BF),
        ],
        node_in,
        proc_gath,
        latent,
        at_src,
        enc_gath,
        received,
        enc_dst,
        preact,
        normed,
        scaling,
        me=me,
        scratch=[pltpu.VMEM((width, 4 * width), BF), pltpu.VMEM((nodes, width), F32)],
    )
    slot_back = exchange(slot_out.reshape(dom, caps, width), DOM)
    second = onward(*second)
    out_rows, first_sum = call(
        out_kernel, [((own, width), BF), ((rows, width), BF)], latent, *first, me=me
    )
    (level,) = call(level_kernel, [((rows // 2, 6 * width), BF)], first_sum, *second)
    slot_back, level = lax.optimization_barrier((slot_back, level))
    across = lax.axis_size("x")
    thin = rows // (2 * across)
    level = exchange(level.reshape(across, thin, 6 * width), "x")
    (level,) = call(sum_kernel, [((thin, 6 * width), BF)], level)
    level = exchange(level.reshape(deep, 2, 3 * width), "z")
    level = level.astype(F32).sum(axis=0).astype(BF)
    level = exchange(jnp.broadcast_to(level[None], (deep, *level.shape)), "z")
    level = level.reshape(deep, 6 * width)
    near = lax.axis_size(("x", "c"))
    totals = exchange(jnp.broadcast_to(level[None], (near, *level.shape)), ("c", "x"))
    totals = call(bind(split_kernel, factor), [((rows, width), F32)] * 6, totals)
    (g_mesh,) = call(
        bind(mesh_kernel, rows), [((own, width), BF)], node_grad, enc_gath, *second, me=me
    )
    (g_grid,) = call(
        bind(grid_kernel, rows),
        [(grid_feat.shape, BF)],
        slot_back.reshape(dom, caps * width),
        enc_send,
        enc_gath,
    )
    return (out_rows, g_grid, g_mesh) + tuple(totals)


def solution(mesh):
    dom, feat = mesh.shape["dom"], mesh.shape["feat"]
    x = 4 if dom % 8 == 0 else 1
    finer = Mesh(mesh.devices.reshape(dom // (2 * x), x, 2, feat), ALL)
    return jax.shard_map(
        per_device,
        mesh=finer,
        in_specs=(
            P(ALL, None),
            P(ALL, None),
            P("y", None),
            P("y", None),
            P("y", None),
            P("y", None),
            P("y", None),
            P("y", None),
            P(ALL, None),
            P(ALL, None),
            P(DOM, None),
            P(ALL),
            P(ALL),
            P(ALL, None),
        ),
        out_specs=(
            P(ALL, None),
            P(ALL, None),
            P(ALL, None),
            P("y", None),
            P("y", None),
            P("y", None),
            P("y", None),
            P("y", None),
            P("y", None),
        ),
        check_vma=False,
    )
```

```python
import functools
import math

import jax
import jax.numpy as jnp
from jax import lax
from jax.experimental import pallas as pl
from jax.experimental.pallas import tpu as pltpu
from jax.sharding import Mesh
from jax.sharding import PartitionSpec as P

DOM = ("z", "x", "c")
ALL = ("z", "x", "c", "y")
EPS = 1e-05
BF = jnp.bfloat16
F32 = jnp.float32
PAD = 16


def call(kernel, outs, *operands, me=None, scratch=()):
    specs = [pl.BlockSpec()] * len(operands)
    if me is not None:
        operands = (me, *operands)
        specs = [pl.BlockSpec(memory_space=pltpu.SMEM), *specs]
    return pl.pallas_call(
        kernel,
        out_shape=tuple(jax.ShapeDtypeStruct(s, d) for s, d in outs),
        in_specs=specs,
        out_specs=tuple(pl.BlockSpec() for _ in outs),
        scratch_shapes=list(scratch),
        compiler_params=pltpu.CompilerParams(vmem_limit_bytes=60 * 1024 * 1024),
    )(*operands)


def over_feat(keep, give, tail):
    n = lax.axis_size("y")
    given = lax.ppermute(give, "c", [(0, 1), (1, 0)])
    size = (keep.shape[0] + tail.shape[0], keep.shape[1])
    (both,) = call(functools.partial(merge_kernel, n), [(size, BF)], keep, given, tail)
    return lax.psum_scatter(both, "y", scatter_dimension=0, tiled=True)


def exchange(array, axes):
    return lax.all_to_all(array, axes, 0, 0, tiled=True)


def dot(left, right):
    return jnp.dot(left, right, preferred_element_type=F32)


def dot_t(left, right):
    return lax.dot_general(left, right, (((1,), (1,)), ((), ())), preferred_element_type=F32)


def outer(left, right):
    return lax.dot_general(left, right, (((0,), (0,)), ((), ())), preferred_element_type=F32)


def one_hot(row, count):
    places = lax.broadcasted_iota(jnp.int32, (count, row.shape[1]), 0)
    return jnp.where(places == row, 1.0, 0.0).astype(BF)


def slots_hot(indices, count):
    return jnp.concatenate(
        [one_hot(indices[c : c + 1, :], count) for c in range(indices.shape[0])], axis=1
    )


def slot_rows(wide, width):
    return jnp.concatenate(
        [wide[:, c * width : (c + 1) * width] for c in range(wide.shape[1] // width)], axis=0
    )


def wide_rows(rows, count):
    each = rows.shape[0] // count
    return jnp.concatenate([rows[c * each : (c + 1) * each] for c in range(count)], axis=1)


def whole(ref, at, rows):
    return jnp.concatenate(
        [ref[y, at * rows : (at + 1) * rows, :] for y in range(ref.shape[0])], axis=0
    )


def sigmoid(v):
    return 1.0 / (1.0 + jnp.exp(-v))


def layer_norm(values):
    center = values - jnp.mean(values, axis=-1, keepdims=True)
    spread = jnp.mean(center * center, axis=-1, keepdims=True)
    scaling = lax.rsqrt(spread + EPS)
    return (center * scaling, scaling)


def norm_back(normed, scaling, upstream):
    inner = jnp.mean(upstream, axis=-1, keepdims=True)
    along = jnp.mean(upstream * normed, axis=-1, keepdims=True)
    return scaling * (upstream - inner - normed * along)


def pack_kernel(
    send_ref, grid_ref, src_ref, dst_ref, wg_ref, wm_ref, we_ref, ws_ref, wd_ref, wp_ref, mesh_ref, cot_ref,
    out_ref, enc_ref, proc_ref, line_ref,
):
    grid = grid_ref[...]
    width = grid.shape[1]
    for c in range(send_ref.shape[0]):
        hot = one_hot(send_ref[c : c + 1, :], grid.shape[0])
        out_ref[:, c * width : (c + 1) * width] = outer(hot, grid).astype(BF)
    edges = src_ref.shape[1]
    spare = line_ref.shape[0]
    line_ref[...] = jnp.zeros_like(line_ref)
    place = lax.broadcasted_iota(jnp.int32, (spare, edges), 0)
    source = jnp.broadcast_to(src_ref[...], (spare, edges))
    target = jnp.broadcast_to(dst_ref[...], (spare, edges))
    values = jnp.where(place == 0, source >> 4, jnp.where(place == 1, source & 15, target))
    line_ref[:, :edges] = jnp.where(place < 3, values, 0).astype(F32)
    rows = wg_ref.shape[0]
    for ref, arrays, tail in (
        (enc_ref, (wg_ref, wm_ref, we_ref), mesh_ref),
        (proc_ref, (ws_ref, wd_ref, wp_ref), cot_ref),
    ):
        for k, array in enumerate(arrays):
            ref[k * rows : (k + 1) * rows, :] = array[...]
        both = jnp.concatenate([tail[...].astype(F32), line_ref[...]], axis=0)
        ref[3 * rows :, :] = both.astype(BF)


def node_rows(gath_ref, at, own):
    return jnp.concatenate(
        [gath_ref[y, at:, :].astype(F32)[:own] for y in range(gath_ref.shape[0])], axis=0
    )


def own_row(ref, me):
    table = ref[...]
    place = lax.broadcasted_iota(jnp.int32, table.shape, 0)
    return jnp.sum(jnp.where(place == me, table, 0), axis=0, keepdims=True)


def total_of(refs):
    total = refs[0].astype(F32)
    for block in refs[1:]:
        total = total + block.astype(F32)
    return total


def encode_kernel(rows, own, recv_ref, dst_ref, gath_ref, sum_ref, pre_ref, norm_ref, scale_ref):
    width = gath_ref.shape[2]
    mesh_part = node_rows(gath_ref, 3 * rows, own).astype(BF)
    received = slot_rows(recv_ref[...], width)
    hot = slots_hot(dst_ref[...], mesh_part.shape[0])
    projected = dot(received, whole(gath_ref, 0, rows)).astype(BF)
    nodes = outer(hot, mesh_part).astype(BF)
    preact = projected.astype(F32) + dot(nodes, whole(gath_ref, 1, rows))
    pre_ref[...] = preact
    hidden = (preact * sigmoid(preact)).astype(BF)
    normed, scaling = layer_norm(dot(hidden, whole(gath_ref, 2, rows)))
    norm_ref[...] = normed
    scale_ref[...] = scaling
    partial_sum = dot(hot, normed.astype(BF)).astype(BF)
    for y in range(sum_ref.shape[0]):
        sum_ref[y] = partial_sum


def latent_kernel(rows, own, me_ref, sums_ref, gath_ref, send_ref, latent_ref, halo_ref):
    total = total_of([sums_ref[y] for y in range(sums_ref.shape[0])])
    latent = (node_rows(gath_ref, 3 * rows, own) + total).astype(BF)
    latent_ref[...] = latent
    hot = one_hot(own_row(send_ref, me_ref[0]), latent.shape[0])
    halo_ref[...] = outer(hot, latent).astype(BF)


def deal(me_ref, keep_ref, give_ref, tail_ref, term_ref, rows, node_ref, own):
    width = keep_ref.shape[1]
    terms = term_ref.shape[1] // width
    count = term_ref.shape[0] // rows
    half = rows // 2
    held = tail_ref.shape[0] // count
    core = me_ref[1]
    for y in range(count):
        for ref, side in ((keep_ref, core), (give_ref, 1 - core)):
            at = pl.ds(pl.multiple_of(y * rows + side * half, half), half)
            for t in range(terms):
                place = (y * terms + t) * half
                ref[place : place + half, :] = term_ref[at, t * width : (t + 1) * width]
        block = node_ref[y * own : (y + 1) * own, :]
        block = jnp.concatenate([block, jnp.zeros((held - own, width), F32)], axis=0)
        tail_ref[y * held : (y + 1) * held, :] = block.astype(BF)


def merge_kernel(count, keep_ref, given_ref, tail_ref, out_ref):
    size, held = keep_ref.shape[0] // count, tail_ref.shape[0] // count
    for y in range(count):
        at, start = slice(y * size, (y + 1) * size), y * (size + held)
        out_ref[start : start + size, :] = total_of([keep_ref[at, :], given_ref[at, :]]).astype(BF)
        out_ref[start + size : start + size + held, :] = tail_ref[y * held : (y + 1) * held, :]


def process_kernel(
    rows, own, latent_ref, halo_ref, source_ref, target_ref, gath_ref,
    back_ref, local_ref, dst_ref, node_ref, hidden_ref, mid_ref,
):
    latent = latent_ref[...]
    table = jnp.concatenate([latent, halo_ref[...]], axis=0)
    nodes = latent.shape[0]
    hot_src = one_hot(source_ref[...], table.shape[0])
    hot_dst = one_hot(target_ref[...], nodes)
    w_src, w_dst, w_out = [whole(gath_ref, k, rows) for k in range(3)]
    src_rows = outer(hot_src, table).astype(BF)
    dst_rows = outer(hot_dst, latent).astype(BF)
    preact = dot(src_rows, w_src) + dot(dst_rows, w_dst)
    gate = sigmoid(preact)
    hidden = (preact * gate).astype(BF)
    hidden_ref[...] = hidden
    normed, scaling = layer_norm(dot(hidden, w_out))
    node_ref[...] = dot(hot_dst, normed.astype(BF))
    upstream = outer(hot_dst, node_rows(gath_ref, 3 * rows, own).astype(BF))
    mid = norm_back(normed, scaling, upstream).astype(BF)
    mid_ref[...] = mid
    grad = (dot_t(mid, w_out) * (gate * (1.0 + preact * (1.0 - gate)))).astype(BF)
    dst_ref[...] = dot(hot_dst, grad).astype(BF)
    at_src = dot(hot_src, grad)
    local_ref[...] = at_src[:nodes]
    back_ref[...] = at_src[nodes:].astype(BF)


def process_terms_kernel(
    rows, own, me_ref, latent_ref, dst_ref, hidden_ref, mid_ref, node_ref,
    keep_ref, give_ref, tail_ref, term_ref,
):
    width = latent_ref.shape[1]
    term_ref[:, :width] = outer(latent_ref[...], dst_ref[...]).astype(BF)
    term_ref[:, width:] = outer(hidden_ref[...], mid_ref[...]).astype(BF)
    deal(me_ref, keep_ref, give_ref, tail_ref, term_ref, rows, node_ref, own)


def owner_kernel(rows, me_ref, back_ref, send_ref, local_ref, dst_ref, gath_ref, out_ref, src_ref):
    hot = one_hot(own_row(send_ref, me_ref[0]), local_ref.shape[0])
    at_src = (local_ref[...] + dot(hot, back_ref[...])).astype(BF)
    src_ref[...] = at_src
    total = dot_t(at_src, whole(gath_ref, 0, rows)) + dot_t(dst_ref[...], whole(gath_ref, 1, rows))
    total = total.astype(BF)
    for y in range(out_ref.shape[0]):
        out_ref[y] = total


def backward_kernel(
    rows, own, me_ref, sums_ref, proc_ref, latent_ref, src_ref, enc_ref, recv_ref, dst_ref,
    pre_ref, norm_ref, scale_ref,
    node_ref, slot_ref, keep_ref, give_ref, tail_ref, term_ref, share_ref,
):
    nodes, width = latent_ref.shape
    node_grad = node_rows(proc_ref, 3 * rows, own) + total_of(
        [sums_ref[y] for y in range(sums_ref.shape[0])]
    )
    node_ref[...] = node_grad
    hot = slots_hot(dst_ref[...], nodes)
    upstream = outer(hot, node_grad.astype(BF))
    mid = norm_back(norm_ref[...], scale_ref[...], upstream).astype(BF)
    preact = pre_ref[...]
    gate = sigmoid(preact)
    hidden = (preact * gate).astype(BF)
    grad = dot_t(mid, whole(enc_ref, 2, rows)) * (gate * (1.0 + preact * (1.0 - gate)))
    grad = grad.astype(BF)
    slot_ref[...] = wide_rows(grad, recv_ref.shape[1] // width)
    at_node = dot(hot, grad)
    share_ref[...] = at_node
    terms = (
        outer(slot_rows(recv_ref[...], width), grad),
        outer(node_rows(enc_ref, 3 * rows, own).astype(BF), at_node.astype(BF)),
        outer(hidden, mid),
        outer(latent_ref[...], src_ref[...]),
    )
    for k, term in enumerate(terms):
        term_ref[:, k * width : (k + 1) * width] = term.astype(BF)
    deal(me_ref, keep_ref, give_ref, tail_ref, term_ref, rows, share_ref, own)


def grid_kernel(rows, back_ref, send_ref, enc_ref, out_ref):
    nodes, width = out_ref.shape
    grads = dot_t(slot_rows(back_ref[...], width), whole(enc_ref, 0, rows)).astype(BF)
    out_ref[...] = dot(slots_hot(send_ref[...], nodes), grads).astype(BF)


def out_kernel(me_ref, latent_ref, first_ref, out_ref):
    own, nodes = out_ref.shape[0], latent_ref.shape[0]
    held = own + (-own % PAD)
    mine = lax.broadcasted_iota(jnp.int32, (1, own), 1) + me_ref[0] * own
    latent = outer(one_hot(mine, nodes), latent_ref[...])
    out_ref[...] = (latent + first_ref[first_ref.shape[0] - held :, :].astype(F32)[:own]).astype(BF)


def level_kernel(first_ref, second_ref, out_ref):
    width = first_ref.shape[1]
    half = out_ref.shape[0]
    for k in range(6):
        ref, t = (second_ref, k) if k < 4 else (first_ref, k - 4)
        out_ref[:, k * width : (k + 1) * width] = ref[t * half : (t + 1) * half, :]


def mesh_kernel(rows, me_ref, node_ref, enc_ref, second_ref, mesh_ref):
    own = mesh_ref.shape[0]
    held = own + (-own % PAD)
    total = second_ref[second_ref.shape[0] - held :, :]
    back = dot_t(total, whole(enc_ref, 1, rows))[:own]
    node = node_ref[pl.ds(pl.multiple_of(me_ref[0] * own, 8), own), :]
    mesh_ref[...] = (node + back).astype(BF)


def sum_kernel(in_ref, out_ref):
    out_ref[...] = total_of([in_ref[k] for k in range(in_ref.shape[0])]).astype(out_ref.dtype)


def split_kernel(factor, in_ref, *out_refs):
    count, thin, _ = in_ref.shape
    width = out_refs[0].shape[1]
    for r in range(count):
        for k, ref in enumerate(out_refs):
            block = in_ref[r, :, k * width : (k + 1) * width]
            ref[r * thin : (r + 1) * thin, :] = block.astype(F32) * factor


def per_device(
    grid_feat,
    mesh_feat,
    w_grid,
    w_mesh,
    w_enc2,
    w_src,
    w_dst,
    w_proc2,
    enc_send,
    enc_dst,
    hal_send,
    proc_src,
    proc_dst,
    cotangent,
):
    enc_send, enc_dst, hal_send = enc_send.T, enc_dst.T, hal_send.T
    dom = lax.axis_size(DOM)
    feat = lax.axis_size("y")
    deep = lax.axis_size("z")
    own, width = mesh_feat.shape
    nodes = own * feat
    rows = w_grid.shape[0]
    caps = enc_send.shape[0]
    pair = (dom, 2, width // 2)
    halo = hal_send.shape[0]
    edges = proc_src.shape[0]
    held = own + (-own % PAD)
    factor = 1.0 / math.sqrt(own * dom * feat)
    index = lax.axis_index("y")
    me = jnp.stack([index, lax.axis_index("c")])
    if halo != feat or held - own < 8 or edges > width:
        raise ValueError("sizes")
    bind = functools.partial

    packed = ((3 * rows + held, width), BF)
    outgoing, enc_pack, proc_pack = call(
        pack_kernel,
        [((dom, caps * width), BF), packed, packed],
        enc_send,
        grid_feat,
        proc_src.reshape(1, edges),
        proc_dst.reshape(1, edges),
        w_grid,
        w_mesh,
        w_enc2,
        w_src,
        w_dst,
        w_proc2,
        mesh_feat,
        cotangent,
        scratch=[pltpu.VMEM((held - own, width), F32)],
    )
    received = exchange(outgoing.reshape(dom, caps, width), DOM).reshape(dom, caps * width)
    enc_gath = lax.all_gather(enc_pack, "y", axis=0)
    proc_gath = lax.all_gather(proc_pack, "y", axis=0)

    slots = dom * caps
    one_sum, all_sums = ((nodes, width), BF), ((feat, nodes, width), BF)
    partial_sum, preact, normed, scaling = call(
        bind(encode_kernel, rows, own),
        [all_sums, ((slots, width), F32), ((slots, width), F32), ((slots, 1), F32)],
        received,
        enc_dst,
        enc_gath,
    )
    latent, halo_out = call(
        bind(latent_kernel, rows, own),
        [one_sum, ((dom, width), BF)],
        exchange(partial_sum, "y"),
        enc_gath,
        hal_send,
        me=me,
    )
    halo_rows = exchange(halo_out.reshape(pair), DOM).reshape(dom, width)

    lines = enc_gath[:, 3 * rows + own : 3 * rows + own + 3, :edges].astype(jnp.int32)
    source = lines[:, 0] * 16 + lines[:, 1]
    slot = source - nodes
    place = jnp.where(slot < 0, source, nodes + slot // halo)
    keeper = jnp.where(slot < 0, jnp.arange(feat, dtype=jnp.int32)[:, None], slot % halo)
    mine = keeper == index
    halo_back, at_local, at_dst, messages, hidden, mid = call(
        bind(process_kernel, rows, own),
        [
            ((dom, width), BF),
            ((nodes, width), F32),
            one_sum,
            ((nodes, width), F32),
            ((feat * edges, width), BF),
            ((feat * edges, width), BF),
        ],
        latent,
        halo_rows,
        jnp.where(mine, place, -1).reshape(1, feat * edges),
        jnp.where(mine, lines[:, 2], -1).reshape(1, feat * edges),
        proc_gath,
    )
    returned = exchange(halo_back.reshape(pair), DOM)
    first = call(
        bind(process_terms_kernel, rows, own),
        [((4 * rows, width), BF), ((4 * rows, width), BF), ((feat * held, width), BF)],
        latent,
        at_dst,
        hidden,
        mid,
        messages,
        me=me,
        scratch=[pltpu.VMEM((width, 2 * width), BF)],
    )
    first = over_feat(*first)
    node_part, at_src = call(
        bind(owner_kernel, rows),
        [all_sums, one_sum],
        returned.reshape(dom, width),
        hal_send,
        at_local,
        at_dst,
        proc_gath,
        me=me,
    )

    node_in = exchange(node_part, "y")

    node_grad, slot_out, *second = call(
        bind(backward_kernel, rows, own),
        [
            ((nodes, width), F32),
            ((dom, caps * width), BF),
            ((8 * rows, width), BF),
            ((8 * rows, width), BF),
            ((feat * held, width), BF),
        ],
        node_in,
        proc_gath,
        latent,
        at_src,
        enc_gath,
        received,
        enc_dst,
        preact,
        normed,
        scaling,
        me=me,
        scratch=[pltpu.VMEM((width, 4 * width), BF), pltpu.VMEM((nodes, width), F32)],
    )
    slot_back = exchange(slot_out.reshape(dom, caps, width), DOM)
    second = over_feat(*second)
    (level,) = call(level_kernel, [((rows // 2, 6 * width), BF)], first, second)
    slot_back, level = lax.optimization_barrier((slot_back, level))
    across = lax.axis_size("x")
    thin = rows // (2 * across)
    level = exchange(level.reshape(across, thin, 6 * width), "x")
    (level,) = call(sum_kernel, [((thin, 6 * width), BF)], level)
    level = exchange(level.reshape(deep, 2, 3 * width), "z")
    level = level.astype(F32).sum(axis=0).astype(BF)
    level = exchange(jnp.broadcast_to(level[None], (deep, *level.shape)), "z")
    level = level.reshape(deep, 6 * width)
    near = lax.axis_size(("x", "c"))
    totals = exchange(jnp.broadcast_to(level[None], (near, *level.shape)), ("c", "x"))
    totals = call(bind(split_kernel, factor), [((rows, width), F32)] * 6, totals)
    (out_rows,) = call(out_kernel, [((own, width), BF)], latent, first, me=me)
    (g_mesh,) = call(
        bind(mesh_kernel, rows), [((own, width), BF)], node_grad, enc_gath, second, me=me
    )
    (g_grid,) = call(
        bind(grid_kernel, rows),
        [(grid_feat.shape, BF)],
        slot_back.reshape(dom, caps * width),
        enc_send,
        enc_gath,
    )
    return (out_rows, g_grid, g_mesh) + tuple(totals)


def solution(mesh):
    dom, feat = mesh.shape["dom"], mesh.shape["feat"]
    x = 4 if dom % 8 == 0 else 1
    finer = Mesh(mesh.devices.reshape(dom // (2 * x), x, 2, feat), ALL)
    return jax.shard_map(
        per_device,
        mesh=finer,
        in_specs=(
            P(ALL, None),
            P(ALL, None),
            P("y", None),
            P("y", None),
            P("y", None),
            P("y", None),
            P("y", None),
            P("y", None),
            P(ALL, None),
            P(ALL, None),
            P(DOM, None),
            P(ALL),
            P(ALL),
            P(ALL, None),
        ),
        out_specs=(
            P(ALL, None),
            P(ALL, None),
            P(ALL, None),
            P("y", None),
            P("y", None),
            P("y", None),
            P("y", None),
            P("y", None),
            P("y", None),
        ),
        check_vma=False,
    )
```

```python
import functools
import math

import jax
import jax.numpy as jnp
from jax import lax
from jax.experimental import pallas as pl
from jax.experimental.pallas import tpu as pltpu
from jax.sharding import Mesh
from jax.sharding import PartitionSpec as P

DOM = ("z", "x", "c")
ALL = ("z", "x", "c", "y")
EPS = 1e-05
BF = jnp.bfloat16
F32 = jnp.float32
PAD = 16


def call(kernel, outs, *operands, me=None, scratch=()):
    specs = [pl.BlockSpec()] * len(operands)
    if me is not None:
        operands = (me, *operands)
        specs = [pl.BlockSpec(memory_space=pltpu.SMEM), *specs]
    return pl.pallas_call(
        kernel,
        out_shape=tuple(jax.ShapeDtypeStruct(s, d) for s, d in outs),
        in_specs=specs,
        out_specs=tuple(pl.BlockSpec() for _ in outs),
        scratch_shapes=list(scratch),
        compiler_params=pltpu.CompilerParams(vmem_limit_bytes=60 * 1024 * 1024),
    )(*operands)


def over_cores(keep, give, tail):
    given = lax.ppermute(give, "c", [(0, 1), (1, 0)])
    size = (keep.shape[0] + tail.shape[0], keep.shape[1])
    kernel = functools.partial(merge_kernel, lax.axis_size("y"))
    return call(kernel, [(size, BF)], keep, given, tail)[0]


def onward(array, me):
    n = lax.axis_size("y")
    size = (array.shape[0] // n, array.shape[1])
    blocks = call(deal_out_kernel, [(size, BF)] * n, array, me=me)
    return [blocks[0]] + [
        lax.ppermute(blocks[k], "y", [(i, (i + k) % n) for i in range(n)]) for k in range(1, n)
    ]


def exchange(array, axes):
    return lax.all_to_all(array, axes, 0, 0, tiled=True)


def dot(left, right):
    return jnp.dot(left, right, preferred_element_type=F32)


def dot_t(left, right):
    return lax.dot_general(left, right, (((1,), (1,)), ((), ())), preferred_element_type=F32)


def outer(left, right):
    return lax.dot_general(left, right, (((0,), (0,)), ((), ())), preferred_element_type=F32)


def one_hot(row, count):
    places = lax.broadcasted_iota(jnp.int32, (count, row.shape[1]), 0)
    return jnp.where(places == row, 1.0, 0.0).astype(BF)


def slots_hot(indices, count):
    return jnp.concatenate(
        [one_hot(indices[c : c + 1, :], count) for c in range(indices.shape[0])], axis=1
    )


def slot_rows(wide, width):
    return jnp.concatenate(
        [wide[:, c * width : (c + 1) * width] for c in range(wide.shape[1] // width)], axis=0
    )


def wide_rows(rows, count):
    each = rows.shape[0] // count
    return jnp.concatenate([rows[c * each : (c + 1) * each] for c in range(count)], axis=1)


def whole(ref, at, rows):
    return jnp.concatenate(
        [ref[y, at * rows : (at + 1) * rows, :] for y in range(ref.shape[0])], axis=0
    )


def sigmoid(v):
    return 1.0 / (1.0 + jnp.exp(-v))


def layer_norm(values):
    center = values - jnp.mean(values, axis=-1, keepdims=True)
    spread = jnp.mean(center * center, axis=-1, keepdims=True)
    scaling = lax.rsqrt(spread + EPS)
    return (center * scaling, scaling)


def norm_back(normed, scaling, upstream):
    inner = jnp.mean(upstream, axis=-1, keepdims=True)
    along = jnp.mean(upstream * normed, axis=-1, keepdims=True)
    return scaling * (upstream - inner - normed * along)


def pack_kernel(
    send_ref, grid_ref, src_ref, dst_ref, wg_ref, wm_ref, ws_ref, wd_ref, wp_ref, mesh_ref, cot_ref,
    out_ref, enc_ref, proc_ref, line_ref,
):
    grid = grid_ref[...]
    width = grid.shape[1]
    for c in range(send_ref.shape[0]):
        hot = one_hot(send_ref[c : c + 1, :], grid.shape[0])
        out_ref[:, c * width : (c + 1) * width] = outer(hot, grid).astype(BF)
    edges = src_ref.shape[1]
    spare = line_ref.shape[0]
    line_ref[...] = jnp.zeros_like(line_ref)
    place = lax.broadcasted_iota(jnp.int32, (spare, edges), 0)
    source = jnp.broadcast_to(src_ref[...], (spare, edges))
    target = jnp.broadcast_to(dst_ref[...], (spare, edges))
    values = jnp.where(place == 0, source >> 4, jnp.where(place == 1, source & 15, target))
    line_ref[:, :edges] = jnp.where(place < 3, values, 0).astype(F32)
    rows = wg_ref.shape[0]
    for ref, arrays, tail in (
        (enc_ref, (wg_ref, wm_ref), mesh_ref),
        (proc_ref, (ws_ref, wd_ref, wp_ref), cot_ref),
    ):
        for k, array in enumerate(arrays):
            ref[k * rows : (k + 1) * rows, :] = array[...]
        both = jnp.concatenate([tail[...].astype(F32), line_ref[...]], axis=0)
        ref[len(arrays) * rows :, :] = both.astype(BF)


def node_rows(gath_ref, at, own):
    return jnp.concatenate(
        [gath_ref[y, at:, :].astype(F32)[:own] for y in range(gath_ref.shape[0])], axis=0
    )


def own_row(ref, me):
    table = ref[...]
    place = lax.broadcasted_iota(jnp.int32, table.shape, 0)
    return jnp.sum(jnp.where(place == me, table, 0), axis=0, keepdims=True)


def total_of(refs):
    total = refs[0].astype(F32)
    for block in refs[1:]:
        total = total + block.astype(F32)
    return total


def encode_kernel(rows, own, recv_ref, dst_ref, gath_ref, w_ref, sum_ref, pre_ref, norm_ref, scale_ref):
    width = gath_ref.shape[2]
    mesh_part = node_rows(gath_ref, 2 * rows, own).astype(BF)
    received = slot_rows(recv_ref[...], width)
    hot = slots_hot(dst_ref[...], mesh_part.shape[0])
    projected = dot(received, whole(gath_ref, 0, rows)).astype(BF)
    nodes = outer(hot, mesh_part).astype(BF)
    preact = projected.astype(F32) + dot(nodes, whole(gath_ref, 1, rows))
    pre_ref[...] = preact
    hidden = (preact * sigmoid(preact)).astype(BF)
    normed, scaling = layer_norm(dot(hidden, w_ref[...]))
    norm_ref[...] = normed
    scale_ref[...] = scaling
    partial_sum = dot(hot, normed.astype(BF)).astype(BF)
    for y in range(sum_ref.shape[0]):
        sum_ref[y] = partial_sum


def latent_kernel(rows, own, me_ref, sums_ref, gath_ref, send_ref, latent_ref, halo_ref):
    total = total_of([sums_ref[y] for y in range(sums_ref.shape[0])])
    latent = (node_rows(gath_ref, 2 * rows, own) + total).astype(BF)
    latent_ref[...] = latent
    hot = one_hot(own_row(send_ref, me_ref[0]), latent.shape[0])
    halo_ref[...] = outer(hot, latent).astype(BF)


def deal(me_ref, keep_ref, give_ref, tail_ref, term_ref, rows, node_ref, own):
    width = keep_ref.shape[1]
    terms = term_ref.shape[1] // width
    count = term_ref.shape[0] // rows
    half = rows // 2
    held = tail_ref.shape[0] // count
    core = me_ref[1]
    for y in range(count):
        for ref, side in ((keep_ref, core), (give_ref, 1 - core)):
            at = pl.ds(pl.multiple_of(y * rows + side * half, half), half)
            for t in range(terms):
                place = (y * terms + t) * half
                ref[place : place + half, :] = term_ref[at, t * width : (t + 1) * width]
        block = node_ref[y * own : (y + 1) * own, :]
        block = jnp.concatenate([block, jnp.zeros((held - own, width), F32)], axis=0)
        tail_ref[y * held : (y + 1) * held, :] = block.astype(BF)


def merge_kernel(count, keep_ref, given_ref, tail_ref, out_ref):
    size, held = keep_ref.shape[0] // count, tail_ref.shape[0] // count
    for y in range(count):
        at, start = slice(y * size, (y + 1) * size), y * (size + held)
        out_ref[start : start + size, :] = total_of([keep_ref[at, :], given_ref[at, :]]).astype(BF)
        out_ref[start + size : start + size + held, :] = tail_ref[y * held : (y + 1) * held, :]


def process_kernel(
    rows, own, latent_ref, halo_ref, source_ref, target_ref, gath_ref,
    back_ref, local_ref, dst_ref, node_ref, hidden_ref, mid_ref,
):
    latent = latent_ref[...]
    table = jnp.concatenate([latent, halo_ref[...]], axis=0)
    nodes = latent.shape[0]
    hot_src = one_hot(source_ref[...], table.shape[0])
    hot_dst = one_hot(target_ref[...], nodes)
    w_src, w_dst, w_out = [whole(gath_ref, k, rows) for k in range(3)]
    src_rows = outer(hot_src, table).astype(BF)
    dst_rows = outer(hot_dst, latent).astype(BF)
    preact = dot(src_rows, w_src) + dot(dst_rows, w_dst)
    gate = sigmoid(preact)
    hidden = (preact * gate).astype(BF)
    hidden_ref[...] = hidden
    normed, scaling = layer_norm(dot(hidden, w_out))
    node_ref[...] = dot(hot_dst, normed.astype(BF))
    upstream = outer(hot_dst, node_rows(gath_ref, 3 * rows, own).astype(BF))
    mid = norm_back(normed, scaling, upstream).astype(BF)
    mid_ref[...] = mid
    grad = (dot_t(mid, w_out) * (gate * (1.0 + preact * (1.0 - gate)))).astype(BF)
    dst_ref[...] = dot(hot_dst, grad).astype(BF)
    at_src = dot(hot_src, grad)
    local_ref[...] = at_src[:nodes]
    back_ref[...] = at_src[nodes:].astype(BF)


def process_terms_kernel(
    rows, own, me_ref, latent_ref, dst_ref, hidden_ref, mid_ref, node_ref,
    keep_ref, give_ref, tail_ref, term_ref,
):
    width = latent_ref.shape[1]
    term_ref[:, :width] = outer(latent_ref[...], dst_ref[...]).astype(BF)
    term_ref[:, width:] = outer(hidden_ref[...], mid_ref[...]).astype(BF)
    deal(me_ref, keep_ref, give_ref, tail_ref, term_ref, rows, node_ref, own)


def owner_kernel(rows, me_ref, back_ref, send_ref, local_ref, dst_ref, gath_ref, out_ref, src_ref):
    hot = one_hot(own_row(send_ref, me_ref[0]), local_ref.shape[0])
    at_src = (local_ref[...] + dot(hot, back_ref[...])).astype(BF)
    src_ref[...] = at_src
    total = dot_t(at_src, whole(gath_ref, 0, rows)) + dot_t(dst_ref[...], whole(gath_ref, 1, rows))
    total = total.astype(BF)
    for y in range(out_ref.shape[0]):
        out_ref[y] = total


def backward_kernel(
    rows, own, me_ref, sums_ref, proc_ref, latent_ref, src_ref, enc_ref, w_ref, recv_ref, dst_ref,
    pre_ref, norm_ref, scale_ref,
    node_ref, slot_ref, keep_ref, give_ref, tail_ref, term_ref, share_ref,
):
    nodes, width = latent_ref.shape
    node_grad = node_rows(proc_ref, 3 * rows, own) + total_of(
        [sums_ref[y] for y in range(sums_ref.shape[0])]
    )
    node_ref[...] = node_grad
    hot = slots_hot(dst_ref[...], nodes)
    upstream = outer(hot, node_grad.astype(BF))
    mid = norm_back(norm_ref[...], scale_ref[...], upstream).astype(BF)
    preact = pre_ref[...]
    gate = sigmoid(preact)
    hidden = (preact * gate).astype(BF)
    grad = dot_t(mid, w_ref[...]) * (gate * (1.0 + preact * (1.0 - gate)))
    grad = grad.astype(BF)
    slot_ref[...] = wide_rows(grad, recv_ref.shape[1] // width)
    at_node = dot(hot, grad)
    share_ref[...] = at_node
    terms = (
        outer(slot_rows(recv_ref[...], width), grad),
        outer(node_rows(enc_ref, 2 * rows, own).astype(BF), at_node.astype(BF)),
        outer(hidden, mid),
        outer(latent_ref[...], src_ref[...]),
    )
    for k, term in enumerate(terms):
        term_ref[:, k * width : (k + 1) * width] = term.astype(BF)
    deal(me_ref, keep_ref, give_ref, tail_ref, term_ref, rows, share_ref, own)


def grid_kernel(rows, back_ref, send_ref, enc_ref, out_ref):
    nodes, width = out_ref.shape
    grads = dot_t(slot_rows(back_ref[...], width), whole(enc_ref, 0, rows)).astype(BF)
    out_ref[...] = dot(slots_hot(send_ref[...], nodes), grads).astype(BF)


def out_kernel(me_ref, latent_ref, b0_ref, b1_ref, b2_ref, b3_ref, out_ref):
    own, nodes = out_ref.shape[0], latent_ref.shape[0]
    start = b0_ref.shape[0] - own - (-own % PAD)
    total = total_of([b[start:, :] for b in (b0_ref, b1_ref, b2_ref, b3_ref)])
    mine = lax.broadcasted_iota(jnp.int32, (1, own), 1) + me_ref[0] * own
    latent = outer(one_hot(mine, nodes), latent_ref[...])
    out_ref[...] = (latent + total[:own]).astype(BF)


def level_kernel(second_ref, b0_ref, b1_ref, b2_ref, b3_ref, out_ref):
    width = second_ref.shape[1]
    half = out_ref.shape[0]
    for k in range(4):
        out_ref[:, k * width : (k + 1) * width] = second_ref[k * half : (k + 1) * half, :]
    for k in range(2):
        at = slice(k * half, (k + 1) * half)
        block = total_of([b[at, :] for b in (b0_ref, b1_ref, b2_ref, b3_ref)])
        out_ref[:, (4 + k) * width : (5 + k) * width] = block.astype(BF)


def deal_out_kernel(me_ref, in_ref, *out_refs):
    count = len(out_refs)
    size = out_refs[0].shape[0]
    for k, ref in enumerate(out_refs):
        to = lax.rem(me_ref[0] + k, count)
        ref[...] = in_ref[pl.ds(pl.multiple_of(to * size, PAD), size), :]


def mesh_kernel(rows, me_ref, node_ref, enc_ref, second_ref, mesh_ref):
    own = mesh_ref.shape[0]
    held = own + (-own % PAD)
    total = second_ref[second_ref.shape[0] - held :, :]
    back = dot_t(total, whole(enc_ref, 1, rows))[:own]
    node = node_ref[pl.ds(pl.multiple_of(me_ref[0] * own, 8), own), :]
    mesh_ref[...] = (node + back).astype(BF)


def sum_kernel(in_ref, out_ref):
    out_ref[...] = total_of([in_ref[k] for k in range(in_ref.shape[0])]).astype(out_ref.dtype)


def split_kernel(factor, in_ref, *out_refs):
    count, thin, _ = in_ref.shape
    width = out_refs[0].shape[1]
    for r in range(count):
        for k, ref in enumerate(out_refs):
            block = in_ref[r, :, k * width : (k + 1) * width]
            ref[r * thin : (r + 1) * thin, :] = block.astype(F32) * factor


def per_device(
    grid_feat,
    mesh_feat,
    w_grid,
    w_mesh,
    w_enc2,
    w_src,
    w_dst,
    w_proc2,
    enc_send,
    enc_dst,
    hal_send,
    proc_src,
    proc_dst,
    cotangent,
):
    enc_send, enc_dst, hal_send = enc_send.T, enc_dst.T, hal_send.T
    dom = lax.axis_size(DOM)
    feat = lax.axis_size("y")
    deep = lax.axis_size("z")
    own, width = mesh_feat.shape
    nodes = own * feat
    rows = w_grid.shape[0]
    caps = enc_send.shape[0]
    pair = (dom, 2, width // 2)
    halo = hal_send.shape[0]
    edges = proc_src.shape[0]
    held = own + (-own % PAD)
    factor = 1.0 / math.sqrt(own * dom * feat)
    index = lax.axis_index("y")
    me = jnp.stack([index, lax.axis_index("c")])
    if halo != feat or held - own < 8 or edges > width:
        raise ValueError("sizes")
    bind = functools.partial

    half = rows // 2
    outgoing, enc_pack, proc_pack = call(
        pack_kernel,
        [
            ((dom, caps * width), BF),
            ((2 * rows + held, width), BF),
            ((3 * rows + held, width), BF),
        ],
        enc_send,
        grid_feat,
        proc_src.reshape(1, edges),
        proc_dst.reshape(1, edges),
        w_grid,
        w_mesh,
        w_src,
        w_dst,
        w_proc2,
        mesh_feat,
        cotangent,
        scratch=[pltpu.VMEM((held - own, width), F32)],
    )
    received = exchange(outgoing.reshape(dom, caps, width), DOM).reshape(dom, caps * width)
    enc_gath = lax.all_gather(enc_pack, "y", axis=0)
    full_enc2 = lax.all_gather(w_enc2, "y", axis=0, tiled=True)
    proc_gath = lax.all_gather(proc_pack, "y", axis=0)

    slots = dom * caps
    one_sum, all_sums = ((nodes, width), BF), ((feat, nodes, width), BF)
    partial_sum, preact, normed, scaling = call(
        bind(encode_kernel, rows, own),
        [
            all_sums,
            ((slots, width), F32),
            ((slots, width), F32),
            ((slots, 1), F32),
        ],
        received,
        enc_dst,
        enc_gath,
        full_enc2,
    )
    latent, halo_out = call(
        bind(latent_kernel, rows, own),
        [one_sum, ((dom, width), BF)],
        exchange(partial_sum, "y"),
        enc_gath,
        hal_send,
        me=me,
    )
    halo_rows = exchange(halo_out.reshape(pair), DOM).reshape(dom, width)

    lines = enc_gath[:, 2 * rows + own : 2 * rows + own + 3, :edges].astype(jnp.int32)
    source = lines[:, 0] * 16 + lines[:, 1]
    slot = source - nodes
    place = jnp.where(slot < 0, source, nodes + slot // halo)
    keeper = jnp.where(slot < 0, jnp.arange(feat, dtype=jnp.int32)[:, None], slot % halo)
    mine = keeper == index
    halo_back, at_local, at_dst, messages, hidden, mid = call(
        bind(process_kernel, rows, own),
        [
            ((dom, width), BF),
            ((nodes, width), F32),
            one_sum,
            ((nodes, width), F32),
            ((feat * edges, width), BF),
            ((feat * edges, width), BF),
        ],
        latent,
        halo_rows,
        jnp.where(mine, place, -1).reshape(1, feat * edges),
        jnp.where(mine, lines[:, 2], -1).reshape(1, feat * edges),
        proc_gath,
    )
    returned = exchange(halo_back.reshape(pair), DOM)
    first = call(
        bind(process_terms_kernel, rows, own),
        [((4 * rows, width), BF), ((4 * rows, width), BF), ((feat * held, width), BF)],
        latent,
        at_dst,
        hidden,
        mid,
        messages,
        me=me,
        scratch=[pltpu.VMEM((width, 2 * width), BF)],
    )
    first = over_cores(*first)
    node_part, at_src = call(
        bind(owner_kernel, rows),
        [all_sums, one_sum],
        returned.reshape(dom, width),
        hal_send,
        at_local,
        at_dst,
        proc_gath,
        me=me,
    )

    node_in, first = lax.optimization_barrier((exchange(node_part, "y"), first))

    node_grad, slot_out, *second = call(
        bind(backward_kernel, rows, own),
        [
            ((nodes, width), F32),
            ((dom, caps * width), BF),
            ((8 * rows, width), BF),
            ((8 * rows, width), BF),
            ((feat * held, width), BF),
        ],
        node_in,
        proc_gath,
        latent,
        at_src,
        enc_gath,
        full_enc2,
        received,
        enc_dst,
        preact,
        normed,
        scaling,
        me=me,
        scratch=[pltpu.VMEM((width, 4 * width), BF), pltpu.VMEM((nodes, width), F32)],
    )
    slot_back = exchange(slot_out.reshape(dom, caps, width), DOM)
    second = over_cores(*second)
    first, second = lax.optimization_barrier((first, second))
    first = onward(first, me)
    second = lax.psum_scatter(second, "y", scatter_dimension=0, tiled=True)
    (level,) = call(level_kernel, [((half, 6 * width), BF)], second, *first)
    slot_back, level = lax.optimization_barrier((slot_back, level))
    across = lax.axis_size("x")
    thin = rows // (2 * across)
    level = exchange(level.reshape(across, thin, 6 * width), "x")
    (level,) = call(sum_kernel, [((thin, 6 * width), BF)], level)
    level = exchange(level.reshape(deep, 2, 3 * width), "z")
    level = level.astype(F32).sum(axis=0).astype(BF)
    level = exchange(jnp.broadcast_to(level[None], (deep, *level.shape)), "z")
    level = level.reshape(deep, 6 * width)
    near = lax.axis_size(("x", "c"))
    totals = exchange(jnp.broadcast_to(level[None], (near, *level.shape)), ("c", "x"))
    totals = call(bind(split_kernel, factor), [((rows, width), F32)] * 6, totals)
    (out_rows,) = call(out_kernel, [((own, width), BF)], latent, *first, me=me)
    (g_mesh,) = call(
        bind(mesh_kernel, rows), [((own, width), BF)], node_grad, enc_gath, second, me=me
    )
    (g_grid,) = call(
        bind(grid_kernel, rows),
        [(grid_feat.shape, BF)],
        slot_back.reshape(dom, caps * width),
        enc_send,
        enc_gath,
    )
    return (out_rows, g_grid, g_mesh) + tuple(totals)


def solution(mesh):
    dom, feat = mesh.shape["dom"], mesh.shape["feat"]
    x = 4 if dom % 8 == 0 else 1
    finer = Mesh(mesh.devices.reshape(dom // (2 * x), x, 2, feat), ALL)
    return jax.shard_map(
        per_device,
        mesh=finer,
        in_specs=(
            P(ALL, None),
            P(ALL, None),
            P("y", None),
            P("y", None),
            P("y", None),
            P("y", None),
            P("y", None),
            P("y", None),
            P(ALL, None),
            P(ALL, None),
            P(DOM, None),
            P(ALL),
            P(ALL),
            P(ALL, None),
        ),
        out_specs=(
            P(ALL, None),
            P(ALL, None),
            P(ALL, None),
            P("y", None),
            P("y", None),
            P("y", None),
            P("y", None),
            P("y", None),
            P("y", None),
        ),
        check_vma=False,
    )
```

```python
import functools
import math

import jax
import jax.numpy as jnp
from jax import lax
from jax.experimental import pallas as pl
from jax.experimental.pallas import tpu as pltpu
from jax.sharding import Mesh
from jax.sharding import PartitionSpec as P

DOM = ("z", "x", "c")
ALL = ("z", "x", "c", "y")
EPS = 1e-05
BF = jnp.bfloat16
F32 = jnp.float32
PAD = 16


def call(kernel, outs, *operands, me=None, scratch=()):
    specs = [pl.BlockSpec()] * len(operands)
    if me is not None:
        operands = (me, *operands)
        specs = [pl.BlockSpec(memory_space=pltpu.SMEM), *specs]
    return pl.pallas_call(
        kernel,
        out_shape=tuple(jax.ShapeDtypeStruct(s, d) for s, d in outs),
        in_specs=specs,
        out_specs=tuple(pl.BlockSpec() for _ in outs),
        scratch_shapes=list(scratch),
        compiler_params=pltpu.CompilerParams(vmem_limit_bytes=60 * 1024 * 1024),
    )(*operands)


def over_cores(keep, give, tail):
    given = lax.ppermute(give, "c", [(0, 1), (1, 0)])
    size = (keep.shape[0] + tail.shape[0], keep.shape[1])
    kernel = functools.partial(merge_kernel, lax.axis_size("y"))
    return call(kernel, [(size, BF)], keep, given, tail)[0]


def exchange(array, axes):
    return lax.all_to_all(array, axes, 0, 0, tiled=True)


def dot(left, right):
    return jnp.dot(left, right, preferred_element_type=F32)


def dot_t(left, right):
    return lax.dot_general(left, right, (((1,), (1,)), ((), ())), preferred_element_type=F32)


def outer(left, right):
    return lax.dot_general(left, right, (((0,), (0,)), ((), ())), preferred_element_type=F32)


def one_hot(row, count):
    places = lax.broadcasted_iota(jnp.int32, (count, row.shape[1]), 0)
    return jnp.where(places == row, 1.0, 0.0).astype(BF)


def slots_hot(indices, count):
    return jnp.concatenate(
        [one_hot(indices[c : c + 1, :], count) for c in range(indices.shape[0])], axis=1
    )


def slot_rows(wide, width):
    return jnp.concatenate(
        [wide[:, c * width : (c + 1) * width] for c in range(wide.shape[1] // width)], axis=0
    )


def wide_rows(rows, count):
    each = rows.shape[0] // count
    return jnp.concatenate([rows[c * each : (c + 1) * each] for c in range(count)], axis=1)


def whole(ref, at, rows):
    return jnp.concatenate(
        [ref[y, at * rows : (at + 1) * rows, :] for y in range(ref.shape[0])], axis=0
    )


def sigmoid(v):
    return 1.0 / (1.0 + jnp.exp(-v))


def layer_norm(values):
    center = values - jnp.mean(values, axis=-1, keepdims=True)
    spread = jnp.mean(center * center, axis=-1, keepdims=True)
    scaling = lax.rsqrt(spread + EPS)
    return (center * scaling, scaling)


def norm_back(normed, scaling, upstream):
    inner = jnp.mean(upstream, axis=-1, keepdims=True)
    along = jnp.mean(upstream * normed, axis=-1, keepdims=True)
    return scaling * (upstream - inner - normed * along)


def pack_kernel(
    send_ref, grid_ref, src_ref, dst_ref, wg_ref, wm_ref, ws_ref, wd_ref, wp_ref, mesh_ref, cot_ref,
    out_ref, enc_ref, proc_ref, line_ref,
):
    grid = grid_ref[...]
    width = grid.shape[1]
    for c in range(send_ref.shape[0]):
        hot = one_hot(send_ref[c : c + 1, :], grid.shape[0])
        out_ref[:, c * width : (c + 1) * width] = outer(hot, grid).astype(BF)
    edges = src_ref.shape[1]
    spare = line_ref.shape[0]
    line_ref[...] = jnp.zeros_like(line_ref)
    place = lax.broadcasted_iota(jnp.int32, (spare, edges), 0)
    source = jnp.broadcast_to(src_ref[...], (spare, edges))
    target = jnp.broadcast_to(dst_ref[...], (spare, edges))
    values = jnp.where(place == 0, source >> 4, jnp.where(place == 1, source & 15, target))
    line_ref[:, :edges] = jnp.where(place < 3, values, 0).astype(F32)
    rows = wg_ref.shape[0]
    for ref, arrays, tail in (
        (enc_ref, (wg_ref, wm_ref), mesh_ref),
        (proc_ref, (ws_ref, wd_ref, wp_ref), cot_ref),
    ):
        for k, array in enumerate(arrays):
            ref[k * rows : (k + 1) * rows, :] = array[...]
        both = jnp.concatenate([tail[...].astype(F32), line_ref[...]], axis=0)
        ref[len(arrays) * rows :, :] = both.astype(BF)


def node_rows(gath_ref, at, own):
    return jnp.concatenate(
        [gath_ref[y, at:, :].astype(F32)[:own] for y in range(gath_ref.shape[0])], axis=0
    )


def own_row(ref, me):
    table = ref[...]
    place = lax.broadcasted_iota(jnp.int32, table.shape, 0)
    return jnp.sum(jnp.where(place == me, table, 0), axis=0, keepdims=True)


def total_of(refs):
    total = refs[0].astype(F32)
    for block in refs[1:]:
        total = total + block.astype(F32)
    return total


def encode_kernel(rows, own, recv_ref, dst_ref, gath_ref, w_ref, sum_ref, pre_ref, norm_ref, scale_ref):
    width = gath_ref.shape[2]
    mesh_part = node_rows(gath_ref, 2 * rows, own).astype(BF)
    received = slot_rows(recv_ref[...], width)
    hot = slots_hot(dst_ref[...], mesh_part.shape[0])
    projected = dot(received, whole(gath_ref, 0, rows)).astype(BF)
    nodes = outer(hot, mesh_part).astype(BF)
    preact = projected.astype(F32) + dot(nodes, whole(gath_ref, 1, rows))
    pre_ref[...] = preact
    hidden = (preact * sigmoid(preact)).astype(BF)
    normed, scaling = layer_norm(dot(hidden, w_ref[...]))
    norm_ref[...] = normed
    scale_ref[...] = scaling
    partial_sum = dot(hot, normed.astype(BF)).astype(BF)
    for y in range(sum_ref.shape[0]):
        sum_ref[y] = partial_sum


def latent_kernel(rows, own, me_ref, sums_ref, gath_ref, send_ref, latent_ref, halo_ref):
    total = total_of([sums_ref[y] for y in range(sums_ref.shape[0])])
    latent = (node_rows(gath_ref, 2 * rows, own) + total).astype(BF)
    latent_ref[...] = latent
    hot = one_hot(own_row(send_ref, me_ref[0]), latent.shape[0])
    halo_ref[...] = outer(hot, latent).astype(BF)


def deal(me_ref, keep_ref, give_ref, tail_ref, term_ref, rows, node_ref, own):
    width = keep_ref.shape[1]
    terms = term_ref.shape[1] // width
    count = term_ref.shape[0] // rows
    half = rows // 2
    held = tail_ref.shape[0] // count
    core = me_ref[1]
    for y in range(count):
        for ref, side in ((keep_ref, core), (give_ref, 1 - core)):
            at = pl.ds(pl.multiple_of(y * rows + side * half, half), half)
            for t in range(terms):
                place = (y * terms + t) * half
                ref[place : place + half, :] = term_ref[at, t * width : (t + 1) * width]
        block = node_ref[y * own : (y + 1) * own, :]
        block = jnp.concatenate([block, jnp.zeros((held - own, width), F32)], axis=0)
        tail_ref[y * held : (y + 1) * held, :] = block.astype(BF)


def merge_kernel(count, keep_ref, given_ref, tail_ref, out_ref):
    size, held = keep_ref.shape[0] // count, tail_ref.shape[0] // count
    for y in range(count):
        at, start = slice(y * size, (y + 1) * size), y * (size + held)
        out_ref[start : start + size, :] = total_of([keep_ref[at, :], given_ref[at, :]]).astype(BF)
        out_ref[start + size : start + size + held, :] = tail_ref[y * held : (y + 1) * held, :]


def process_kernel(
    rows, own, latent_ref, halo_ref, source_ref, target_ref, gath_ref,
    back_ref, local_ref, dst_ref, node_ref, hidden_ref, mid_ref,
):
    latent = latent_ref[...]
    table = jnp.concatenate([latent, halo_ref[...]], axis=0)
    nodes = latent.shape[0]
    hot_src = one_hot(source_ref[...], table.shape[0])
    hot_dst = one_hot(target_ref[...], nodes)
    w_src, w_dst, w_out = [whole(gath_ref, k, rows) for k in range(3)]
    src_rows = outer(hot_src, table).astype(BF)
    dst_rows = outer(hot_dst, latent).astype(BF)
    preact = dot(src_rows, w_src) + dot(dst_rows, w_dst)
    gate = sigmoid(preact)
    hidden = (preact * gate).astype(BF)
    hidden_ref[...] = hidden
    normed, scaling = layer_norm(dot(hidden, w_out))
    node_ref[...] = dot(hot_dst, normed.astype(BF))
    upstream = outer(hot_dst, node_rows(gath_ref, 3 * rows, own).astype(BF))
    mid = norm_back(normed, scaling, upstream).astype(BF)
    mid_ref[...] = mid
    grad = (dot_t(mid, w_out) * (gate * (1.0 + preact * (1.0 - gate)))).astype(BF)
    dst_ref[...] = dot(hot_dst, grad).astype(BF)
    at_src = dot(hot_src, grad)
    local_ref[...] = at_src[:nodes]
    back_ref[...] = at_src[nodes:].astype(BF)


def process_terms_kernel(rows, own, latent_ref, dst_ref, hidden_ref, mid_ref, node_ref, out_ref, term_ref):
    width = latent_ref.shape[1]
    term_ref[:, :width] = outer(latent_ref[...], dst_ref[...]).astype(BF)
    term_ref[:, width:] = outer(hidden_ref[...], mid_ref[...]).astype(BF)
    count = term_ref.shape[0] // rows
    size = out_ref.shape[0] // count
    for y in range(count):
        for t in range(2):
            at = y * size + t * rows
            block = term_ref[y * rows : (y + 1) * rows, t * width : (t + 1) * width]
            out_ref[at : at + rows, :] = block
        block = node_ref[y * own : (y + 1) * own, :]
        block = jnp.concatenate([block, jnp.zeros((size - 2 * rows - own, width), F32)], axis=0)
        out_ref[y * size + 2 * rows : (y + 1) * size, :] = block.astype(BF)


def owner_kernel(rows, me_ref, back_ref, send_ref, local_ref, dst_ref, gath_ref, out_ref, src_ref):
    hot = one_hot(own_row(send_ref, me_ref[0]), local_ref.shape[0])
    at_src = (local_ref[...] + dot(hot, back_ref[...])).astype(BF)
    src_ref[...] = at_src
    total = dot_t(at_src, whole(gath_ref, 0, rows)) + dot_t(dst_ref[...], whole(gath_ref, 1, rows))
    total = total.astype(BF)
    for y in range(out_ref.shape[0]):
        out_ref[y] = total


def backward_kernel(
    rows, own, me_ref, sums_ref, proc_ref, latent_ref, src_ref, enc_ref, w_ref, recv_ref, dst_ref,
    pre_ref, norm_ref, scale_ref,
    node_ref, slot_ref, keep_ref, give_ref, tail_ref, term_ref, share_ref,
):
    nodes, width = latent_ref.shape
    node_grad = node_rows(proc_ref, 3 * rows, own) + total_of(
        [sums_ref[y] for y in range(sums_ref.shape[0])]
    )
    node_ref[...] = node_grad
    hot = slots_hot(dst_ref[...], nodes)
    upstream = outer(hot, node_grad.astype(BF))
    mid = norm_back(norm_ref[...], scale_ref[...], upstream).astype(BF)
    preact = pre_ref[...]
    gate = sigmoid(preact)
    hidden = (preact * gate).astype(BF)
    grad = dot_t(mid, w_ref[...]) * (gate * (1.0 + preact * (1.0 - gate)))
    grad = grad.astype(BF)
    slot_ref[...] = wide_rows(grad, recv_ref.shape[1] // width)
    at_node = dot(hot, grad)
    share_ref[...] = at_node
    terms = (
        outer(slot_rows(recv_ref[...], width), grad),
        outer(node_rows(enc_ref, 2 * rows, own).astype(BF), at_node.astype(BF)),
        outer(hidden, mid),
        outer(latent_ref[...], src_ref[...]),
    )
    for k, term in enumerate(terms):
        term_ref[:, k * width : (k + 1) * width] = term.astype(BF)
    deal(me_ref, keep_ref, give_ref, tail_ref, term_ref, rows, share_ref, own)


def grid_kernel(rows, back_ref, send_ref, enc_ref, out_ref):
    nodes, width = out_ref.shape
    grads = dot_t(slot_rows(back_ref[...], width), whole(enc_ref, 0, rows)).astype(BF)
    out_ref[...] = dot(slots_hot(send_ref[...], nodes), grads).astype(BF)


def out_kernel(rows, me_ref, latent_ref, first_ref, out_ref):
    own, nodes = out_ref.shape[0], latent_ref.shape[0]
    mine = lax.broadcasted_iota(jnp.int32, (1, own), 1) + me_ref[0] * own
    latent = outer(one_hot(mine, nodes), latent_ref[...])
    out_ref[...] = (latent + first_ref[2 * rows :, :].astype(F32)[:own]).astype(BF)


def level_kernel(me_ref, second_ref, first_ref, given_ref, out_ref):
    width = second_ref.shape[1]
    half = out_ref.shape[0]
    for k in range(4):
        out_ref[:, k * width : (k + 1) * width] = second_ref[k * half : (k + 1) * half, :]
    for k in range(2):
        mine = pl.ds(pl.multiple_of((2 * k + me_ref[1]) * half, half), half)
        block = total_of([first_ref[mine, :], given_ref[k * half : (k + 1) * half, :]])
        out_ref[:, (4 + k) * width : (5 + k) * width] = block.astype(BF)


def mesh_kernel(rows, me_ref, node_ref, enc_ref, second_ref, mesh_ref):
    own = mesh_ref.shape[0]
    held = own + (-own % PAD)
    total = second_ref[second_ref.shape[0] - held :, :]
    back = dot_t(total, whole(enc_ref, 1, rows))[:own]
    node = node_ref[pl.ds(pl.multiple_of(me_ref[0] * own, 8), own), :]
    mesh_ref[...] = (node + back).astype(BF)


def sum_kernel(in_ref, out_ref):
    out_ref[...] = total_of([in_ref[k] for k in range(in_ref.shape[0])]).astype(out_ref.dtype)


def split_kernel(factor, in_ref, *out_refs):
    count, thin, _ = in_ref.shape
    width = out_refs[0].shape[1]
    for r in range(count):
        for k, ref in enumerate(out_refs):
            block = in_ref[r, :, k * width : (k + 1) * width]
            ref[r * thin : (r + 1) * thin, :] = block.astype(F32) * factor


def per_device(
    grid_feat,
    mesh_feat,
    w_grid,
    w_mesh,
    w_enc2,
    w_src,
    w_dst,
    w_proc2,
    enc_send,
    enc_dst,
    hal_send,
    proc_src,
    proc_dst,
    cotangent,
):
    enc_send, enc_dst, hal_send = enc_send.T, enc_dst.T, hal_send.T
    dom = lax.axis_size(DOM)
    feat = lax.axis_size("y")
    deep = lax.axis_size("z")
    own, width = mesh_feat.shape
    nodes = own * feat
    rows = w_grid.shape[0]
    caps = enc_send.shape[0]
    pair = (dom, 2, width // 2)
    halo = hal_send.shape[0]
    edges = proc_src.shape[0]
    held = own + (-own % PAD)
    factor = 1.0 / math.sqrt(own * dom * feat)
    index = lax.axis_index("y")
    me = jnp.stack([index, lax.axis_index("c")])
    if halo != feat or held - own < 8 or edges > width:
        raise ValueError("sizes")
    bind = functools.partial

    half = rows // 2
    outgoing, enc_pack, proc_pack = call(
        pack_kernel,
        [
            ((dom, caps * width), BF),
            ((2 * rows + held, width), BF),
            ((3 * rows + held, width), BF),
        ],
        enc_send,
        grid_feat,
        proc_src.reshape(1, edges),
        proc_dst.reshape(1, edges),
        w_grid,
        w_mesh,
        w_src,
        w_dst,
        w_proc2,
        mesh_feat,
        cotangent,
        scratch=[pltpu.VMEM((held - own, width), F32)],
    )
    received = exchange(outgoing.reshape(dom, caps, width), DOM).reshape(dom, caps * width)
    enc_gath = lax.all_gather(enc_pack, "y", axis=0)
    full_enc2 = lax.all_gather(w_enc2, "y", axis=0, tiled=True)
    proc_gath = lax.all_gather(proc_pack, "y", axis=0)

    slots = dom * caps
    one_sum, all_sums = ((nodes, width), BF), ((feat, nodes, width), BF)
    partial_sum, preact, normed, scaling = call(
        bind(encode_kernel, rows, own),
        [
            all_sums,
            ((slots, width), F32),
            ((slots, width), F32),
            ((slots, 1), F32),
        ],
        received,
        enc_dst,
        enc_gath,
        full_enc2,
    )
    latent, halo_out = call(
        bind(latent_kernel, rows, own),
        [one_sum, ((dom, width), BF)],
        exchange(partial_sum, "y"),
        enc_gath,
        hal_send,
        me=me,
    )
    halo_rows = exchange(halo_out.reshape(pair), DOM).reshape(dom, width)

    lines = enc_gath[:, 2 * rows + own : 2 * rows + own + 3, :edges].astype(jnp.int32)
    source = lines[:, 0] * 16 + lines[:, 1]
    slot = source - nodes
    place = jnp.where(slot < 0, source, nodes + slot // halo)
    keeper = jnp.where(slot < 0, jnp.arange(feat, dtype=jnp.int32)[:, None], slot % halo)
    mine = keeper == index
    halo_back, at_local, at_dst, messages, hidden, mid = call(
        bind(process_kernel, rows, own),
        [
            ((dom, width), BF),
            ((nodes, width), F32),
            one_sum,
            ((nodes, width), F32),
            ((feat * edges, width), BF),
            ((feat * edges, width), BF),
        ],
        latent,
        halo_rows,
        jnp.where(mine, place, -1).reshape(1, feat * edges),
        jnp.where(mine, lines[:, 2], -1).reshape(1, feat * edges),
        proc_gath,
    )
    returned = exchange(halo_back.reshape(pair), DOM)
    (first,) = call(
        bind(process_terms_kernel, rows, own),
        [((feat * (2 * rows + held), width), BF)],
        latent,
        at_dst,
        hidden,
        mid,
        messages,
        scratch=[pltpu.VMEM((width, 2 * width), BF)],
    )
    returned, first = lax.optimization_barrier((returned, first))
    first = lax.psum_scatter(first, "y", scatter_dimension=0, tiled=True)
    node_part, at_src = call(
        bind(owner_kernel, rows),
        [all_sums, one_sum],
        returned.reshape(dom, width),
        hal_send,
        at_local,
        at_dst,
        proc_gath,
        me=me,
    )

    node_in = exchange(node_part, "y")

    node_grad, slot_out, *second = call(
        bind(backward_kernel, rows, own),
        [
            ((nodes, width), F32),
            ((dom, caps * width), BF),
            ((8 * rows, width), BF),
            ((8 * rows, width), BF),
            ((feat * held, width), BF),
        ],
        node_in,
        proc_gath,
        latent,
        at_src,
        enc_gath,
        full_enc2,
        received,
        enc_dst,
        preact,
        normed,
        scaling,
        me=me,
        scratch=[pltpu.VMEM((width, 4 * width), BF), pltpu.VMEM((nodes, width), F32)],
    )
    slot_back = exchange(slot_out.reshape(dom, caps, width), DOM)
    second = over_cores(*second)
    second = lax.psum_scatter(second, "y", scatter_dimension=0, tiled=True)
    give = lax.dynamic_slice_in_dim(first[: 2 * rows].reshape(2, 2, half, width), 1 - me[1], 1, 1)
    given = lax.ppermute(give.reshape(rows, width), "c", [(0, 1), (1, 0)])
    (level,) = call(level_kernel, [((half, 6 * width), BF)], second, first, given, me=me)
    slot_back, level = lax.optimization_barrier((slot_back, level))
    across = lax.axis_size("x")
    thin = rows // (2 * across)
    level = exchange(level.reshape(across, thin, 6 * width), "x")
    (level,) = call(sum_kernel, [((thin, 6 * width), BF)], level)
    level = exchange(level.reshape(deep, 2, 3 * width), "z")
    level = level.astype(F32).sum(axis=0).astype(BF)
    level = exchange(jnp.broadcast_to(level[None], (deep, *level.shape)), "z")
    level = level.reshape(deep, 6 * width)
    near = lax.axis_size(("x", "c"))
    totals = exchange(jnp.broadcast_to(level[None], (near, *level.shape)), ("c", "x"))
    totals = call(bind(split_kernel, factor), [((rows, width), F32)] * 6, totals)
    (out_rows,) = call(bind(out_kernel, rows), [((own, width), BF)], latent, first, me=me)
    (g_mesh,) = call(
        bind(mesh_kernel, rows), [((own, width), BF)], node_grad, enc_gath, second, me=me
    )
    (g_grid,) = call(
        bind(grid_kernel, rows),
        [(grid_feat.shape, BF)],
        slot_back.reshape(dom, caps * width),
        enc_send,
        enc_gath,
    )
    return (out_rows, g_grid, g_mesh) + tuple(totals)


def solution(mesh):
    dom, feat = mesh.shape["dom"], mesh.shape["feat"]
    x = 4 if dom % 8 == 0 else 1
    finer = Mesh(mesh.devices.reshape(dom // (2 * x), x, 2, feat), ALL)
    return jax.shard_map(
        per_device,
        mesh=finer,
        in_specs=(
            P(ALL, None),
            P(ALL, None),
            P("y", None),
            P("y", None),
            P("y", None),
            P("y", None),
            P("y", None),
            P("y", None),
            P(ALL, None),
            P(ALL, None),
            P(DOM, None),
            P(ALL),
            P(ALL),
            P(ALL, None),
        ),
        out_specs=(
            P(ALL, None),
            P(ALL, None),
            P(ALL, None),
            P("y", None),
            P("y", None),
            P("y", None),
            P("y", None),
            P("y", None),
            P("y", None),
        ),
        check_vma=False,
    )
```

```python
import functools
import math

import jax
import jax.numpy as jnp
from jax import lax
from jax.experimental import pallas as pl
from jax.experimental.pallas import tpu as pltpu
from jax.sharding import Mesh
from jax.sharding import PartitionSpec as P

DOM = ("z", "x", "c")
ALL = ("z", "x", "c", "y")
EPS = 1e-05
BF = jnp.bfloat16
F32 = jnp.float32
PAD = 16


def call(kernel, outs, *operands, me=None, scratch=()):
    specs = [pl.BlockSpec()] * len(operands)
    if me is not None:
        operands = (me, *operands)
        specs = [pl.BlockSpec(memory_space=pltpu.SMEM), *specs]
    return pl.pallas_call(
        kernel,
        out_shape=tuple(jax.ShapeDtypeStruct(s, d) for s, d in outs),
        in_specs=specs,
        out_specs=tuple(pl.BlockSpec() for _ in outs),
        scratch_shapes=list(scratch),
        compiler_params=pltpu.CompilerParams(vmem_limit_bytes=60 * 1024 * 1024),
    )(*operands)


def over_cores(keep, give, tail):
    given = lax.ppermute(give, "c", [(0, 1), (1, 0)])
    size = (keep.shape[0] + tail.shape[0], keep.shape[1])
    kernel = functools.partial(merge_kernel, lax.axis_size("y"))
    return call(kernel, [(size, BF)], keep, given, tail)[0]


def onward(blocks):
    n = lax.axis_size("y")
    return [blocks[0]] + [
        lax.ppermute(blocks[k], "y", [(i, (i + k) % n) for i in range(n)]) for k in range(1, n)
    ]


def exchange(array, axes):
    return lax.all_to_all(array, axes, 0, 0, tiled=True)


def dot(left, right):
    return jnp.dot(left, right, preferred_element_type=F32)


def dot_t(left, right):
    return lax.dot_general(left, right, (((1,), (1,)), ((), ())), preferred_element_type=F32)


def outer(left, right):
    return lax.dot_general(left, right, (((0,), (0,)), ((), ())), preferred_element_type=F32)


def one_hot(row, count):
    places = lax.broadcasted_iota(jnp.int32, (count, row.shape[1]), 0)
    return jnp.where(places == row, 1.0, 0.0).astype(BF)


def slots_hot(indices, count):
    return jnp.concatenate(
        [one_hot(indices[c : c + 1, :], count) for c in range(indices.shape[0])], axis=1
    )


def slot_rows(wide, width):
    return jnp.concatenate(
        [wide[:, c * width : (c + 1) * width] for c in range(wide.shape[1] // width)], axis=0
    )


def wide_rows(rows, count):
    each = rows.shape[0] // count
    return jnp.concatenate([rows[c * each : (c + 1) * each] for c in range(count)], axis=1)


def whole(ref, at, rows):
    return jnp.concatenate(
        [ref[y, at * rows : (at + 1) * rows, :] for y in range(ref.shape[0])], axis=0
    )


def sigmoid(v):
    return 1.0 / (1.0 + jnp.exp(-v))


def layer_norm(values):
    center = values - jnp.mean(values, axis=-1, keepdims=True)
    spread = jnp.mean(center * center, axis=-1, keepdims=True)
    scaling = lax.rsqrt(spread + EPS)
    return (center * scaling, scaling)


def norm_back(normed, scaling, upstream):
    inner = jnp.mean(upstream, axis=-1, keepdims=True)
    along = jnp.mean(upstream * normed, axis=-1, keepdims=True)
    return scaling * (upstream - inner - normed * along)


def pack_kernel(
    send_ref, grid_ref, src_ref, dst_ref, wg_ref, wm_ref, ws_ref, wd_ref, wp_ref, mesh_ref, cot_ref,
    out_ref, enc_ref, proc_ref, line_ref,
):
    grid = grid_ref[...]
    width = grid.shape[1]
    for c in range(send_ref.shape[0]):
        hot = one_hot(send_ref[c : c + 1, :], grid.shape[0])
        out_ref[:, c * width : (c + 1) * width] = outer(hot, grid).astype(BF)
    edges = src_ref.shape[1]
    spare = line_ref.shape[0]
    line_ref[...] = jnp.zeros_like(line_ref)
    place = lax.broadcasted_iota(jnp.int32, (spare, edges), 0)
    source = jnp.broadcast_to(src_ref[...], (spare, edges))
    target = jnp.broadcast_to(dst_ref[...], (spare, edges))
    values = jnp.where(place == 0, source >> 4, jnp.where(place == 1, source & 15, target))
    line_ref[:, :edges] = jnp.where(place < 3, values, 0).astype(F32)
    rows = wg_ref.shape[0]
    for ref, arrays, tail in (
        (enc_ref, (wg_ref, wm_ref), mesh_ref),
        (proc_ref, (ws_ref, wd_ref, wp_ref), cot_ref),
    ):
        for k, array in enumerate(arrays):
            ref[k * rows : (k + 1) * rows, :] = array[...]
        both = jnp.concatenate([tail[...].astype(F32), line_ref[...]], axis=0)
        ref[len(arrays) * rows :, :] = both.astype(BF)


def node_rows(gath_ref, at, own):
    return jnp.concatenate(
        [gath_ref[y, at:, :].astype(F32)[:own] for y in range(gath_ref.shape[0])], axis=0
    )


def own_row(ref, me):
    table = ref[...]
    place = lax.broadcasted_iota(jnp.int32, table.shape, 0)
    return jnp.sum(jnp.where(place == me, table, 0), axis=0, keepdims=True)


def total_of(refs):
    total = refs[0].astype(F32)
    for block in refs[1:]:
        total = total + block.astype(F32)
    return total


def encode_kernel(rows, own, recv_ref, dst_ref, gath_ref, w_ref, sum_ref, pre_ref, norm_ref, scale_ref):
    width = gath_ref.shape[2]
    mesh_part = node_rows(gath_ref, 2 * rows, own).astype(BF)
    received = slot_rows(recv_ref[...], width)
    hot = slots_hot(dst_ref[...], mesh_part.shape[0])
    projected = dot(received, whole(gath_ref, 0, rows)).astype(BF)
    nodes = outer(hot, mesh_part).astype(BF)
    preact = projected.astype(F32) + dot(nodes, whole(gath_ref, 1, rows))
    pre_ref[...] = preact
    hidden = (preact * sigmoid(preact)).astype(BF)
    normed, scaling = layer_norm(dot(hidden, w_ref[...]))
    norm_ref[...] = normed
    scale_ref[...] = scaling
    partial_sum = dot(hot, normed.astype(BF)).astype(BF)
    for y in range(sum_ref.shape[0]):
        sum_ref[y] = partial_sum


def latent_kernel(rows, own, me_ref, sums_ref, gath_ref, send_ref, latent_ref, halo_ref):
    total = total_of([sums_ref[y] for y in range(sums_ref.shape[0])])
    latent = (node_rows(gath_ref, 2 * rows, own) + total).astype(BF)
    latent_ref[...] = latent
    hot = one_hot(own_row(send_ref, me_ref[0]), latent.shape[0])
    halo_ref[...] = outer(hot, latent).astype(BF)


def deal(me_ref, keep_ref, give_ref, tail_ref, term_ref, rows, node_ref, own):
    width = keep_ref.shape[1]
    terms = term_ref.shape[1] // width
    count = term_ref.shape[0] // rows
    half = rows // 2
    held = tail_ref.shape[0] // count
    core = me_ref[1]
    for y in range(count):
        for ref, side in ((keep_ref, core), (give_ref, 1 - core)):
            at = pl.ds(pl.multiple_of(y * rows + side * half, half), half)
            for t in range(terms):
                place = (y * terms + t) * half
                ref[place : place + half, :] = term_ref[at, t * width : (t + 1) * width]
        block = node_ref[y * own : (y + 1) * own, :]
        block = jnp.concatenate([block, jnp.zeros((held - own, width), F32)], axis=0)
        tail_ref[y * held : (y + 1) * held, :] = block.astype(BF)


def merge_kernel(count, keep_ref, given_ref, tail_ref, out_ref):
    size, held = keep_ref.shape[0] // count, tail_ref.shape[0] // count
    for y in range(count):
        at, start = slice(y * size, (y + 1) * size), y * (size + held)
        out_ref[start : start + size, :] = total_of([keep_ref[at, :], given_ref[at, :]]).astype(BF)
        out_ref[start + size : start + size + held, :] = tail_ref[y * held : (y + 1) * held, :]


def process_kernel(
    rows, own, latent_ref, halo_ref, source_ref, target_ref, gath_ref,
    back_ref, local_ref, dst_ref, node_ref, hidden_ref, mid_ref,
):
    latent = latent_ref[...]
    table = jnp.concatenate([latent, halo_ref[...]], axis=0)
    nodes = latent.shape[0]
    hot_src = one_hot(source_ref[...], table.shape[0])
    hot_dst = one_hot(target_ref[...], nodes)
    w_src, w_dst, w_out = [whole(gath_ref, k, rows) for k in range(3)]
    src_rows = outer(hot_src, table).astype(BF)
    dst_rows = outer(hot_dst, latent).astype(BF)
    preact = dot(src_rows, w_src) + dot(dst_rows, w_dst)
    gate = sigmoid(preact)
    hidden = (preact * gate).astype(BF)
    hidden_ref[...] = hidden
    normed, scaling = layer_norm(dot(hidden, w_out))
    node_ref[...] = dot(hot_dst, normed.astype(BF))
    upstream = outer(hot_dst, node_rows(gath_ref, 3 * rows, own).astype(BF))
    mid = norm_back(normed, scaling, upstream).astype(BF)
    mid_ref[...] = mid
    grad = (dot_t(mid, w_out) * (gate * (1.0 + preact * (1.0 - gate)))).astype(BF)
    dst_ref[...] = dot(hot_dst, grad).astype(BF)
    at_src = dot(hot_src, grad)
    local_ref[...] = at_src[:nodes]
    back_ref[...] = at_src[nodes:].astype(BF)


def process_terms_kernel(
    rows, own, me_ref, latent_ref, dst_ref, hidden_ref, mid_ref, node_ref,
    keep_ref, give_ref, tail_ref, term_ref,
):
    width = latent_ref.shape[1]
    term_ref[:, :width] = outer(latent_ref[...], dst_ref[...]).astype(BF)
    term_ref[:, width:] = outer(hidden_ref[...], mid_ref[...]).astype(BF)
    deal(me_ref, keep_ref, give_ref, tail_ref, term_ref, rows, node_ref, own)


def owner_kernel(rows, me_ref, back_ref, send_ref, local_ref, dst_ref, gath_ref, out_ref, src_ref):
    hot = one_hot(own_row(send_ref, me_ref[0]), local_ref.shape[0])
    at_src = (local_ref[...] + dot(hot, back_ref[...])).astype(BF)
    src_ref[...] = at_src
    total = dot_t(at_src, whole(gath_ref, 0, rows)) + dot_t(dst_ref[...], whole(gath_ref, 1, rows))
    total = total.astype(BF)
    for y in range(out_ref.shape[0]):
        out_ref[y] = total


def backward_kernel(
    rows, own, me_ref, sums_ref, proc_ref, latent_ref, src_ref, enc_ref, w_ref, recv_ref, dst_ref,
    pre_ref, norm_ref, scale_ref,
    node_ref, slot_ref, keep_ref, give_ref, tail_ref, term_ref, share_ref,
):
    nodes, width = latent_ref.shape
    node_grad = node_rows(proc_ref, 3 * rows, own) + total_of(
        [sums_ref[y] for y in range(sums_ref.shape[0])]
    )
    node_ref[...] = node_grad
    hot = slots_hot(dst_ref[...], nodes)
    upstream = outer(hot, node_grad.astype(BF))
    mid = norm_back(norm_ref[...], scale_ref[...], upstream).astype(BF)
    preact = pre_ref[...]
    gate = sigmoid(preact)
    hidden = (preact * gate).astype(BF)
    grad = dot_t(mid, w_ref[...]) * (gate * (1.0 + preact * (1.0 - gate)))
    grad = grad.astype(BF)
    slot_ref[...] = wide_rows(grad, recv_ref.shape[1] // width)
    at_node = dot(hot, grad)
    share_ref[...] = at_node
    terms = (
        outer(slot_rows(recv_ref[...], width), grad),
        outer(node_rows(enc_ref, 2 * rows, own).astype(BF), at_node.astype(BF)),
        outer(hidden, mid),
        outer(latent_ref[...], src_ref[...]),
    )
    for k, term in enumerate(terms):
        term_ref[:, k * width : (k + 1) * width] = term.astype(BF)
    deal(me_ref, keep_ref, give_ref, tail_ref, term_ref, rows, share_ref, own)


def grid_kernel(rows, back_ref, send_ref, enc_ref, out_ref):
    nodes, width = out_ref.shape
    grads = dot_t(slot_rows(back_ref[...], width), whole(enc_ref, 0, rows)).astype(BF)
    out_ref[...] = dot(slots_hot(send_ref[...], nodes), grads).astype(BF)


def out_kernel(me_ref, latent_ref, b0_ref, b1_ref, b2_ref, b3_ref, out_ref):
    own, nodes = out_ref.shape[0], latent_ref.shape[0]
    start = b0_ref.shape[0] - own - (-own % PAD)
    total = total_of([b[start:, :] for b in (b0_ref, b1_ref, b2_ref, b3_ref)])
    mine = lax.broadcasted_iota(jnp.int32, (1, own), 1) + me_ref[0] * own
    latent = outer(one_hot(mine, nodes), latent_ref[...])
    out_ref[...] = (latent + total[:own]).astype(BF)


def level_kernel(second_ref, b0_ref, b1_ref, b2_ref, b3_ref, out_ref):
    width = second_ref.shape[1]
    half = out_ref.shape[0]
    for k in range(4):
        out_ref[:, k * width : (k + 1) * width] = second_ref[k * half : (k + 1) * half, :]
    for k in range(2):
        at = slice(k * half, (k + 1) * half)
        block = total_of([b[at, :] for b in (b0_ref, b1_ref, b2_ref, b3_ref)])
        out_ref[:, (4 + k) * width : (5 + k) * width] = block.astype(BF)


def deal_out_kernel(me_ref, in_ref, *out_refs):
    count = len(out_refs)
    size = out_refs[0].shape[0]
    for k, ref in enumerate(out_refs):
        to = lax.rem(me_ref[0] + k, count)
        ref[...] = in_ref[pl.ds(pl.multiple_of(to * size, PAD), size), :]


def mesh_kernel(rows, me_ref, node_ref, enc_ref, second_ref, mesh_ref):
    own = mesh_ref.shape[0]
    held = own + (-own % PAD)
    total = second_ref[second_ref.shape[0] - held :, :]
    back = dot_t(total, whole(enc_ref, 1, rows))[:own]
    node = node_ref[pl.ds(pl.multiple_of(me_ref[0] * own, 8), own), :]
    mesh_ref[...] = (node + back).astype(BF)


def sum_kernel(in_ref, out_ref):
    out_ref[...] = total_of([in_ref[k] for k in range(in_ref.shape[0])]).astype(out_ref.dtype)


def split_kernel(factor, in_ref, *out_refs):
    count, thin, _ = in_ref.shape
    width = out_refs[0].shape[1]
    for r in range(count):
        for k, ref in enumerate(out_refs):
            block = in_ref[r, :, k * width : (k + 1) * width]
            ref[r * thin : (r + 1) * thin, :] = block.astype(F32) * factor


def per_device(
    grid_feat,
    mesh_feat,
    w_grid,
    w_mesh,
    w_enc2,
    w_src,
    w_dst,
    w_proc2,
    enc_send,
    enc_dst,
    hal_send,
    proc_src,
    proc_dst,
    cotangent,
):
    enc_send, enc_dst, hal_send = enc_send.T, enc_dst.T, hal_send.T
    dom = lax.axis_size(DOM)
    feat = lax.axis_size("y")
    deep = lax.axis_size("z")
    own, width = mesh_feat.shape
    nodes = own * feat
    rows = w_grid.shape[0]
    caps = enc_send.shape[0]
    pair = (dom, 2, width // 2)
    halo = hal_send.shape[0]
    edges = proc_src.shape[0]
    held = own + (-own % PAD)
    factor = 1.0 / math.sqrt(own * dom * feat)
    index = lax.axis_index("y")
    me = jnp.stack([index, lax.axis_index("c")])
    if halo != feat or held - own < 8 or edges > width:
        raise ValueError("sizes")
    bind = functools.partial

    half = rows // 2
    outgoing, enc_pack, proc_pack = call(
        pack_kernel,
        [
            ((dom, caps * width), BF),
            ((2 * rows + held, width), BF),
            ((3 * rows + held, width), BF),
        ],
        enc_send,
        grid_feat,
        proc_src.reshape(1, edges),
        proc_dst.reshape(1, edges),
        w_grid,
        w_mesh,
        w_src,
        w_dst,
        w_proc2,
        mesh_feat,
        cotangent,
        scratch=[pltpu.VMEM((held - own, width), F32)],
    )
    received = exchange(outgoing.reshape(dom, caps, width), DOM).reshape(dom, caps * width)
    enc_gath = lax.all_gather(enc_pack, "y", axis=0)
    full_enc2 = lax.all_gather(w_enc2, "y", axis=0, tiled=True)
    proc_gath = lax.all_gather(proc_pack, "y", axis=0)

    slots = dom * caps
    one_sum, all_sums = ((nodes, width), BF), ((feat, nodes, width), BF)
    partial_sum, preact, normed, scaling = call(
        bind(encode_kernel, rows, own),
        [
            all_sums,
            ((slots, width), F32),
            ((slots, width), F32),
            ((slots, 1), F32),
        ],
        received,
        enc_dst,
        enc_gath,
        full_enc2,
    )
    latent, halo_out = call(
        bind(latent_kernel, rows, own),
        [one_sum, ((dom, width), BF)],
        exchange(partial_sum, "y"),
        enc_gath,
        hal_send,
        me=me,
    )
    halo_rows = exchange(halo_out.reshape(pair), DOM).reshape(dom, width)

    lines = enc_gath[:, 2 * rows + own : 2 * rows + own + 3, :edges].astype(jnp.int32)
    source = lines[:, 0] * 16 + lines[:, 1]
    slot = source - nodes
    place = jnp.where(slot < 0, source, nodes + slot // halo)
    keeper = jnp.where(slot < 0, jnp.arange(feat, dtype=jnp.int32)[:, None], slot % halo)
    mine = keeper == index
    halo_back, at_local, at_dst, messages, hidden, mid = call(
        bind(process_kernel, rows, own),
        [
            ((dom, width), BF),
            ((nodes, width), F32),
            one_sum,
            ((nodes, width), F32),
            ((feat * edges, width), BF),
            ((feat * edges, width), BF),
        ],
        latent,
        halo_rows,
        jnp.where(mine, place, -1).reshape(1, feat * edges),
        jnp.where(mine, lines[:, 2], -1).reshape(1, feat * edges),
        proc_gath,
    )
    returned = exchange(halo_back.reshape(pair), DOM)
    first = call(
        bind(process_terms_kernel, rows, own),
        [((4 * rows, width), BF), ((4 * rows, width), BF), ((feat * held, width), BF)],
        latent,
        at_dst,
        hidden,
        mid,
        messages,
        me=me,
        scratch=[pltpu.VMEM((width, 2 * width), BF)],
    )
    first = over_cores(*first)
    first = call(deal_out_kernel, [((first.shape[0] // feat, width), BF)] * feat, first, me=me)
    node_part, at_src = call(
        bind(owner_kernel, rows),
        [all_sums, one_sum],
        returned.reshape(dom, width),
        hal_send,
        at_local,
        at_dst,
        proc_gath,
        me=me,
    )

    node_in, *first = lax.optimization_barrier((exchange(node_part, "y"), *first))

    node_grad, slot_out, *second = call(
        bind(backward_kernel, rows, own),
        [
            ((nodes, width), F32),
            ((dom, caps * width), BF),
            ((8 * rows, width), BF),
            ((8 * rows, width), BF),
            ((feat * held, width), BF),
        ],
        node_in,
        proc_gath,
        latent,
        at_src,
        enc_gath,
        full_enc2,
        received,
        enc_dst,
        preact,
        normed,
        scaling,
        me=me,
        scratch=[pltpu.VMEM((width, 4 * width), BF), pltpu.VMEM((nodes, width), F32)],
    )
    slot_back = exchange(slot_out.reshape(dom, caps, width), DOM)
    second = over_cores(*second)
    second, *first = lax.optimization_barrier((second, *first))
    first = onward(first)
    second = lax.psum_scatter(second, "y", scatter_dimension=0, tiled=True)
    (level,) = call(level_kernel, [((half, 6 * width), BF)], second, *first)
    slot_back, level = lax.optimization_barrier((slot_back, level))
    across = lax.axis_size("x")
    thin = rows // (2 * across)
    level = exchange(level.reshape(across, thin, 6 * width), "x")
    (level,) = call(sum_kernel, [((thin, 6 * width), BF)], level)
    level = exchange(level.reshape(deep, 2, 3 * width), "z")
    level = level.astype(F32).sum(axis=0).astype(BF)
    level = exchange(jnp.broadcast_to(level[None], (deep, *level.shape)), "z")
    level = level.reshape(deep, 6 * width)
    near = lax.axis_size(("x", "c"))
    totals = exchange(jnp.broadcast_to(level[None], (near, *level.shape)), ("c", "x"))
    totals = call(bind(split_kernel, factor), [((rows, width), F32)] * 6, totals)
    (out_rows,) = call(out_kernel, [((own, width), BF)], latent, *first, me=me)
    (g_mesh,) = call(
        bind(mesh_kernel, rows), [((own, width), BF)], node_grad, enc_gath, second, me=me
    )
    (g_grid,) = call(
        bind(grid_kernel, rows),
        [(grid_feat.shape, BF)],
        slot_back.reshape(dom, caps * width),
        enc_send,
        enc_gath,
    )
    return (out_rows, g_grid, g_mesh) + tuple(totals)


def solution(mesh):
    dom, feat = mesh.shape["dom"], mesh.shape["feat"]
    x = 4 if dom % 8 == 0 else 1
    finer = Mesh(mesh.devices.reshape(dom // (2 * x), x, 2, feat), ALL)
    return jax.shard_map(
        per_device,
        mesh=finer,
        in_specs=(
            P(ALL, None),
            P(ALL, None),
            P("y", None),
            P("y", None),
            P("y", None),
            P("y", None),
            P("y", None),
            P("y", None),
            P(ALL, None),
            P(ALL, None),
            P(DOM, None),
            P(ALL),
            P(ALL),
            P(ALL, None),
        ),
        out_specs=(
            P(ALL, None),
            P(ALL, None),
            P(ALL, None),
            P("y", None),
            P("y", None),
            P("y", None),
            P("y", None),
            P("y", None),
            P("y", None),
        ),
        check_vma=False,
    )
```

```python
import functools
import math

import jax
import jax.numpy as jnp
from jax import lax
from jax.experimental import pallas as pl
from jax.experimental.pallas import tpu as pltpu
from jax.sharding import Mesh
from jax.sharding import PartitionSpec as P

DOM = ("z", "x", "c")
ALL = ("z", "x", "c", "y")
EPS = 1e-05
BF = jnp.bfloat16
F32 = jnp.float32
PAD = 16


def call(kernel, outs, *operands, me=None, scratch=()):
    specs = [pl.BlockSpec()] * len(operands)
    if me is not None:
        operands = (me, *operands)
        specs = [pl.BlockSpec(memory_space=pltpu.SMEM), *specs]
    return pl.pallas_call(
        kernel,
        out_shape=tuple(jax.ShapeDtypeStruct(s, d) for s, d in outs),
        in_specs=specs,
        out_specs=tuple(pl.BlockSpec() for _ in outs),
        scratch_shapes=list(scratch),
        compiler_params=pltpu.CompilerParams(vmem_limit_bytes=60 * 1024 * 1024),
    )(*operands)


def over_cores(keep, give, tail):
    given = lax.ppermute(give, "c", [(0, 1), (1, 0)])
    size = (keep.shape[0] + tail.shape[0], keep.shape[1])
    kernel = functools.partial(merge_kernel, lax.axis_size("y"))
    return call(kernel, [(size, BF)], keep, given, tail)[0]


def exchange(array, axes):
    return lax.all_to_all(array, axes, 0, 0, tiled=True)


def dot(left, right):
    return jnp.dot(left, right, preferred_element_type=F32)


def dot_t(left, right):
    return lax.dot_general(left, right, (((1,), (1,)), ((), ())), preferred_element_type=F32)


def outer(left, right):
    return lax.dot_general(left, right, (((0,), (0,)), ((), ())), preferred_element_type=F32)


def one_hot(row, count):
    places = lax.broadcasted_iota(jnp.int32, (count, row.shape[1]), 0)
    return jnp.where(places == row, 1.0, 0.0).astype(BF)


def slots_hot(indices, count):
    return jnp.concatenate(
        [one_hot(indices[c : c + 1, :], count) for c in range(indices.shape[0])], axis=1
    )


def slot_rows(wide, width):
    return jnp.concatenate(
        [wide[:, c * width : (c + 1) * width] for c in range(wide.shape[1] // width)], axis=0
    )


def wide_rows(rows, count):
    each = rows.shape[0] // count
    return jnp.concatenate([rows[c * each : (c + 1) * each] for c in range(count)], axis=1)


def whole(ref, at, rows):
    return jnp.concatenate(
        [ref[y, at * rows : (at + 1) * rows, :] for y in range(ref.shape[0])], axis=0
    )


def sigmoid(v):
    return 1.0 / (1.0 + jnp.exp(-v))


def layer_norm(values):
    center = values - jnp.mean(values, axis=-1, keepdims=True)
    spread = jnp.mean(center * center, axis=-1, keepdims=True)
    scaling = lax.rsqrt(spread + EPS)
    return (center * scaling, scaling)


def norm_back(normed, scaling, upstream):
    inner = jnp.mean(upstream, axis=-1, keepdims=True)
    along = jnp.mean(upstream * normed, axis=-1, keepdims=True)
    return scaling * (upstream - inner - normed * along)


def pack_kernel(
    send_ref, grid_ref, src_ref, dst_ref, wg_ref, wm_ref, ws_ref, wd_ref, wp_ref, mesh_ref, cot_ref,
    out_ref, enc_ref, proc_ref, line_ref,
):
    grid = grid_ref[...]
    width = grid.shape[1]
    for c in range(send_ref.shape[0]):
        hot = one_hot(send_ref[c : c + 1, :], grid.shape[0])
        out_ref[:, c * width : (c + 1) * width] = outer(hot, grid).astype(BF)
    edges = src_ref.shape[1]
    spare = line_ref.shape[0]
    line_ref[...] = jnp.zeros_like(line_ref)
    place = lax.broadcasted_iota(jnp.int32, (spare, edges), 0)
    source = jnp.broadcast_to(src_ref[...], (spare, edges))
    target = jnp.broadcast_to(dst_ref[...], (spare, edges))
    values = jnp.where(place == 0, source >> 4, jnp.where(place == 1, source & 15, target))
    line_ref[:, :edges] = jnp.where(place < 3, values, 0).astype(F32)
    rows = wg_ref.shape[0]
    for ref, arrays, tail in (
        (enc_ref, (wg_ref, wm_ref), mesh_ref),
        (proc_ref, (ws_ref, wd_ref, wp_ref), cot_ref),
    ):
        for k, array in enumerate(arrays):
            ref[k * rows : (k + 1) * rows, :] = array[...]
        both = jnp.concatenate([tail[...].astype(F32), line_ref[...]], axis=0)
        ref[len(arrays) * rows :, :] = both.astype(BF)


def node_rows(gath_ref, at, own):
    return jnp.concatenate(
        [gath_ref[y, at:, :].astype(F32)[:own] for y in range(gath_ref.shape[0])], axis=0
    )


def own_row(ref, me):
    table = ref[...]
    place = lax.broadcasted_iota(jnp.int32, table.shape, 0)
    return jnp.sum(jnp.where(place == me, table, 0), axis=0, keepdims=True)


def total_of(refs):
    total = refs[0].astype(F32)
    for block in refs[1:]:
        total = total + block.astype(F32)
    return total


def encode_kernel(rows, own, recv_ref, dst_ref, gath_ref, w_ref, sum_ref, pre_ref, norm_ref, scale_ref):
    width = gath_ref.shape[2]
    mesh_part = node_rows(gath_ref, 2 * rows, own).astype(BF)
    received = slot_rows(recv_ref[...], width)
    hot = slots_hot(dst_ref[...], mesh_part.shape[0])
    projected = dot(received, whole(gath_ref, 0, rows)).astype(BF)
    nodes = outer(hot, mesh_part).astype(BF)
    preact = projected.astype(F32) + dot(nodes, whole(gath_ref, 1, rows))
    pre_ref[...] = preact
    hidden = (preact * sigmoid(preact)).astype(BF)
    normed, scaling = layer_norm(dot(hidden, w_ref[...]))
    norm_ref[...] = normed
    scale_ref[...] = scaling
    partial_sum = dot(hot, normed.astype(BF)).astype(BF)
    for y in range(sum_ref.shape[0]):
        sum_ref[y] = partial_sum


def latent_kernel(rows, own, me_ref, sums_ref, gath_ref, send_ref, latent_ref, halo_ref):
    total = total_of([sums_ref[y] for y in range(sums_ref.shape[0])])
    latent = (node_rows(gath_ref, 2 * rows, own) + total).astype(BF)
    latent_ref[...] = latent
    hot = one_hot(own_row(send_ref, me_ref[0]), latent.shape[0])
    halo_ref[...] = outer(hot, latent).astype(BF)


def deal(me_ref, keep_ref, give_ref, tail_ref, term_ref, rows, node_ref, own):
    width = keep_ref.shape[1]
    terms = term_ref.shape[1] // width
    count = term_ref.shape[0] // rows
    half = rows // 2
    held = tail_ref.shape[0] // count
    core = me_ref[1]
    for y in range(count):
        for ref, side in ((keep_ref, core), (give_ref, 1 - core)):
            at = pl.ds(pl.multiple_of(y * rows + side * half, half), half)
            for t in range(terms):
                place = (y * terms + t) * half
                ref[place : place + half, :] = term_ref[at, t * width : (t + 1) * width]
        block = node_ref[y * own : (y + 1) * own, :]
        block = jnp.concatenate([block, jnp.zeros((held - own, width), F32)], axis=0)
        tail_ref[y * held : (y + 1) * held, :] = block.astype(BF)


def merge_kernel(count, keep_ref, given_ref, tail_ref, out_ref):
    size, held = keep_ref.shape[0] // count, tail_ref.shape[0] // count
    for y in range(count):
        at, start = slice(y * size, (y + 1) * size), y * (size + held)
        out_ref[start : start + size, :] = total_of([keep_ref[at, :], given_ref[at, :]]).astype(BF)
        out_ref[start + size : start + size + held, :] = tail_ref[y * held : (y + 1) * held, :]


def process_kernel(
    rows, own, latent_ref, halo_ref, source_ref, target_ref, gath_ref,
    back_ref, local_ref, dst_ref, node_ref, hidden_ref, mid_ref,
):
    latent = latent_ref[...]
    table = jnp.concatenate([latent, halo_ref[...]], axis=0)
    nodes = latent.shape[0]
    hot_src = one_hot(source_ref[...], table.shape[0])
    hot_dst = one_hot(target_ref[...], nodes)
    w_src, w_dst, w_out = [whole(gath_ref, k, rows) for k in range(3)]
    src_rows = outer(hot_src, table).astype(BF)
    dst_rows = outer(hot_dst, latent).astype(BF)
    preact = dot(src_rows, w_src) + dot(dst_rows, w_dst)
    gate = sigmoid(preact)
    hidden = (preact * gate).astype(BF)
    hidden_ref[...] = hidden
    normed, scaling = layer_norm(dot(hidden, w_out))
    node_ref[...] = dot(hot_dst, normed.astype(BF))
    upstream = outer(hot_dst, node_rows(gath_ref, 3 * rows, own).astype(BF))
    mid = norm_back(normed, scaling, upstream).astype(BF)
    mid_ref[...] = mid
    grad = (dot_t(mid, w_out) * (gate * (1.0 + preact * (1.0 - gate)))).astype(BF)
    dst_ref[...] = dot(hot_dst, grad).astype(BF)
    at_src = dot(hot_src, grad)
    local_ref[...] = at_src[:nodes]
    back_ref[...] = at_src[nodes:].astype(BF)


def process_terms_kernel(rows, own, latent_ref, dst_ref, hidden_ref, mid_ref, node_ref, out_ref, term_ref):
    width = latent_ref.shape[1]
    term_ref[:, :width] = outer(latent_ref[...], dst_ref[...]).astype(BF)
    term_ref[:, width:] = outer(hidden_ref[...], mid_ref[...]).astype(BF)
    count = term_ref.shape[0] // rows
    size = out_ref.shape[0] // count
    for y in range(count):
        for t in range(2):
            at = y * size + t * rows
            block = term_ref[y * rows : (y + 1) * rows, t * width : (t + 1) * width]
            out_ref[at : at + rows, :] = block
        block = node_ref[y * own : (y + 1) * own, :]
        block = jnp.concatenate([block, jnp.zeros((size - 2 * rows - own, width), F32)], axis=0)
        out_ref[y * size + 2 * rows : (y + 1) * size, :] = block.astype(BF)


def owner_kernel(rows, me_ref, back_ref, send_ref, local_ref, dst_ref, gath_ref, out_ref, src_ref):
    hot = one_hot(own_row(send_ref, me_ref[0]), local_ref.shape[0])
    at_src = (local_ref[...] + dot(hot, back_ref[...])).astype(BF)
    src_ref[...] = at_src
    total = dot_t(at_src, whole(gath_ref, 0, rows)) + dot_t(dst_ref[...], whole(gath_ref, 1, rows))
    total = total.astype(BF)
    for y in range(out_ref.shape[0]):
        out_ref[y] = total


def backward_kernel(
    rows, own, me_ref, sums_ref, proc_ref, latent_ref, src_ref, enc_ref, w_ref, recv_ref, dst_ref,
    pre_ref, norm_ref, scale_ref,
    node_ref, slot_ref, keep_ref, give_ref, tail_ref, term_ref, share_ref,
):
    nodes, width = latent_ref.shape
    node_grad = node_rows(proc_ref, 3 * rows, own) + total_of(
        [sums_ref[y] for y in range(sums_ref.shape[0])]
    )
    node_ref[...] = node_grad
    hot = slots_hot(dst_ref[...], nodes)
    upstream = outer(hot, node_grad.astype(BF))
    mid = norm_back(norm_ref[...], scale_ref[...], upstream).astype(BF)
    preact = pre_ref[...]
    gate = sigmoid(preact)
    hidden = (preact * gate).astype(BF)
    grad = dot_t(mid, w_ref[...]) * (gate * (1.0 + preact * (1.0 - gate)))
    grad = grad.astype(BF)
    slot_ref[...] = wide_rows(grad, recv_ref.shape[1] // width)
    at_node = dot(hot, grad)
    share_ref[...] = at_node
    terms = (
        outer(slot_rows(recv_ref[...], width), grad),
        outer(node_rows(enc_ref, 2 * rows, own).astype(BF), at_node.astype(BF)),
        outer(hidden, mid),
        outer(latent_ref[...], src_ref[...]),
    )
    for k, term in enumerate(terms):
        term_ref[:, k * width : (k + 1) * width] = term.astype(BF)
    deal(me_ref, keep_ref, give_ref, tail_ref, term_ref, rows, share_ref, own)


def grid_kernel(rows, back_ref, send_ref, enc_ref, out_ref):
    nodes, width = out_ref.shape
    grads = dot_t(slot_rows(back_ref[...], width), whole(enc_ref, 0, rows)).astype(BF)
    out_ref[...] = dot(slots_hot(send_ref[...], nodes), grads).astype(BF)


def out_kernel(rows, me_ref, latent_ref, first_ref, out_ref):
    own, nodes = out_ref.shape[0], latent_ref.shape[0]
    mine = lax.broadcasted_iota(jnp.int32, (1, own), 1) + me_ref[0] * own
    latent = outer(one_hot(mine, nodes), latent_ref[...])
    out_ref[...] = (latent + first_ref[2 * rows :, :].astype(F32)[:own]).astype(BF)


def level_kernel(me_ref, second_ref, first_ref, given_ref, out_ref):
    width = second_ref.shape[1]
    half = out_ref.shape[0]
    for k in range(4):
        out_ref[:, k * width : (k + 1) * width] = second_ref[k * half : (k + 1) * half, :]
    for k in range(2):
        mine = pl.ds(pl.multiple_of((2 * k + me_ref[1]) * half, half), half)
        block = total_of([first_ref[mine, :], given_ref[k * half : (k + 1) * half, :]])
        out_ref[:, (4 + k) * width : (5 + k) * width] = block.astype(BF)


def mesh_kernel(rows, me_ref, node_ref, enc_ref, second_ref, mesh_ref):
    own = mesh_ref.shape[0]
    held = own + (-own % PAD)
    total = second_ref[second_ref.shape[0] - held :, :]
    back = dot_t(total, whole(enc_ref, 1, rows))[:own]
    node = node_ref[pl.ds(pl.multiple_of(me_ref[0] * own, 8), own), :]
    mesh_ref[...] = (node + back).astype(BF)


def sum_kernel(in_ref, out_ref):
    out_ref[...] = total_of([in_ref[k] for k in range(in_ref.shape[0])]).astype(out_ref.dtype)


def split_kernel(factor, in_ref, *out_refs):
    count, thin, _ = in_ref.shape
    width = out_refs[0].shape[1]
    for r in range(count):
        for k, ref in enumerate(out_refs):
            block = in_ref[r, :, k * width : (k + 1) * width]
            ref[r * thin : (r + 1) * thin, :] = block.astype(F32) * factor


def per_device(
    grid_feat,
    mesh_feat,
    w_grid,
    w_mesh,
    w_enc2,
    w_src,
    w_dst,
    w_proc2,
    enc_send,
    enc_dst,
    hal_send,
    proc_src,
    proc_dst,
    cotangent,
):
    enc_send, enc_dst, hal_send = enc_send.T, enc_dst.T, hal_send.T
    dom = lax.axis_size(DOM)
    feat = lax.axis_size("y")
    deep = lax.axis_size("z")
    own, width = mesh_feat.shape
    nodes = own * feat
    rows = w_grid.shape[0]
    caps = enc_send.shape[0]
    pair = (dom, 2, width // 2)
    halo = hal_send.shape[0]
    edges = proc_src.shape[0]
    held = own + (-own % PAD)
    factor = 1.0 / math.sqrt(own * dom * feat)
    index = lax.axis_index("y")
    me = jnp.stack([index, lax.axis_index("c")])
    if halo != feat or held - own < 8 or edges > width:
        raise ValueError("sizes")
    bind = functools.partial

    half = rows // 2
    outgoing, enc_pack, proc_pack = call(
        pack_kernel,
        [
            ((dom, caps * width), BF),
            ((2 * rows + held, width), BF),
            ((3 * rows + held, width), BF),
        ],
        enc_send,
        grid_feat,
        proc_src.reshape(1, edges),
        proc_dst.reshape(1, edges),
        w_grid,
        w_mesh,
        w_src,
        w_dst,
        w_proc2,
        mesh_feat,
        cotangent,
        scratch=[pltpu.VMEM((held - own, width), F32)],
    )
    received = exchange(outgoing.reshape(dom, caps, width), DOM).reshape(dom, caps * width)
    enc_gath = lax.all_gather(enc_pack, "y", axis=0)
    full_enc2 = lax.all_gather(w_enc2, "y", axis=0, tiled=True)
    proc_gath = lax.all_gather(proc_pack, "y", axis=0)

    slots = dom * caps
    one_sum, all_sums = ((nodes, width), BF), ((feat, nodes, width), BF)
    partial_sum, preact, normed, scaling = call(
        bind(encode_kernel, rows, own),
        [
            all_sums,
            ((slots, width), F32),
            ((slots, width), F32),
            ((slots, 1), F32),
        ],
        received,
        enc_dst,
        enc_gath,
        full_enc2,
    )
    latent, halo_out = call(
        bind(latent_kernel, rows, own),
        [one_sum, ((dom, width), BF)],
        exchange(partial_sum, "y"),
        enc_gath,
        hal_send,
        me=me,
    )
    halo_rows = exchange(halo_out.reshape(pair), DOM).reshape(dom, width)

    lines = enc_gath[:, 2 * rows + own : 2 * rows + own + 3, :edges].astype(jnp.int32)
    source = lines[:, 0] * 16 + lines[:, 1]
    slot = source - nodes
    place = jnp.where(slot < 0, source, nodes + slot // halo)
    keeper = jnp.where(slot < 0, jnp.arange(feat, dtype=jnp.int32)[:, None], slot % halo)
    mine = keeper == index
    halo_back, at_local, at_dst, messages, hidden, mid = call(
        bind(process_kernel, rows, own),
        [
            ((dom, width), BF),
            ((nodes, width), F32),
            one_sum,
            ((nodes, width), F32),
            ((feat * edges, width), BF),
            ((feat * edges, width), BF),
        ],
        latent,
        halo_rows,
        jnp.where(mine, place, -1).reshape(1, feat * edges),
        jnp.where(mine, lines[:, 2], -1).reshape(1, feat * edges),
        proc_gath,
    )
    returned = exchange(halo_back.reshape(pair), DOM)
    (first,) = call(
        bind(process_terms_kernel, rows, own),
        [((feat * (2 * rows + held), width), BF)],
        latent,
        at_dst,
        hidden,
        mid,
        messages,
        scratch=[pltpu.VMEM((width, 2 * width), BF)],
    )
    first = lax.psum_scatter(first, "y", scatter_dimension=0, tiled=True)
    node_part, at_src = call(
        bind(owner_kernel, rows),
        [all_sums, one_sum],
        returned.reshape(dom, width),
        hal_send,
        at_local,
        at_dst,
        proc_gath,
        me=me,
    )

    node_in = exchange(node_part, "y")

    node_grad, slot_out, *second = call(
        bind(backward_kernel, rows, own),
        [
            ((nodes, width), F32),
            ((dom, caps * width), BF),
            ((8 * rows, width), BF),
            ((8 * rows, width), BF),
            ((feat * held, width), BF),
        ],
        node_in,
        proc_gath,
        latent,
        at_src,
        enc_gath,
        full_enc2,
        received,
        enc_dst,
        preact,
        normed,
        scaling,
        me=me,
        scratch=[pltpu.VMEM((width, 4 * width), BF), pltpu.VMEM((nodes, width), F32)],
    )
    slot_back = exchange(slot_out.reshape(dom, caps, width), DOM)
    second = over_cores(*second)
    second = lax.psum_scatter(second, "y", scatter_dimension=0, tiled=True)
    give = lax.dynamic_slice_in_dim(first[: 2 * rows].reshape(2, 2, half, width), 1 - me[1], 1, 1)
    given = lax.ppermute(give.reshape(rows, width), "c", [(0, 1), (1, 0)])
    (level,) = call(level_kernel, [((half, 6 * width), BF)], second, first, given, me=me)
    slot_back, level = lax.optimization_barrier((slot_back, level))
    across = lax.axis_size("x")
    thin = rows // (2 * across)
    level = exchange(level.reshape(across, thin, 6 * width), "x")
    (level,) = call(sum_kernel, [((thin, 6 * width), BF)], level)
    level = exchange(level.reshape(deep, 2, 3 * width), "z")
    level = level.astype(F32).sum(axis=0).astype(BF)
    level = exchange(jnp.broadcast_to(level[None], (deep, *level.shape)), "z")
    level = level.reshape(deep, 6 * width)
    near = lax.axis_size(("x", "c"))
    totals = exchange(jnp.broadcast_to(level[None], (near, *level.shape)), ("c", "x"))
    totals = call(bind(split_kernel, factor), [((rows, width), F32)] * 6, totals)
    (out_rows,) = call(bind(out_kernel, rows), [((own, width), BF)], latent, first, me=me)
    (g_mesh,) = call(
        bind(mesh_kernel, rows), [((own, width), BF)], node_grad, enc_gath, second, me=me
    )
    (g_grid,) = call(
        bind(grid_kernel, rows),
        [(grid_feat.shape, BF)],
        slot_back.reshape(dom, caps * width),
        enc_send,
        enc_gath,
    )
    return (out_rows, g_grid, g_mesh) + tuple(totals)


def solution(mesh):
    dom, feat = mesh.shape["dom"], mesh.shape["feat"]
    x = 4 if dom % 8 == 0 else 1
    finer = Mesh(mesh.devices.reshape(dom // (2 * x), x, 2, feat), ALL)
    return jax.shard_map(
        per_device,
        mesh=finer,
        in_specs=(
            P(ALL, None),
            P(ALL, None),
            P("y", None),
            P("y", None),
            P("y", None),
            P("y", None),
            P("y", None),
            P("y", None),
            P(ALL, None),
            P(ALL, None),
            P(DOM, None),
            P(ALL),
            P(ALL),
            P(ALL, None),
        ),
        out_specs=(
            P(ALL, None),
            P(ALL, None),
            P(ALL, None),
            P("y", None),
            P("y", None),
            P("y", None),
            P("y", None),
            P("y", None),
            P("y", None),
        ),
        check_vma=False,
    )
```
